32 devices in a mesh: dp: 8 (over z, core), seq: 4 (over y, x).
Axes of the slice: x: 2, y: 2, z: 4, core: 2. Of those that a mesh axis runs over, the one named last changes fastest.
Arguments:
- tokens: bfloat16 [2, 8192, 2048], P(None, ('dp', 'seq')), may hold values from -6 to 6
- cotangent: bfloat16 [2, 8192, 2048], P(None, ('dp', 'seq')), may hold values from -6 to 6
- segments: int32 [2, 8192], P(None, 'dp'), may hold values from 0 to 3, as said below
- in_weight: float32 [2048, 8512], P(('dp', 'seq')), may hold values from -0.125 to 0.125
- in_m: float32 [2048, 8512], P(('dp', 'seq')), may hold values from -0.0014648438 to 0.0014648438
- in_v: float32 [2048, 8512], P(('dp', 'seq')), may hold values from 1e-09 to 1e-07
- conv_weight: float32 [5, 4352], P(None, ('dp', 'seq')), may hold values from -3 to 3
- conv_m: float32 [5, 4352], P(None, ('dp', 'seq')), may hold values from -0.0014648438 to 0.0014648438
- conv_v: float32 [5, 4352], P(None, ('dp', 'seq')), may hold values from 1e-09 to 1e-07
- out_weight: float32 [4096, 2048], P(None, ('dp', 'seq')), may hold values from -0.09375 to 0.09375
- out_m: float32 [4096, 2048], P(None, ('dp', 'seq')), may hold values from -0.0014648438 to 0.0014648438
- out_v: float32 [4096, 2048], P(None, ('dp', 'seq')), may hold values from 1e-09 to 1e-07
- packed: float32 [6336], replicated, may hold values from -7 to 2, as said below
- packed_m: float32 [6336], replicated, may hold values from -0.0014648438 to 0.0014648438
- packed_v: float32 [6336], replicated, may hold values from 1e-09 to 1e-07
Outputs:
- output: bfloat16 [2, 8192, 2048], P(None, ('dp', 'seq'))
- input_grad: bfloat16 [2, 8192, 2048], P(None, ('dp', 'seq'))
- grad_norm: float32 [], replicated
- in_weight_new: float32 [2048, 8512], P(('dp', 'seq'))
- in_m_new: float32 [2048, 8512], P(('dp', 'seq'))
- in_v_new: float32 [2048, 8512], P(('dp', 'seq'))
- conv_weight_step: float32 [5, 4352], P(None, ('dp', 'seq'))
- conv_m_new: float32 [5, 4352], P(None, ('dp', 'seq'))
- conv_v_new: float32 [5, 4352], P(None, ('dp', 'seq'))
- out_weight_new: float32 [4096, 2048], P(None, ('dp', 'seq'))
- out_m_new: float32 [4096, 2048], P(None, ('dp', 'seq'))
- out_v_new: float32 [4096, 2048], P(None, ('dp', 'seq'))
- packed_step: float32 [6336], replicated
- packed_m_new: float32 [6336], replicated
- packed_v_new: float32 [6336], replicated
The draws below stay inside these ranges and needn't reach their ends.
Inputs may be any that keep to these rules, and one draw needn't show every extreme that they name: `segments`: for each micro-batch and each index of dp the ids of its 1024 tokens start at 0 and never fall; id 1 begins within the first 256 tokens and ends within the last 256; ids 2 and 3 follow it. `packed`: gains and skip factors are positive.
All inputs are finite; a program needn't handle non-finite values.
Results may differ from the reference program's by a relative error of at most 0.015.
Values may be sent and summed in bfloat16 or wider, within the bound.
No kernel may reach another device: no remote copies, remote signals or barrier semaphores. Data moves between devices by JAX's collectives and lax.ppermute only.
A program may use at most 448 MiB of HBM per device.

```python
import math
import jax
import jax.numpy as jnp
from jax import lax

D = 2048
HEADS = 64
HEADDIM = 64
STATE = 128
CONV = 4
BLOCK = 256
MICRO = 2
INNER = 4096
CH = 4352
PROJ = 8512
VEC = 6336
PIECE = 256
LENGTH = 1024
ROWS = 8192


def draw_segments(key, part):
    key = jax.random.fold_in(key, 3)
    subkeys = jax.random.split(key, 3)
    row_count = MICRO * (ROWS // LENGTH)
    first_end = jax.random.randint(subkeys[0], (row_count, 1), 1, PIECE)
    long_end = jax.random.randint(subkeys[1], (row_count, 1), LENGTH - PIECE + 1, LENGTH - 1)
    last_start = jax.random.randint(subkeys[2], (row_count, 1), long_end + 1, LENGTH)
    positions = jnp.arange(LENGTH)[None, :]
    segment_ids = (positions >= first_end).astype(jnp.int32) + (positions >= long_end).astype(jnp.int32) + (positions >= last_start).astype(jnp.int32)
    return segment_ids.reshape(MICRO, ROWS).astype(jnp.int32)


def draw_packed(key, part):
    key = jax.random.fold_in(key, 7)
    subkeys = jax.random.split(key, 6)
    slow_share = 0.5
    slow_head = jax.random.uniform(subkeys[0], (HEADS,)) < slow_share
    slow_rate = jnp.exp(jax.random.uniform(subkeys[1], (HEADS,), minval=math.log(0.3), maxval=math.log(2.0))) / LENGTH
    fast_rate = jnp.exp(jax.random.uniform(subkeys[2], (HEADS,), minval=math.log(1.0 / 48.0), maxval=math.log(1.0 / 24.0)))
    decay_rate = jnp.where(slow_head, slow_rate, fast_rate)
    jitter = jax.random.uniform(subkeys[3], (HEADS,), minval=-0.5, maxval=0.5)
    a_log = 0.5 * jnp.log(decay_rate) + jitter
    step_dt = jnp.sqrt(decay_rate) * jnp.exp(-jitter)
    dt_bias = jnp.log(jnp.expm1(step_dt))
    skip_gain = jax.random.uniform(subkeys[4], (HEADS,), minval=0.5, maxval=1.5)
    gains = jnp.exp(jax.random.uniform(subkeys[5], (D + INNER,), minval=-0.4, maxval=0.4))
    return jnp.concatenate([a_log, skip_gain, dt_bias, gains]).astype(jnp.float32)


def steps_of(rng, extent, pieces, low, high):
    loudness = 1.0
    for dim, parts in pieces:
        steps = jax.random.uniform(jax.random.fold_in(jax.random.fold_in(rng, 6), dim), (parts,), jnp.float32, low / len(pieces), high / len(pieces))
        loudness = loudness * jnp.repeat(jnp.exp(steps), extent[dim] // parts).reshape((-1,) + (1,) * (len(extent) - 1 - dim))
    return loudness


def normal_values(stream_key, shape, scale, most, shards=(), held_as=jnp.bfloat16):
    values = jax.random.normal(stream_key, shape, jnp.float32) * scale
    if len(shards) > 0:
        values = steps_of(stream_key, shape, shards, -0.22, 0.18) * values
    return jnp.clip(values, min=-most, max=most).astype(held_as)


def setup_inputs(seed: int = 0) -> dict:
    streams_of = jax.random.split(jax.random.key(seed), 16)
    return {
        "tokens": normal_values(streams_of[0], (MICRO, ROWS, D), 1.0, 6.0, ((1, 32),)),
        "cotangent": normal_values(streams_of[1], (MICRO, ROWS, D), 1.0, 6.0, ((1, 32),)),
        "segments": draw_segments(jax.random.fold_in(streams_of[15], 71), 0),
        "in_weight": normal_values(streams_of[3], (D, PROJ), D ** -0.5, 0.125, ((0, 32),), jnp.float32),
        "in_m": normal_values(streams_of[4], (D, PROJ), 0.0001, 0.0014648438, ((0, 32),), jnp.float32),
        "in_v": jnp.clip(jnp.exp(math.log(1.0000000116860974e-07) - 4.6051702 * jax.random.uniform(streams_of[5], (D, PROJ), jnp.float32) ** steps_of(streams_of[5], (D, PROJ), ((0, 32),), -0.2, 0.2)), 9.999999717180685e-10, 1.0000000116860974e-07),
        "conv_weight": normal_values(streams_of[6], (CONV + 1, CH), CONV ** -0.5, 3.0, ((1, 32),), jnp.float32),
        "conv_m": normal_values(streams_of[7], (CONV + 1, CH), 0.0001, 0.0014648438, ((1, 32),), jnp.float32),
        "conv_v": jnp.clip(jnp.exp(math.log(1.0000000116860974e-07) - 4.6051702 * jax.random.uniform(streams_of[8], (CONV + 1, CH), jnp.float32) ** steps_of(streams_of[8], (CONV + 1, CH), ((1, 32),), -0.2, 0.2)), 9.999999717180685e-10, 1.0000000116860974e-07),
        "out_weight": normal_values(streams_of[9], (INNER, D), INNER ** -0.5, 0.09375, ((1, 32),), jnp.float32),
        "out_m": normal_values(streams_of[10], (INNER, D), 0.0001, 0.0014648438, ((1, 32),), jnp.float32),
        "out_v": jnp.clip(jnp.exp(math.log(1.0000000116860974e-07) - 4.6051702 * jax.random.uniform(streams_of[11], (INNER, D), jnp.float32) ** steps_of(streams_of[11], (INNER, D), ((1, 32),), -0.2, 0.2)), 9.999999717180685e-10, 1.0000000116860974e-07),
        "packed": draw_packed(jax.random.fold_in(streams_of[15], 71), 0),
        "packed_m": normal_values(streams_of[13], (VEC,), 0.0001, 0.0014648438, (), jnp.float32),
        "packed_v": jnp.clip(jnp.exp(jax.random.uniform(streams_of[14], (VEC,), jnp.float32, math.log(9.999999717180685e-10), math.log(1.0000000116860974e-07))), 9.999999717180685e-10, 1.0000000116860974e-07),
    }


@jax.custom_vjp
def low(v):
    return lax.optimization_barrier(v.astype(jnp.bfloat16)).astype(jnp.float32)

@jax.custom_vjp
def low_back(v):
    return v

def low_keep(v):
    return (low(v), None)

def low_pass(kept, grad):
    return (grad,)

def back_keep(v):
    return (v, None)

def back_low(kept, grad):
    return (low(grad),)
low.defvjp(low_keep, low_pass)
low_back.defvjp(back_keep, back_low)
HIGHEST_PREC = lax.Precision.HIGHEST
NORM_EPS = 1e-05
LEARN_RATE = 0.004
BETA_ONE = 0.9
BETA_TWO = 0.95
FIX_ONE = 1.0 - 0.9 ** 10
FIX_TWO = 1.0 - 0.95 ** 10
ADAM_EPS = 1e-08
WEIGHT_DECAY = 0.1
CLIP_NORM = 1.0

def unpack_vector(packed):
    return (packed[:HEADS], packed[HEADS:2 * HEADS], packed[2 * HEADS:3 * HEADS], packed[3 * HEADS:3 * HEADS + D], packed[3 * HEADS + D:])

def pre_norm(row_x, gain_in):
    return row_x * lax.rsqrt(lax.optimization_barrier(jnp.mean(row_x * row_x, axis=-1, keepdims=True)) + NORM_EPS) * gain_in

def gated_norm(mixed_y, gate_z, gain_out):
    gated_y = mixed_y * jax.nn.silu(gate_z)
    return gated_y * lax.rsqrt(lax.optimization_barrier(jnp.mean(gated_y * gated_y, axis=-1, keepdims=True)) + NORM_EPS) * gain_out

def causal_conv(padded, seg_padded, conv_w, length):
    tap_count = conv_w.shape[0] - 1
    segment = seg_padded[tap_count - 1:]
    summed = conv_w[tap_count][None, :] + jnp.zeros_like(padded[:length])
    for tap_at in range(tap_count):
        valid = (seg_padded[tap_at:tap_at + length] == segment).astype(padded.dtype)
        summed = summed + conv_w[tap_at][None, :] * padded[tap_at:tap_at + length] * valid[:, None]
    return summed

def block_parts(x_heads, b_proj, c_proj, step_dt, a_neg, segment, seg_prev, precision):
    width = x_heads.shape[0]
    cumulative = jnp.cumsum(step_dt * a_neg[None, :], axis=0)
    positions = jnp.arange(width)
    same_doc = ((segment[:, None] == segment[None, :]) & (positions[:, None] >= positions[None, :])).astype(step_dt.dtype)
    cum_heads = cumulative.T
    gaps_log = cum_heads[:, :, None] - cum_heads[:, None, :]
    decay_mask = jnp.exp(jnp.minimum(gaps_log, 0.0)) * same_doc[None]
    inner_cb = jnp.einsum('tn,sn->ts', c_proj, b_proj, precision=precision)
    mixing = low_back(low(inner_cb[None] * decay_mask * step_dt.T[:, None, :]))
    y_intra = jnp.einsum('hts,shp->thp', mixing, x_heads, precision=precision)
    end_weight = jnp.exp(cumulative[-1][None, :] - cumulative) * (segment == segment[-1]).astype(step_dt.dtype)[:, None]
    weighted = low_back(low(x_heads * (end_weight * step_dt)[:, :, None]))
    s_block = jnp.einsum('shp,sn->hpn', weighted, b_proj, precision=precision)
    a_block = jnp.exp(cumulative[-1]) * (segment[-1] == seg_prev).astype(step_dt.dtype)
    entry_decay = jnp.exp(cumulative) * (segment == seg_prev).astype(step_dt.dtype)[:, None]
    return (y_intra, s_block, a_block, entry_decay)

def row_forward(row_x, segment, w_in, conv_w, w_out, packed):
    a_log, skip_gain, dt_bias, gain_in, gain_out = unpack_vector(packed)
    length = row_x.shape[0]
    hidden = low(pre_norm(row_x, gain_in))
    projected = low_back(low(jnp.dot(hidden, w_in, precision=HIGHEST_PREC)))
    gate_z = projected[:, :INNER]
    conv_in = projected[:, INNER:INNER + CH]
    dt_raw = projected[:, INNER + CH:]
    padded = jnp.concatenate([jnp.zeros((CONV - 1, CH), row_x.dtype), conv_in], axis=0)
    seg_padded = jnp.concatenate([jnp.full((CONV - 1,), -1, jnp.int32), segment.astype(jnp.int32)])
    activated = low_back(low(jax.nn.silu(causal_conv(padded, seg_padded, conv_w, length))))
    x_heads = activated[:, :INNER].reshape(length, HEADS, HEADDIM)
    b_proj = activated[:, INNER:INNER + STATE]
    c_proj = activated[:, INNER + STATE:]
    step_dt = jax.nn.softplus(dt_raw + dt_bias[None, :])
    a_neg = -jnp.exp(a_log)
    block_count = length // BLOCK
    seg_prev = jnp.concatenate([jnp.full((1,), -1, jnp.int32), segment.reshape(block_count, BLOCK)[:, -1][:block_count - 1].astype(jnp.int32)])
    block_inputs = (x_heads.reshape(block_count, BLOCK, HEADS, HEADDIM), b_proj.reshape(block_count, BLOCK, STATE), c_proj.reshape(block_count, BLOCK, STATE), step_dt.reshape(block_count, BLOCK, HEADS), segment.reshape(block_count, BLOCK), seg_prev)

    def block_step(carried, inputs_one):
        xh_c, b_c, c_c, dt_c, seg_c, prev_c = inputs_one
        y_intra, s_block, a_block, entry_decay = block_parts(xh_c, b_c, c_c, dt_c, a_neg, seg_c, prev_c, HIGHEST_PREC)
        y_state = entry_decay[:, :, None] * jnp.einsum('tn,hpn->thp', c_c, low(carried), precision=HIGHEST_PREC)
        y_block = y_intra + y_state + skip_gain[None, :, None] * xh_c
        return (a_block[:, None, None] * carried + s_block, y_block)
    start_state = jnp.zeros((HEADS, HEADDIM, STATE), row_x.dtype)
    _, y_blocks = lax.scan(jax.checkpoint(block_step), start_state, block_inputs)
    mixed_y = low_back(y_blocks.reshape(length, INNER))
    normed = low(gated_norm(mixed_y, gate_z, gain_out))
    return row_x + jnp.dot(normed, w_out, precision=HIGHEST_PREC)

def adamw(master, gradient, first_moment, second_moment, clip_scale, decay):
    clipped = gradient * clip_scale
    first_new = BETA_ONE * first_moment + (1.0 - BETA_ONE) * clipped
    second_new = BETA_TWO * second_moment + (1.0 - BETA_TWO) * clipped * clipped
    update = first_new / FIX_ONE / (jnp.sqrt(second_new / FIX_TWO) + ADAM_EPS) + decay * master
    return (-LEARN_RATE * update, first_new, second_new)

def reference(tokens, cotangent, segments, in_weight, in_m, in_v, conv_weight, conv_m, conv_v, out_weight, out_m, out_v, packed, packed_m, packed_v):
    row_count = MICRO * (ROWS // LENGTH)
    x_all = tokens.astype(jnp.float32).reshape(row_count, LENGTH, D)
    cot_all = cotangent.astype(jnp.float32).reshape(row_count, LENGTH, D)
    seg_all = segments.reshape(row_count, LENGTH).astype(jnp.int32)

    def forward(x_rows, w_in, conv_w, w_out, vector):
        w_in_low = low(w_in)
        conv_low = low(conv_w)
        w_out_low = low(w_out)

        def row_step(carried, inputs_row):
            return (carried, row_forward(inputs_row[0], inputs_row[1], w_in_low, conv_low, w_out_low, vector))
        _, results = lax.scan(row_step, None, (x_rows, seg_all))
        return results
    result, pullback = jax.vjp(forward, x_all, in_weight.astype(jnp.float32), conv_weight.astype(jnp.float32), out_weight.astype(jnp.float32), packed.astype(jnp.float32))
    grad_x, grad_in, grad_conv, grad_out, grad_vec = pullback(cot_all)
    grad_norm = jnp.sqrt(jnp.sum(grad_in * grad_in) + jnp.sum(grad_conv * grad_conv) + jnp.sum(grad_out * grad_out) + jnp.sum(grad_vec * grad_vec))
    clip_scale = jnp.minimum(1.0, CLIP_NORM / (grad_norm + 1e-06))
    in_new = adamw(in_weight, grad_in, in_m, in_v, clip_scale, WEIGHT_DECAY)
    conv_new = adamw(conv_weight, grad_conv, conv_m, conv_v, clip_scale, WEIGHT_DECAY)
    out_new = adamw(out_weight, grad_out, out_m, out_v, clip_scale, WEIGHT_DECAY)
    vec_new = adamw(packed, grad_vec, packed_m, packed_v, clip_scale, 0.0)
    return (result.reshape(MICRO, ROWS, D).astype(jnp.bfloat16), grad_x.reshape(MICRO, ROWS, D).astype(jnp.bfloat16), grad_norm, in_weight + in_new[0], in_new[1], in_new[2], conv_new[0], conv_new[1], conv_new[2], out_weight + out_new[0], out_new[1], out_new[2], vec_new[0], vec_new[1], vec_new[2])
```

```python
import jax
import jax.numpy as jnp
from jax import lax
from jax.sharding import PartitionSpec as P

D = 2048
HEADS = 64
HEADDIM = 64
STATE = 128
CONV = 4
BLOCK = 256
MICRO = 2
INNER = 4096
CH = 4352
NORM_EPS = 1e-05
LEARN_RATE = 0.004
BETA_ONE = 0.9
BETA_TWO = 0.95
FIX_ONE = 1.0 - 0.9**10
FIX_TWO = 1.0 - 0.95**10
ADAM_EPS = 1e-08
WEIGHT_DECAY = 0.1
CLIP_NORM = 1.0
BF = jnp.bfloat16
F32 = jnp.float32
ALL = ("dp", "seq")


def to_bfloat(value):
    return value.astype(BF).astype(F32)


def rounding_pair():
    def value_plain(value):
        return to_bfloat(value)

    def value_keep(value):
        return (to_bfloat(value), None)

    def value_pass(kept, grad):
        return (grad,)

    def grad_plain(value):
        return value

    def grad_keep(value):
        return (value, None)

    def grad_round(kept, grad):
        return (to_bfloat(grad),)

    value_op = jax.custom_vjp(value_plain)
    value_op.defvjp(value_keep, value_pass)
    grad_op = jax.custom_vjp(grad_plain)
    grad_op.defvjp(grad_keep, grad_round)
    return (value_op, grad_op)


value_lower, grad_lower = rounding_pair()


def causal_conv(padded, seg_padded, conv_w, length):
    segment = seg_padded[CONV - 1 :]
    summed = conv_w[CONV][None, :] + jnp.zeros_like(padded[:length])
    for tap in range(CONV):
        valid = (seg_padded[tap : tap + length] == segment).astype(padded.dtype)
        summed = summed + conv_w[tap][None, :] * padded[tap : tap + length] * valid[:, None]
    return summed


def block_parts(xh, bm, cm, dt, a_neg, seg, seg_prev):
    width = xh.shape[0]
    cum = jnp.cumsum(dt * a_neg[None, :], axis=0)
    pos = jnp.arange(width)
    same = ((seg[:, None] == seg[None, :]) & (pos[:, None] >= pos[None, :])).astype(F32)
    ch = cum.T
    decay = jnp.exp(jnp.minimum(ch[:, :, None] - ch[:, None, :], 0.0)) * same[None]
    inner = jnp.einsum("tn,sn->ts", cm, bm)
    mix = grad_lower(value_lower(inner[None] * decay * dt.T[:, None, :]))
    y_intra = jnp.einsum("hts,shp->thp", mix, xh)
    end_w = jnp.exp(cum[-1][None, :] - cum) * (seg == seg[-1]).astype(F32)[:, None]
    weighted = grad_lower(value_lower(xh * (end_w * dt)[:, :, None]))
    s_block = jnp.einsum("shp,sn->hpn", weighted, bm)
    a_block = jnp.exp(cum[-1]) * (seg[-1] == seg_prev).astype(F32)
    entry = jnp.exp(cum) * (seg == seg_prev).astype(F32)[:, None]
    return (y_intra, s_block, a_block, entry)


def mixer(conv_in, dt_raw, conv_w, a_log, skip, dt_bias, seg):
    length = conv_in.shape[0]
    hl = dt_raw.shape[1]
    xw = hl * HEADDIM
    nb = length // BLOCK
    padded = jnp.concatenate([jnp.zeros((CONV - 1, conv_in.shape[1]), F32), conv_in], axis=0)
    seg_pad = jnp.concatenate([jnp.full((CONV - 1,), -1, jnp.int32), seg])
    act = grad_lower(value_lower(jax.nn.silu(causal_conv(padded, seg_pad, conv_w, length))))
    xh = act[:, :xw].reshape(nb, BLOCK, hl, HEADDIM)
    bm = act[:, xw : xw + STATE].reshape(nb, BLOCK, STATE)
    cm = act[:, xw + STATE :].reshape(nb, BLOCK, STATE)
    dt = jax.nn.softplus(dt_raw + dt_bias[None, :]).reshape(nb, BLOCK, hl)
    a_neg = -jnp.exp(a_log)
    segb = seg.reshape(nb, BLOCK)
    seg_prev = jnp.concatenate([jnp.full((1,), -1, jnp.int32), segb[:-1, -1]])

    def step(state, ins):
        x_c, b_c, c_c, dt_c, s_c, p_c = ins
        y_in, s_blk, a_blk, entry = block_parts(x_c, b_c, c_c, dt_c, a_neg, s_c, p_c)
        y_st = entry[:, :, None] * jnp.einsum("tn,hpn->thp", c_c, value_lower(state))
        y = y_in + y_st + skip[None, :, None] * x_c
        return (a_blk[:, None, None] * state + s_blk, y)

    start = jnp.zeros((hl, HEADDIM, STATE), F32)
    _, y = lax.scan(jax.checkpoint(step), start, (xh, bm, cm, dt, segb, seg_prev))
    return grad_lower(y.reshape(length, xw))


def adamw(master, gradient, first, second, clip, decay):
    clipped = gradient * clip
    first_new = BETA_ONE * first + (1.0 - BETA_ONE) * clipped
    second_new = BETA_TWO * second + (1.0 - BETA_TWO) * clipped * clipped
    update = first_new / FIX_ONE / (jnp.sqrt(second_new / FIX_TWO) + ADAM_EPS) + decay * master
    return (-LEARN_RATE * update, first_new, second_new)


def dot(a, b, dims, out=F32):
    return lax.dot_general(a, b, (dims, ((), ())), preferred_element_type=out)


NN = ((1,), (0,))
NT = ((1,), (1,))
TN = ((0,), (0,))


def per_device(tokens, cotangent, segments, in_weight, in_m, in_v, conv_weight, conv_m, conv_v,
               out_weight, out_m, out_v, packed, packed_m, packed_v):
    n = lax.axis_size("seq")
    rank = lax.axis_index("seq")
    ndev = n * lax.axis_size("dp")
    hl = HEADS // n
    xw = hl * HEADDIM
    rows = D // ndev
    piece = tokens.shape[1]
    length = piece * n

    in_low = in_weight.astype(BF)
    out_low = out_weight.astype(BF).T
    xs = INNER + INNER
    parts_z = in_low[:, :INNER].reshape(rows, n, xw).transpose(1, 0, 2)
    parts_x = in_low[:, INNER:xs].reshape(rows, n, xw).transpose(1, 0, 2)
    parts_bc = jnp.broadcast_to(in_low[None, :, xs : xs + 2 * STATE], (n, rows, 2 * STATE))
    parts_dt = jnp.pad(in_low[:, xs + 2 * STATE :].reshape(rows, n, hl).transpose(1, 0, 2), ((0, 0), (0, 0), (0, 128 - hl)))
    parts_o = out_low.reshape(rows, n, xw).transpose(1, 0, 2)
    send = jnp.concatenate([parts_x, parts_bc, parts_dt, parts_z, parts_o], axis=2)
    got = lax.all_to_all(send, "seq", 0, 0).reshape(n * rows, -1)
    xc = xw + 2 * STATE + 128
    w_x = lax.all_gather(got[:, :xc], "dp", axis=0, tiled=True)
    w_z = lax.all_gather(got[:, xc : xc + xw], "dp", axis=0, tiled=True)
    w_o = lax.all_gather(got[:, xc + xw :], "dp", axis=0, tiled=True)
    conv_full = lax.all_gather(conv_weight.astype(BF), ALL, axis=1, tiled=True)
    conv_loc = jnp.concatenate([lax.dynamic_slice_in_dim(conv_full, rank * xw, xw, 1), conv_full[:, INNER:]], axis=1).astype(F32)

    a_log = lax.dynamic_slice_in_dim(packed, rank * hl, hl)
    skip = lax.dynamic_slice_in_dim(packed, HEADS + rank * hl, hl)
    dt_bias = lax.dynamic_slice_in_dim(packed, 2 * HEADS + rank * hl, hl)
    gain_in = packed[3 * HEADS : 3 * HEADS + D]
    gain_out = lax.dynamic_slice_in_dim(packed, 3 * HEADS + D + rank * xw, xw)

    tok = tokens.astype(F32)
    r_in = lax.rsqrt(jnp.mean(tok * tok, axis=-1, keepdims=True) + NORM_EPS)
    hidden_own = (tok * r_in * gain_in).astype(BF)
    hidden = lax.all_gather(hidden_own, "seq", axis=1, tiled=True).reshape(MICRO * length, D)
    cot = lax.all_gather(cotangent, "seq", axis=1, tiled=True).reshape(MICRO * length, D)

    proj_x = dot(hidden, w_x, NN).astype(BF)
    proj_z = dot(hidden, w_z, NN).astype(BF)
    conv_in = proj_x[:, : xw + 2 * STATE].astype(F32).reshape(MICRO, length, -1)
    dt_raw = proj_x[:, xw + 2 * STATE : xw + 2 * STATE + hl].astype(F32).reshape(MICRO, length, hl)
    mix_fn = lambda ci, dr, cw, al, sk, db: jax.vmap(mixer, (0, 0, None, None, None, None, 0))(ci, dr, cw, al, sk, db, segments)
    y, pull = jax.vjp(mix_fn, conv_in, dt_raw, conv_loc, a_log, skip, dt_bias)
    y = y.reshape(MICRO * length, xw)
    z = proj_z.astype(F32)
    sig = jax.nn.sigmoid(z)
    gz = y * z * sig
    dnr = dot(cot, w_o, NN)
    dng = dnr * gain_out
    sums = lax.psum(jnp.stack([jnp.sum(gz * gz, axis=1), jnp.sum(dng * gz, axis=1)]), "seq")
    r = lax.rsqrt(sums[0] / INNER + NORM_EPS)
    normed = (gz * r[:, None] * gain_out).astype(BF)
    d_gz = r[:, None] * dng - gz * (r * r * r * sums[1] / INNER)[:, None]
    d_gain_out = jnp.sum(dnr * gz * r[:, None], axis=0)
    dy = d_gz * z * sig
    dz = (d_gz * y * (sig * (1.0 + z * (1.0 - sig)))).astype(BF)

    out_part = dot(normed, w_o, NT).astype(BF).reshape(MICRO, length, D)
    out_sum = lax.psum_scatter(out_part, "seq", scatter_dimension=1, tiled=True)
    output = (tok + out_sum.astype(F32)).astype(BF)
    dw_o = lax.psum_scatter(dot(cot, normed, TN).astype(BF), "dp", scatter_dimension=0, tiled=True)
    dw_z = lax.psum_scatter(dot(hidden, dz, TN).astype(BF), "dp", scatter_dimension=0, tiled=True)

    d_ci, d_dr, d_conv, d_alog, d_skip, d_dtb = pull(dy.reshape(MICRO, length, xw))
    d_px = jnp.concatenate([d_ci.reshape(MICRO * length, -1), jnp.pad(d_dr.reshape(MICRO * length, hl), ((0, 0), (0, 128 - hl)))], axis=1).astype(BF)
    d_hid = (dot(dz, w_z, NT) + dot(d_px, w_x, NT)).astype(BF).reshape(MICRO, length, D)
    d_hidden = lax.psum_scatter(d_hid, "seq", scatter_dimension=1, tiled=True).astype(F32)
    dw_x = lax.psum_scatter(dot(hidden, d_px, TN).astype(BF), "dp", scatter_dimension=0, tiled=True)

    grad_piece = jnp.concatenate([dw_x, dw_z, dw_o], axis=1).reshape(n, rows, -1)
    grad_got = lax.all_to_all(grad_piece, "seq", 0, 0)
    flat = lambda a: a.transpose(1, 0, 2).reshape(rows, -1)
    g_x = flat(grad_got[:, :, :xw]).astype(F32)
    g_bc = jnp.sum(grad_got[:, :, xw : xw + 2 * STATE].astype(F32), axis=0)
    g_dt = flat(grad_got[:, :, xw + 2 * STATE : xw + 2 * STATE + hl]).astype(F32)
    g_z = flat(grad_got[:, :, xc : xc + xw]).astype(F32)
    shard_in = jnp.concatenate([g_z, g_x, g_bc, g_dt], axis=1)
    shard_out = flat(grad_got[:, :, xc + xw :]).astype(F32).T

    dh = d_hidden * gain_in
    d_gain_in = jnp.sum(d_hidden * tok * r_in, axis=(0, 1))
    d_tok = r_in * (dh - tok * (r_in * r_in) * jnp.mean(dh * tok, axis=-1, keepdims=True))
    input_grad = (cotangent.astype(F32) + d_tok).astype(BF)

    conv_part = jnp.zeros((CONV + 1, CH), F32)
    conv_part = lax.dynamic_update_slice(conv_part, d_conv[:, :xw], (0, rank * xw))
    conv_part = conv_part.at[:, INNER:].set(d_conv[:, xw:])
    vec_part = jnp.zeros((packed.shape[0],), F32)
    vec_part = lax.dynamic_update_slice(vec_part, d_alog, (rank * hl,))
    vec_part = lax.dynamic_update_slice(vec_part, d_skip, (HEADS + rank * hl,))
    vec_part = lax.dynamic_update_slice(vec_part, d_dtb, (2 * HEADS + rank * hl,))
    vec_part = lax.dynamic_update_slice(vec_part, d_gain_in, (3 * HEADS,))
    vec_part = lax.dynamic_update_slice(vec_part, d_gain_out, (3 * HEADS + D + rank * xw,))
    partial_sq = jnp.sum(shard_in * shard_in) + jnp.sum(shard_out * shard_out)
    total_sq, conv_tot, vec_tot = lax.psum((partial_sq, conv_part, vec_part), ALL)
    cw = conv_weight.shape[1]
    shard_conv = lax.dynamic_slice_in_dim(conv_tot, (lax.axis_index("dp") * n + rank) * cw, cw, 1)
    grad_norm = jnp.sqrt(total_sq + jnp.sum(conv_tot * conv_tot) + jnp.sum(vec_tot * vec_tot))
    clip = jnp.minimum(1.0, CLIP_NORM / (grad_norm + 1e-06))
    in_new = adamw(in_weight, shard_in, in_m, in_v, clip, WEIGHT_DECAY)
    conv_new = adamw(conv_weight, shard_conv, conv_m, conv_v, clip, WEIGHT_DECAY)
    out_new = adamw(out_weight, shard_out, out_m, out_v, clip, WEIGHT_DECAY)
    vec_new = adamw(packed, vec_tot, packed_m, packed_v, clip, 0.0)
    return (
        output, input_grad, grad_norm,
        in_weight + in_new[0], in_new[1], in_new[2],
        conv_new[0], conv_new[1], conv_new[2],
        out_weight + out_new[0], out_new[1], out_new[2],
        vec_new[0], vec_new[1], vec_new[2],
    )


def solution(mesh):
    tok, col, row = P(None, ALL, None), P(None, ALL), P(ALL, None)
    return jax.shard_map(
        per_device,
        mesh=mesh,
        in_specs=(tok, tok, P(None, "dp"), row, row, row, col, col, col, col, col, col, P(), P(), P()),
        out_specs=(tok, tok, P(), row, row, row, col, col, col, col, col, col, P(), P(), P()),
        check_vma=False,
    )
```

```python
import functools

import jax
import jax.numpy as jnp
from jax import lax
from jax.experimental import pallas as pl
from jax.experimental.pallas import tpu as pltpu
from jax.sharding import PartitionSpec as P

D = 2048
HEADS = 64
HEADDIM = 64
STATE = 128
CONV = 4
BLOCK = 256
MICRO = 2
INNER = 4096
CH = 4352
NORM_EPS = 1e-05
LEARN_RATE = 0.004
BETA_ONE = 0.9
BETA_TWO = 0.95
FIX_ONE = 1.0 - 0.9**10
FIX_TWO = 1.0 - 0.95**10
ADAM_EPS = 1e-08
WEIGHT_DECAY = 0.1
CLIP_NORM = 1.0
BF = jnp.bfloat16
F32 = jnp.float32
ALL = ("dp", "seq")


def dot(a, b, dims, out=F32):
    return lax.dot_general(a, b, (dims, ((), ())), preferred_element_type=out)


NN = ((1,), (0,))
NT = ((1,), (1,))
TN = ((0,), (0,))
LANES = 128
PAIR = 2 * HEADDIM
VMEM = 56 * 1024 * 1024


def iota2(shape, dim):
    return lax.broadcasted_iota(jnp.int32, shape, dim)


def running_sum(values, reverse):
    row, col = iota2((BLOCK, BLOCK), 0), iota2((BLOCK, BLOCK), 1)
    ones = jnp.where(row <= col if reverse else row >= col, 1.0, 0.0).astype(BF)
    high = values.astype(BF)
    rest = values - high.astype(F32)
    mid = rest.astype(BF)
    low = (rest - mid.astype(F32)).astype(BF)
    return dot(ones, high, NN) + dot(ones, mid, NN) + dot(ones, low, NN)


def step_sizes(raw, bias, a_neg):
    lifted = raw + bias
    dt = jnp.maximum(lifted, 0.0) + jnp.log1p(jnp.exp(-jnp.abs(lifted)))
    cum = running_sum(dt * a_neg, False)
    return lifted, dt, cum


def pick(left, columns, first):
    return jnp.where(left, columns[:, first : first + 1], columns[:, first + 1 : first + 2])


def conv_chunk(window, conv_w, aux, lo, hi):
    out = conv_w[CONV : CONV + 1, lo:hi] + conv_w[CONV - 1 : CONV, lo:hi] * window[8 : 8 + BLOCK, lo:hi]
    for tap in range(CONV - 1):
        out += conv_w[tap : tap + 1, lo:hi] * (window[5 + tap : 5 + tap + BLOCK, lo:hi] * aux[:, tap : tap + 1])
    return out


def forward_kernel(place, proj, conv_w, rows, aux, seg_row, y_out, s_out, window, act, state, *, hl):
    width = hl * HEADDIM
    conv_width = width + 2 * STATE
    step = pl.program_id(1)

    @pl.when(step == 0)
    def _():
        window[0:8, :] = jnp.zeros((8, conv_width), F32)
        state[...] = jnp.zeros(state.shape, F32)

    aux_v = aux[...]
    for lo in range(0, conv_width, LANES):
        hi = lo + LANES
        window[8 : 8 + BLOCK, lo:hi] = proj[:, lo:hi].astype(F32)
        out = conv_chunk(window, conv_w, aux_v, lo, hi)
        act[:, lo:hi] = (out * jax.nn.sigmoid(out)).astype(BF)
    window[0:8, :] = window[BLOCK : BLOCK + 8, :]

    _, dt, cum = step_sizes(proj[:, conv_width : conv_width + LANES].astype(F32), rows[0:1, :LANES], rows[1:2, :LANES])
    entry = jnp.exp(cum) * aux_v[:, 3:4]
    dt_end = dt * jnp.exp(cum[BLOCK - 1 : BLOCK, :] - cum) * aux_v[:, 4:5]
    cum_t, dt_t = cum.T, dt.T
    bm, cm = act[:, width : width + STATE], act[:, width + STATE :]
    same = (aux_v[:, 8:9] == seg_row[0:1, :]) & (iota2((BLOCK, BLOCK), 0) >= iota2((BLOCK, BLOCK), 1))
    inner = jnp.where(same, dot(cm, bm, NT), 0.0)
    left = iota2((BLOCK, PAIR), 1) < HEADDIM
    top = iota2((PAIR, STATE), 0) < HEADDIM
    for pair in range(hl // 2):
        first = 2 * pair
        lo, hi = pair * PAIR, (pair + 1) * PAIR
        xp = act[:, lo:hi]
        halves = []
        for h in (first, first + 1):
            decay = jnp.exp(jnp.minimum(cum[:, h : h + 1] - cum_t[h : h + 1, :], 0.0))
            mix = (inner * (decay * dt_t[h : h + 1, :])).astype(BF)
            halves.append(dot(mix, xp, NN))
        entering = state[lo:hi, :]
        low = entering.astype(BF)
        s_out[0, lo:hi, :] = low
        xf = xp.astype(F32)
        y = jnp.where(left, halves[0], halves[1]) + pick(left, entry, first) * dot(cm, low, NT) + rows[2:3, lo:hi] * xf
        y_out[:, lo:hi] = y.astype(BF)
        weighted = (xf * pick(left, dt_end, first)).astype(BF)
        last = entry[BLOCK - 1 : BLOCK, :]
        keep = jnp.where(top, last[:, first : first + 1], last[:, first + 1 : first + 2])
        state[lo:hi, :] = keep * entering + dot(weighted, bm, TN)


def backward_kernel(place, proj, before, conv_w, rows, aux, seg_row, dy, s_in, dproj, dconv, dvec,
                    window, act, dwin, grad_s, dcb, colsum, *, hl):
    width = hl * HEADDIM
    conv_width = width + 2 * STATE
    step = pl.program_id(1)

    @pl.when((step == 0) & (pl.program_id(0) == 0))
    def _():
        dconv[...] = jnp.zeros(dconv.shape, F32)
        dvec[...] = jnp.zeros(dvec.shape, F32)

    @pl.when(step == 0)
    def _():
        dwin[BLOCK : BLOCK + 8, :] = jnp.zeros((8, conv_width), F32)
        grad_s[...] = jnp.zeros(grad_s.shape, F32)
        colsum[...] = jnp.zeros(colsum.shape, F32)

    aux_v = aux[...]
    window[0:8, :] = before[8:16, :conv_width].astype(F32)
    for lo in range(0, conv_width, LANES):
        hi = lo + LANES
        window[8 : 8 + BLOCK, lo:hi] = proj[:, lo:hi].astype(F32)
        out = conv_chunk(window, conv_w, aux_v, lo, hi)
        sig = jax.nn.sigmoid(out)
        act[:, lo:hi] = (out * sig).astype(BF)
        dwin[0:BLOCK, lo:hi] = sig * (1.0 + out * (1.0 - sig))

    lifted, dt, cum = step_sizes(proj[:, conv_width : conv_width + LANES].astype(F32), rows[0:1, :LANES], rows[1:2, :LANES])
    a_neg = rows[1:2, :LANES]
    entry = jnp.exp(cum) * aux_v[:, 3:4]
    end = jnp.exp(cum[BLOCK - 1 : BLOCK, :] - cum) * aux_v[:, 4:5]
    dt_end = dt * end
    cum_t = cum.T
    bm, cm = act[:, width : width + STATE], act[:, width + STATE :]
    same = (aux_v[:, 8:9] == seg_row[0:1, :]) & (iota2((BLOCK, BLOCK), 0) <= iota2((BLOCK, BLOCK), 1))
    inner = jnp.where(same, dot(bm, cm, NT), 0.0)
    left = iota2((BLOCK, PAIR), 1) < HEADDIM
    top = iota2((PAIR, STATE), 0) < HEADDIM
    lane = iota2((BLOCK, LANES), 1)
    lane_one = iota2((1, LANES), 1)
    last = entry[BLOCK - 1 : BLOCK, :]
    d_dt = jnp.zeros((BLOCK, LANES), F32)
    d_cum = jnp.zeros((BLOCK, LANES), F32)
    d_last = jnp.zeros((1, LANES), F32)
    d_skip = jnp.zeros((1, LANES), F32)
    d_b = jnp.zeros((BLOCK, STATE), F32)
    d_c = jnp.zeros((BLOCK, STATE), F32)

    def through_silu(grad, lo, hi):
        dwin[0:BLOCK, lo:hi] = dwin[0:BLOCK, lo:hi] * grad.astype(BF).astype(F32)

    for pair in range(hl // 2):
        first = 2 * pair
        lo, hi = pair * PAIR, (pair + 1) * PAIR
        xp, dyp = act[:, lo:hi], dy[:, lo:hi]
        xf, dyf = xp.astype(F32), dyp.astype(F32)
        zero = jnp.zeros_like(xp)
        halves = []
        for h in (first, first + 1):
            mine = left if h == first else ~left
            decay = jnp.exp(jnp.minimum(cum_t[h : h + 1, :] - cum[:, h : h + 1], 0.0))
            d_mix = dot(jnp.where(mine, xp, zero), dyp, NT).astype(BF).astype(F32)
            dt_col = dt[:, h : h + 1]
            part = d_mix * decay
            scaled = inner * decay
            mix = (scaled * dt_col).astype(BF)
            weighted_part = part * dt_col
            if h == 0:
                dcb[...] = weighted_part
            else:
                dcb[...] += weighted_part
            pairwise = part * inner
            row_sum = jnp.sum(pairwise, axis=1, keepdims=True)
            d_dt += jnp.where(lane == h, row_sum, 0.0)
            colsum[h : h + 1, :] = jnp.sum(pairwise * dt_col, axis=0, keepdims=True)
            halves.append(dot(mix, dyp, NN))
        later = grad_s[lo:hi, :]
        later_b = later.astype(BF)
        low = s_in[0, lo:hi, :]
        entry_p = pick(left, entry, first)
        d_w = dot(bm, later_b, NT).astype(BF).astype(F32)
        skip_row = rows[2:3, lo:hi]
        dx = jnp.where(left, halves[0], halves[1]) + d_w * pick(left, dt_end, first) + skip_row * dyf
        through_silu(dx, lo, hi)
        used = d_w * xf
        into = dyf * dot(cm, low, NT)
        for h in (first, first + 1):
            mine = left if h == first else ~left
            u = jnp.sum(jnp.where(mine, used, 0.0), axis=1, keepdims=True) * end[:, h : h + 1]
            d_dt += jnp.where(lane == h, u, 0.0)
            d_last += jnp.where(lane_one == h, jnp.sum(u * dt[:, h : h + 1], axis=0, keepdims=True), 0.0)
            d_e = jnp.sum(jnp.where(mine, into, 0.0), axis=1, keepdims=True) * entry[:, h : h + 1]
            d_cum += jnp.where(lane == h, d_e, 0.0)
            rows_mine = top if h == first else ~top
            d_a = jnp.sum(jnp.where(rows_mine, later * low.astype(F32), 0.0), axis=0, keepdims=True)
            d_a = jnp.sum(d_a, axis=1, keepdims=True) * last[:, h : h + 1]
            d_last += jnp.where(lane_one == h, d_a, 0.0)
            ds = jnp.sum(jnp.where(mine, xf * dyf, 0.0), axis=0, keepdims=True)
            d_skip += jnp.where(lane_one == h, jnp.sum(ds, axis=1, keepdims=True), 0.0)
        weighted = (xf * pick(left, dt_end, first)).astype(BF)
        d_b += dot(weighted, later_b, NN)
        entering = (entry_p * dyf).astype(BF)
        d_c += dot(entering, low, NN)
        keep = jnp.where(top, last[:, first : first + 1], last[:, first + 1 : first + 2])
        grad_s[lo:hi, :] = dot(entering, cm, TN) + keep * later

    d_inner = jnp.where(same, dcb[...], 0.0).astype(BF)
    d_b += dot(d_inner, cm, NN)
    d_c += dot(d_inner, bm, TN)
    through_silu(d_b, width, width + STATE)
    through_silu(d_c, width + STATE, conv_width)

    d_cum += colsum[...].T - d_dt * dt
    d_cum += jnp.where(iota2((BLOCK, LANES), 0) == BLOCK - 1, d_last, 0.0)
    d_a = running_sum(d_cum, True)
    d_raw = (d_dt + d_a * a_neg) * jax.nn.sigmoid(lifted)
    d_raw = jnp.where(lane < hl, d_raw, 0.0)
    dproj[:, conv_width : conv_width + LANES] = d_raw.astype(BF)
    dvec[0:1, :] += jnp.sum(d_a * dt, axis=0, keepdims=True) * a_neg
    dvec[1:2, :] += d_skip
    dvec[2:3, :] += jnp.sum(d_raw, axis=0, keepdims=True)

    for lo in range(0, conv_width, LANES):
        hi = lo + LANES
        grad = conv_w[CONV - 1 : CONV, lo:hi] * dwin[0:BLOCK, lo:hi]
        for tap in range(CONV - 1):
            ahead = CONV - 1 - tap
            grad += conv_w[tap : tap + 1, lo:hi] * (dwin[ahead : ahead + BLOCK, lo:hi] * aux_v[:, 5 + tap : 6 + tap])
        dproj[:, lo:hi] = grad.astype(BF)
        own = dwin[0:BLOCK, lo:hi]
        fold = lambda a: jnp.sum(a.reshape(BLOCK // 8, 8, LANES), axis=0)
        dconv[CONV * 8 : CONV * 8 + 8, lo:hi] += fold(own)
        dconv[(CONV - 1) * 8 : CONV * 8, lo:hi] += fold(own * window[8 : 8 + BLOCK, lo:hi])
        for tap in range(CONV - 1):
            moved = window[5 + tap : 5 + tap + BLOCK, lo:hi] * aux_v[:, tap : tap + 1]
            dconv[tap * 8 : tap * 8 + 8, lo:hi] += fold(own * moved)
    dwin[BLOCK : BLOCK + 8, :] = dwin[0:8, :]


def segment_aux(segments):
    micro, length = segments.shape
    nb = length // BLOCK
    seg = segments.astype(F32)
    blocks = seg.reshape(micro, nb, BLOCK)
    prev = jnp.concatenate([jnp.full((micro, 1), -1.0, F32), blocks[:, :-1, -1]], axis=1)
    entry = (blocks == prev[:, :, None]).reshape(micro, length)
    end = (blocks == blocks[:, :, -1:]).reshape(micro, length)
    cols = []
    for tap in range(CONV - 1):
        back = CONV - 1 - tap
        cols.append(jnp.pad(seg, ((0, 0), (back, 0)), constant_values=-1.0)[:, :length] == seg)
    cols += [entry, end]
    for tap in range(CONV - 1):
        ahead = CONV - 1 - tap
        cols.append(jnp.pad(seg, ((0, 0), (0, ahead)), constant_values=-1.0)[:, ahead:] == seg)
    cols.append(seg)
    cols = [c.astype(F32) for c in cols] + [jnp.zeros_like(seg)] * 7
    aux = jnp.stack(cols, axis=-1).reshape(micro * length, 16)
    seg_row = jnp.broadcast_to(blocks.reshape(micro * nb, 1, BLOCK), (micro * nb, 8, BLOCK)).reshape(micro * nb * 8, BLOCK)
    return aux, seg_row


def scan_forward(place, proj, conv_w, rows, aux, seg_row, hl):
    tokens = proj.shape[0]
    nb = tokens // MICRO // BLOCK
    width = hl * HEADDIM
    conv_width = width + 2 * STATE
    held = lambda m, j, place: (m * nb + (j ^ place[0]), 0)
    at = lambda m, j, place: (m * nb + j, 0)
    whole = lambda m, j, place: (0, 0)
    grid_spec = pltpu.PrefetchScalarGridSpec(
        num_scalar_prefetch=1,
        grid=(MICRO, nb),
        in_specs=[
            pl.BlockSpec((BLOCK, conv_width + LANES), held),
            pl.BlockSpec((8, conv_width), whole),
            pl.BlockSpec(rows.shape, whole),
            pl.BlockSpec((BLOCK, 16), at),
            pl.BlockSpec((8, BLOCK), at),
        ],
        out_specs=[
            pl.BlockSpec((BLOCK, width), held),
            pl.BlockSpec((1, width, STATE), lambda m, j, place: (m * nb + j, 0, 0)),
        ],
        scratch_shapes=[
            pltpu.VMEM((BLOCK + 8, conv_width), F32),
            pltpu.VMEM((BLOCK, conv_width), BF),
            pltpu.VMEM((width, STATE), F32),
        ],
    )
    return pl.pallas_call(
        functools.partial(forward_kernel, hl=hl),
        grid_spec=grid_spec,
        out_shape=[
            jax.ShapeDtypeStruct((tokens, width), BF),
            jax.ShapeDtypeStruct((MICRO * nb, width, STATE), BF),
        ],
        compiler_params=pltpu.CompilerParams(vmem_limit_bytes=VMEM, dimension_semantics=("arbitrary", "arbitrary")),
        name="scan_forward",
    )(place, proj, conv_w, rows, aux, seg_row)


def scan_backward(place, proj, conv_w, rows, aux, seg_row, dy, states, hl):
    tokens = proj.shape[0]
    nb = tokens // MICRO // BLOCK
    width = hl * HEADDIM
    conv_width = width + 2 * STATE
    full = conv_width + LANES
    held = lambda m, j, place: (m * nb + ((nb - 1 - j) ^ place[0]), 0)
    ahead_of = lambda m, j, place: ((m * nb + (jnp.maximum(nb - 2 - j, 0) ^ place[0])) * (BLOCK // 16) + BLOCK // 16 - 1, 0)
    at = lambda m, j, place: (m * nb + nb - 1 - j, 0)
    whole = lambda m, j, place: (0, 0)
    grid_spec = pltpu.PrefetchScalarGridSpec(
        num_scalar_prefetch=1,
        grid=(MICRO, nb),
        in_specs=[
            pl.BlockSpec((BLOCK, full), held),
            pl.BlockSpec((16, full), ahead_of),
            pl.BlockSpec((8, conv_width), whole),
            pl.BlockSpec(rows.shape, whole),
            pl.BlockSpec((BLOCK, 16), at),
            pl.BlockSpec((8, BLOCK), at),
            pl.BlockSpec((BLOCK, width), held),
            pl.BlockSpec((1, width, STATE), lambda m, j, place: (m * nb + nb - 1 - j, 0, 0)),
        ],
        out_specs=[
            pl.BlockSpec((BLOCK, full), held),
            pl.BlockSpec((8 * (CONV + 1), conv_width), whole),
            pl.BlockSpec((8, LANES), whole),
        ],
        scratch_shapes=[
            pltpu.VMEM((BLOCK + 8, conv_width), F32),
            pltpu.VMEM((BLOCK, conv_width), BF),
            pltpu.VMEM((BLOCK + 8, conv_width), F32),
            pltpu.VMEM((width, STATE), F32),
            pltpu.VMEM((BLOCK, BLOCK), F32),
            pltpu.VMEM((LANES, BLOCK), F32),
        ],
    )
    return pl.pallas_call(
        functools.partial(backward_kernel, hl=hl),
        grid_spec=grid_spec,
        out_shape=[
            jax.ShapeDtypeStruct((tokens, full), BF),
            jax.ShapeDtypeStruct((8 * (CONV + 1), conv_width), F32),
            jax.ShapeDtypeStruct((8, LANES), F32),
        ],
        compiler_params=pltpu.CompilerParams(vmem_limit_bytes=VMEM, dimension_semantics=("arbitrary", "arbitrary")),
        name="scan_backward",
    )(place, proj, proj, conv_w, rows, aux, seg_row, dy, states)


def scan_rows(a_log, skip, dt_bias, hl):
    width = max(hl * HEADDIM, LANES)
    pad = lambda v: jnp.pad(v, (0, width - v.shape[0]))
    return jnp.pad(jnp.stack([pad(dt_bias), pad(-jnp.exp(a_log)), pad(jnp.repeat(skip, HEADDIM))]), ((0, 5), (0, 0)))


def swapped(value, axis, mask):
    return lax.ppermute(value, axis, [(i, i ^ mask) for i in range(lax.axis_size(axis))])


def axis_bits(axis):
    return [1 << i for i in range(lax.axis_size(axis).bit_length() - 1)]


def micro_order(micro, axis):
    bits = axis_bits(axis)
    return bits if micro % 2 == 0 else bits[::-1]


def gather_pieces(own):
    out = []
    for micro in range(MICRO):
        pieces = {0: own[micro]}
        for bit in micro_order(micro, "seq"):
            for at in list(pieces):
                pieces[at ^ bit] = swapped(pieces[at], "seq", bit)
        out += [pieces[at] for at in range(len(pieces))]
    return jnp.concatenate(out, axis=0)


def scatter_pieces(parts):
    out = []
    for micro in range(MICRO):
        pieces = {at: parts[micro, at] for at in range(parts.shape[1])}
        for bit in micro_order(micro, "seq"):
            pieces = {
                at: (pieces[at].astype(F32) + swapped(pieces[at | bit], "seq", bit).astype(F32)).astype(BF)
                for at in pieces
                if not at & bit
            }
        out.append(pieces[0])
    return jnp.stack(out)


def exchange(table, rank):
    n = table.shape[0]
    out = jnp.zeros_like(table)
    for mask in range(n):
        entry = lax.dynamic_index_in_dim(table, rank ^ mask, 0, True)
        if mask:
            entry = swapped(entry, "seq", mask)
        out = lax.dynamic_update_slice_in_dim(out, entry, rank ^ mask, 0)
    return out


def sum_all(value):
    for axis in ("dp", "seq"):
        for bit in axis_bits(axis):
            value = value + swapped(value, axis, bit)
    return value


def sum_pieces(value):
    n = value.shape[-2]
    total = value
    for mask in range(1, n):
        got = swapped(value, "seq", mask)
        total = total + jnp.concatenate([got[..., at ^ mask : (at ^ mask) + 1, :] for at in range(n)], axis=-2)
    return total


def adamw(master, gradient, first, second, clip, decay):
    clipped = gradient * clip
    first_new = BETA_ONE * first + (1.0 - BETA_ONE) * clipped
    second_new = BETA_TWO * second + (1.0 - BETA_TWO) * clipped * clipped
    update = first_new / FIX_ONE / (jnp.sqrt(second_new / FIX_TWO) + ADAM_EPS) + decay * master
    return (-LEARN_RATE * update, first_new, second_new)


def per_device(tokens, cotangent, segments, in_weight, in_m, in_v, conv_weight, conv_m, conv_v,
               out_weight, out_m, out_v, packed, packed_m, packed_v):
    n = lax.axis_size("seq")
    rank = lax.axis_index("seq")
    place = rank.astype(jnp.int32).reshape(1)
    ndev = n * lax.axis_size("dp")
    hl = HEADS // n
    xw = hl * HEADDIM
    rows = D // ndev
    piece = tokens.shape[1]
    count = MICRO * n * piece
    xs = INNER + INNER
    bc = 2 * STATE
    xc = xw + bc + LANES
    cw = conv_weight.shape[1]
    conv_cols = -(-(CONV + 1) * cw // rows)

    in_low = in_weight.astype(BF)
    out_low = out_weight.astype(BF).T
    conv_flat = conv_weight.astype(BF).reshape(-1)
    conv_flat = jnp.pad(conv_flat, (0, conv_cols * rows - conv_flat.shape[0])).reshape(rows, conv_cols)
    by_rank = lambda a: a.reshape(rows, n, -1).transpose(1, 0, 2)
    to_all = lambda a: jnp.broadcast_to(a[None], (n,) + a.shape)
    steps = jnp.concatenate([by_rank(in_low[:, xs + bc :]), to_all(conv_flat), jnp.zeros((n, rows, LANES - hl - conv_cols), BF)], axis=2)
    send_x = jnp.concatenate([by_rank(in_low[:, INNER:xs]), to_all(in_low[:, xs : xs + bc]), steps], axis=2)
    send_z = by_rank(in_low[:, :INNER])
    send_o = by_rank(out_low)
    w_x = lax.all_gather(exchange(send_x, rank).reshape(n * rows, -1), "dp", axis=0, tiled=True)
    w_z = lax.all_gather(exchange(send_z, rank).reshape(n * rows, -1), "dp", axis=0, tiled=True)
    w_o = lax.all_gather(exchange(send_o, rank).reshape(n * rows, -1), "dp", axis=0, tiled=True)
    conv_full = w_x[:, xw + bc + hl : xw + bc + hl + conv_cols].reshape(ndev, rows * conv_cols)[:, : (CONV + 1) * cw]
    conv_full = conv_full.reshape(ndev, CONV + 1, cw).transpose(1, 0, 2).reshape(CONV + 1, CH)
    conv_loc = jnp.concatenate([lax.dynamic_slice_in_dim(conv_full, rank * xw, xw, 1), conv_full[:, INNER:]], axis=1).astype(F32)
    conv_loc = jnp.pad(conv_loc, ((0, 8 - CONV - 1), (0, 0)))

    a_log = lax.dynamic_slice_in_dim(packed, rank * hl, hl)
    skip = lax.dynamic_slice_in_dim(packed, HEADS + rank * hl, hl)
    dt_bias = lax.dynamic_slice_in_dim(packed, 2 * HEADS + rank * hl, hl)
    gain_in = packed[3 * HEADS : 3 * HEADS + D]
    gain_out = lax.dynamic_slice_in_dim(packed, 3 * HEADS + D + rank * xw, xw)
    aux, seg_row = segment_aux(segments)
    scan_row = scan_rows(a_log, skip, dt_bias, hl)

    tok = tokens.astype(F32)
    r_in = lax.rsqrt(jnp.mean(tok * tok, axis=-1, keepdims=True) + NORM_EPS)
    hidden = gather_pieces((tok * r_in * gain_in).astype(BF))
    cot = gather_pieces(cotangent)

    proj_x = dot(hidden, w_x, NN).astype(BF)
    y, states = scan_forward(place, proj_x, conv_loc, scan_row, aux, seg_row, hl)
    z = dot(hidden, w_z, NN).astype(BF).astype(F32)
    y = y.astype(F32)
    sig = jax.nn.sigmoid(z)
    gz = y * z * sig
    dnr = dot(cot, w_o, NN)
    dng = dnr * gain_out
    sums = jnp.stack([jnp.sum(gz * gz, axis=1), jnp.sum(dng * gz, axis=1)])
    sums = sum_pieces(sums.reshape(2, MICRO, n, piece)).reshape(2, count)
    r = lax.rsqrt(sums[0] / INNER + NORM_EPS)
    normed = (gz * r[:, None] * gain_out).astype(BF)
    d_gz = r[:, None] * dng - gz * (r * r * r * sums[1] / INNER)[:, None]
    d_gain_out = jnp.sum(dnr * gz * r[:, None], axis=0)
    dy = (d_gz * z * sig).astype(BF)
    dz = (d_gz * y * (sig * (1.0 + z * (1.0 - sig)))).astype(BF)

    scatter = lambda a: lax.psum_scatter(a, "dp", scatter_dimension=0, tiled=True).reshape(n, rows, -1)
    out_part = dot(normed, w_o, NT).astype(BF).reshape(MICRO, n, piece, D)
    output = (tok + scatter_pieces(out_part).astype(F32)).astype(BF)
    got_o = exchange(scatter(dot(cot, normed, TN).astype(BF)), rank)
    got_z = exchange(scatter(dot(hidden, dz, TN).astype(BF)), rank)

    d_px, d_conv, d_vec = scan_backward(place, proj_x, conv_loc, scan_row, aux, seg_row, dy, states, hl)
    d_hid = (dot(dz, w_z, NT) + dot(d_px, w_x, NT)).astype(BF).reshape(MICRO, n, piece, D)
    d_hidden = scatter_pieces(d_hid).astype(F32)
    got_x = exchange(scatter(dot(hidden, d_px, TN).astype(BF)), rank)

    flat = lambda a: a.transpose(1, 0, 2).reshape(rows, -1)
    g_bc = jnp.sum(got_x[:, :, xw : xw + bc].astype(F32), axis=0)
    shard_in = jnp.concatenate(
        [flat(got_z).astype(F32), flat(got_x[:, :, :xw]).astype(F32), g_bc, flat(got_x[:, :, xw + bc : xw + bc + hl]).astype(F32)], axis=1
    )
    shard_out = flat(got_o).astype(F32).T

    dh = d_hidden * gain_in
    d_tok = r_in * (dh - tok * (r_in * r_in) * jnp.mean(dh * tok, axis=-1, keepdims=True))
    input_grad = (cotangent.astype(F32) + d_tok).astype(BF)

    d_conv = d_conv.reshape(CONV + 1, 8, -1).sum(axis=1)
    conv_part = lax.dynamic_update_slice(jnp.zeros((CONV + 1, CH), F32), d_conv[:, :xw], (0, rank * xw))
    conv_part = lax.dynamic_update_slice(conv_part, d_conv[:, xw:], (0, INNER))
    vec_part = jnp.zeros((3 * HEADS + INNER,), F32)
    for at in range(3):
        vec_part = lax.dynamic_update_slice(vec_part, d_vec[at, :hl], (at * HEADS + rank * hl,))
    vec_part = lax.dynamic_update_slice(vec_part, d_gain_out, (3 * HEADS + rank * xw,))
    small = jnp.concatenate([conv_part.reshape(-1), vec_part])
    small = jnp.pad(small, (0, -small.shape[0] % 1024)).reshape(-1, LANES)
    small = sum_all(small).reshape(-1)
    conv_tot = small[: (CONV + 1) * CH].reshape(CONV + 1, CH)
    vec_tot = small[(CONV + 1) * CH : (CONV + 1) * CH + 3 * HEADS + INNER]

    own = lax.axis_index("dp") * n + rank
    own_gain = lax.dynamic_slice_in_dim(gain_in, own * rows, rows)
    d_gain_in = jnp.sum(in_low.astype(F32) * shard_in, axis=1) / own_gain
    partial_sq = jnp.sum(shard_in * shard_in) + jnp.sum(shard_out * shard_out)
    last = lax.dynamic_update_slice(jnp.zeros((D + 1024,), F32), d_gain_in, (own * rows,))
    last = lax.dynamic_update_slice(last, partial_sq[None], (D,))
    last = sum_all(last.reshape(-1, LANES)).reshape(-1)
    vec_tot = jnp.concatenate([vec_tot[: 3 * HEADS], last[:D], vec_tot[3 * HEADS :]])
    shard_conv = lax.dynamic_slice_in_dim(conv_tot, own * cw, cw, 1)
    grad_norm = jnp.sqrt(last[D] + jnp.sum(conv_tot * conv_tot) + jnp.sum(vec_tot * vec_tot))
    clip = jnp.minimum(1.0, CLIP_NORM / (grad_norm + 1e-06))
    in_new = adamw(in_weight, shard_in, in_m, in_v, clip, WEIGHT_DECAY)
    conv_new = adamw(conv_weight, shard_conv, conv_m, conv_v, clip, WEIGHT_DECAY)
    out_new = adamw(out_weight, shard_out, out_m, out_v, clip, WEIGHT_DECAY)
    vec_new = adamw(packed, vec_tot, packed_m, packed_v, clip, 0.0)
    return (
        output, input_grad, grad_norm,
        in_weight + in_new[0], in_new[1], in_new[2],
        conv_new[0], conv_new[1], conv_new[2],
        out_weight + out_new[0], out_new[1], out_new[2],
        vec_new[0], vec_new[1], vec_new[2],
    )


def solution(mesh):
    tok, col, row = P(None, ALL, None), P(None, ALL), P(ALL, None)
    return jax.shard_map(
        per_device,
        mesh=mesh,
        in_specs=(tok, tok, P(None, "dp"), row, row, row, col, col, col, col, col, col, P(), P(), P()),
        out_specs=(tok, tok, P(), row, row, row, col, col, col, col, col, col, P(), P(), P()),
        check_vma=False,
    )
```

```python
import functools

import jax
import jax.numpy as jnp
from jax import lax
from jax.experimental import pallas as pl
from jax.experimental.pallas import tpu as pltpu
from jax.sharding import PartitionSpec as P

D = 2048
HEADS = 64
HEADDIM = 64
STATE = 128
CONV = 4
BLOCK = 256
MICRO = 2
INNER = 4096
CH = 4352
NORM_EPS = 1e-05
LEARN_RATE = 0.004
BETA_ONE = 0.9
BETA_TWO = 0.95
FIX_ONE = 1.0 - 0.9**10
FIX_TWO = 1.0 - 0.95**10
ADAM_EPS = 1e-08
WEIGHT_DECAY = 0.1
CLIP_NORM = 1.0
BF = jnp.bfloat16
F32 = jnp.float32
ALL = ("dp", "seq")


def dot(a, b, dims, out=F32):
    return lax.dot_general(a, b, (dims, ((), ())), preferred_element_type=out)


NN = ((1,), (0,))
NT = ((1,), (1,))
TN = ((0,), (0,))
LANES = 128
PAIR = 2 * HEADDIM
VMEM = 56 * 1024 * 1024
TINY = 1e-37
CAP = 85.0


def iota2(shape, dim):
    return lax.broadcasted_iota(jnp.int32, shape, dim)


def running_sum(values, reverse):
    row, col = iota2((BLOCK, BLOCK), 0), iota2((BLOCK, BLOCK), 1)
    ones = jnp.where(row <= col if reverse else row >= col, 1.0, 0.0).astype(BF)
    high = values.astype(BF)
    rest = values - high.astype(F32)
    mid = rest.astype(BF)
    low = (rest - mid.astype(F32)).astype(BF)
    return dot(ones, high, NN) + dot(ones, mid, NN) + dot(ones, low, NN)


def step_sizes(raw, bias, a_neg):
    lifted = raw + bias
    dt = jnp.maximum(lifted, 0.0) + jnp.log1p(jnp.exp(-jnp.abs(lifted)))
    cum = running_sum(dt * a_neg, False)
    return lifted, dt, cum


def pick(left, columns, first):
    return jnp.where(left, columns[:, first : first + 1], columns[:, first + 1 : first + 2])


def thirds(value):
    high = value.astype(BF).astype(F32)
    rest = value - high
    mid = rest.astype(BF).astype(F32)
    return high, mid, (rest - mid).astype(BF).astype(F32)


def gap_depth(hl):
    return -(-3 * hl // 16) * 16 + 16


def gap_left(values, hl):
    lane = iota2(values.shape, 1)
    base = gap_depth(hl) - 16
    out = jnp.where((lane >= base) & (lane < base + 3), 1.0, 0.0)
    for at, part in enumerate(thirds(values)):
        part = jnp.where(lane < hl, part, 0.0)
        out += pltpu.roll(part, at * hl, 1) if at else part
    return out[:, : base + 16].astype(BF)


def gap_right_init(right, hl):
    base = gap_depth(hl) - 16
    row, col = iota2((base, BLOCK), 0), iota2((base, BLOCK), 1)
    for h in range(hl):
        hit = (row == h) | (row == hl + h) | (row == 2 * hl + h)
        right[0:base, h * BLOCK : (h + 1) * BLOCK] = jnp.where(hit, 1.0, 0.0).astype(BF)


def gap_right_fill(right, values_t, hl):
    base = gap_depth(hl) - 16
    row = iota2((16, BLOCK), 0)
    high, mid, low = thirds(values_t)
    for h in range(hl):
        one = slice(h, h + 1)
        slab = jnp.where(row == 0, high[one], jnp.where(row == 1, mid[one], jnp.where(row == 2, low[one], 0.0)))
        right[base : base + 16, h * BLOCK : (h + 1) * BLOCK] = slab.astype(BF)


def head_spread_init(spreads, hl):
    row, col = iota2(spreads.shape, 0), iota2(spreads.shape, 1)
    spreads[...] = jnp.where((row & (LANES - 1)) == col // HEADDIM, 1.0, 0.0).astype(BF)


def head_spread(values, spreads):
    high = values.astype(BF)
    low = (values - high.astype(F32)).astype(BF)
    return dot(jnp.concatenate([high, low], axis=1), spreads[...], NN)


def head_sum(values, spreads):
    return dot(values, spreads[0:LANES, :], NT)


def stacked(left, pair_values):
    zero = jnp.zeros_like(pair_values)
    return jnp.concatenate([jnp.where(left, pair_values, zero), jnp.where(left, zero, pair_values)], axis=0)


def conv_chunk(window, conv_w, valid, lo, hi):
    out = conv_w[CONV : CONV + 1, lo:hi] + conv_w[CONV - 1 : CONV, lo:hi] * window[8 : 8 + BLOCK, lo:hi]
    for tap in range(CONV - 1):
        out += conv_w[tap : tap + 1, lo:hi] * (window[5 + tap : 5 + tap + BLOCK, lo:hi] * valid[tap])
    return out


def spread(aux_v, at):
    return jnp.broadcast_to(aux_v[:, at : at + 1], (BLOCK, LANES))


def forward_kernel(place, proj, conv_w, rows, aux, seg_row, y_out, s_out, window, act, state, right, carried, spreads, end_s, *, hl):
    width = hl * HEADDIM
    conv_width = width + 2 * STATE

    @pl.when(pl.program_id(1) == 0)
    def _():
        window[0:8, :] = jnp.zeros((8, conv_width), F32)
        state[...] = jnp.zeros(state.shape, F32)
        gap_right_init(right, hl)
        head_spread_init(spreads, hl)

    aux_v = aux[...]
    valid = [spread(aux_v, tap) for tap in range(CONV - 1)]
    for lo in range(0, conv_width, LANES):
        hi = lo + LANES
        window[8 : 8 + BLOCK, lo:hi] = proj[:, lo:hi].astype(F32)
        out = conv_chunk(window, conv_w, valid, lo, hi)
        act[:, lo:hi] = (out * jax.nn.sigmoid(out)).astype(BF)
    window[0:8, :] = window[BLOCK : BLOCK + 8, :]

    _, dt, cum = step_sizes(proj[:, conv_width : conv_width + LANES].astype(F32), rows[0:1, :LANES], rows[1:2, :LANES])
    entry = jnp.exp(cum) * aux_v[:, 3:4]
    dt_end = dt * jnp.exp(cum[BLOCK - 1 : BLOCK, :] - cum) * aux_v[:, 4:5]
    shifted = jnp.log(jnp.maximum(dt, TINY)) - cum
    gaps = gap_left(cum, hl)
    gap_right_fill(right, shifted.T, hl)
    bm, cm = act[:, width : width + STATE], act[:, width + STATE :]
    same = (aux_v[:, 8:9] == seg_row[0:1, :]) & (iota2((BLOCK, BLOCK), 0) >= iota2((BLOCK, BLOCK), 1))
    inner = jnp.where(same, dot(cm, bm, NT), 0.0)
    left = iota2((BLOCK, PAIR), 1) < HEADDIM
    top = iota2((PAIR, STATE), 0) < HEADDIM
    last = entry[BLOCK - 1 : BLOCK, :]
    s_out[0] = state[...].astype(BF)
    carried[...] = dot(cm, s_out[0], NT) * head_spread(entry, spreads)
    end_s[...] = head_spread(dt_end, spreads)
    for pair in range(hl // 2):
        first = 2 * pair
        lo, hi = pair * PAIR, (pair + 1) * PAIR
        xp = act[:, lo:hi]
        mix = []
        for h in (first, first + 1):
            decay = jnp.exp(jnp.minimum(dot(gaps, right[:, h * BLOCK : (h + 1) * BLOCK], NN), CAP))
            mix.append((inner * decay).astype(BF))
        xf = xp.astype(F32)
        y = dot(jnp.concatenate(mix, axis=1), stacked(left, xp), NN)
        y += carried[:, lo:hi] + rows[2:3, lo:hi] * xf
        y_out[:, lo:hi] = y.astype(BF)
        weighted = (xf * end_s[:, lo:hi]).astype(BF)
        keep = jnp.where(top, last[:, first : first + 1], last[:, first + 1 : first + 2])
        state[lo:hi, :] = keep * state[lo:hi, :] + dot(weighted, bm, TN)


def backward_kernel(place, proj, before, conv_w, rows, aux, seg_row, dy, s_in, *refs, hl):
    dproj, dconv, dvec, dskip, window, act, dwin, grad_s, dcb, colsum, dkeep, right, carried, later_w, spreads, picks, entry_s, end_s, used, into = refs[-20:]
    width = hl * HEADDIM
    conv_width = width + 2 * STATE

    @pl.when(pl.program_id(0) == 0)
    def _():
        dconv[...] = jnp.zeros(dconv.shape, F32)
        dvec[...] = jnp.zeros(dvec.shape, F32)
        dskip[...] = jnp.zeros(dskip.shape, F32)
        dwin[BLOCK : BLOCK + 8, :] = jnp.zeros((8, conv_width), F32)
        grad_s[...] = jnp.zeros(grad_s.shape, F32)
        colsum[...] = jnp.zeros(colsum.shape, F32)
        dkeep[...] = jnp.zeros(dkeep.shape, F32)
        gap_right_init(right, hl)
        head_spread_init(spreads, hl)
        picks[...] = jnp.where(iota2(picks.shape, 0) == iota2(picks.shape, 1) // BLOCK, 1.0, 0.0).astype(BF)

    aux_v = aux[...]
    window[0:8, :] = before[8:16, :conv_width].astype(F32)
    valid = [spread(aux_v, tap) for tap in range(CONV - 1)]
    for lo in range(0, conv_width, LANES):
        hi = lo + LANES
        window[8 : 8 + BLOCK, lo:hi] = proj[:, lo:hi].astype(F32)
        out = conv_chunk(window, conv_w, valid, lo, hi)
        sig = jax.nn.sigmoid(out)
        act[:, lo:hi] = (out * sig).astype(BF)
        dwin[0:BLOCK, lo:hi] = sig * (1.0 + out * (1.0 - sig))

    lifted, dt, cum = step_sizes(proj[:, conv_width : conv_width + LANES].astype(F32), rows[0:1, :LANES], rows[1:2, :LANES])
    a_neg = rows[1:2, :LANES]
    entry = jnp.exp(cum) * aux_v[:, 3:4]
    dt_end = dt * jnp.exp(cum[BLOCK - 1 : BLOCK, :] - cum) * aux_v[:, 4:5]
    gaps = gap_left(jnp.log(jnp.maximum(dt, TINY)) - cum, hl)
    gap_right_fill(right, cum.T, hl)
    bm, cm = act[:, width : width + STATE], act[:, width + STATE :]
    same = (aux_v[:, 8:9] == seg_row[0:1, :]) & (iota2((BLOCK, BLOCK), 0) <= iota2((BLOCK, BLOCK), 1))
    inner = jnp.where(same, dot(bm, cm, NT), 0.0)
    left = iota2((BLOCK, PAIR), 1) < HEADDIM
    top = iota2((PAIR, STATE), 0) < HEADDIM
    lane = iota2((BLOCK, LANES), 1)
    last = entry[BLOCK - 1 : BLOCK, :]
    d_row = jnp.zeros((BLOCK, LANES), F32)
    d_b = jnp.zeros((BLOCK, STATE), F32)
    d_c = jnp.zeros((BLOCK, STATE), F32)
    carried[...] = dot(cm, s_in[0], NT)
    end_s[...] = head_spread(dt_end, spreads)
    later_w[...] = dot(bm, grad_s[...].astype(BF), NT) * end_s[...]
    entry_s[...] = head_spread(entry, spreads)

    for pair in range(hl // 2):
        first = 2 * pair
        lo, hi = pair * PAIR, (pair + 1) * PAIR
        xp, dyp = act[:, lo:hi], dy[:, lo:hi]
        xf, dyf = xp.astype(F32), dyp.astype(F32)
        d_mix = dot(stacked(left, xp), dyp, NT)
        mix, pairwise = [], []
        d_inner = 0.0
        for at, h in enumerate((first, first + 1)):
            decay = jnp.exp(jnp.minimum(dot(gaps, right[:, h * BLOCK : (h + 1) * BLOCK], NN), CAP))
            mix.append((inner * decay).astype(BF))
            part = d_mix[at * BLOCK : (at + 1) * BLOCK] * decay
            d_inner += part
            part = (part * inner).astype(BF)
            pairwise.append(part)
            colsum[h : h + 1, :] = jnp.sum(part.astype(F32), axis=0, keepdims=True)
        d_row += dot(jnp.concatenate(pairwise, axis=1), picks[:, first * BLOCK : (first + 2) * BLOCK], NT)
        if pair == 0:
            dcb[...] = d_inner
        else:
            dcb[...] += d_inner
        later = grad_s[lo:hi, :]
        low = s_in[0, lo:hi, :]
        from_end = later_w[:, lo:hi]
        dx = dot(jnp.concatenate(mix, axis=1), stacked(left, dyp), NN) + from_end + rows[2:3, lo:hi] * dyf
        dwin[0:BLOCK, lo:hi] = dwin[0:BLOCK, lo:hi] * dx
        used[:, lo:hi] = (from_end * xf).astype(BF)
        entering = entry_s[:, lo:hi] * dyf
        into[:, lo:hi] = (entering * carried[:, lo:hi]).astype(BF)
        entering = entering.astype(BF)
        dskip[:, lo:hi] += jnp.sum((xf * dyf).reshape(BLOCK // 8, 8, PAIR), axis=0)
        kept = later * low.astype(F32)
        dkeep[first : first + 1, :] = jnp.sum(kept[:HEADDIM], axis=0, keepdims=True)
        dkeep[first + 1 : first + 2, :] = jnp.sum(kept[HEADDIM:], axis=0, keepdims=True)
        weighted = (xf * end_s[:, lo:hi]).astype(BF)
        d_b += dot(weighted, later.astype(BF), NN)
        d_c += dot(entering, low, NN)
        keep = jnp.where(top, last[:, first : first + 1], last[:, first + 1 : first + 2])
        grad_s[lo:hi, :] = dot(entering, cm, TN) + keep * later

    d_inner = jnp.where(same, dcb[...], 0.0).astype(BF)
    d_b += dot(d_inner, cm, NN)
    d_c += dot(d_inner, bm, TN)
    dwin[0:BLOCK, width : width + STATE] = dwin[0:BLOCK, width : width + STATE] * d_b
    dwin[0:BLOCK, width + STATE :] = dwin[0:BLOCK, width + STATE :] * d_c

    d_end = head_sum(used[...], spreads)
    d_cum = head_sum(into[...], spreads)
    through = d_row + d_end
    d_last = jnp.sum(d_end, axis=0, keepdims=True) + jnp.sum(dkeep[...].T, axis=0, keepdims=True) * last
    d_cum += colsum[...].T - through
    d_cum += jnp.where(iota2((BLOCK, LANES), 0) == BLOCK - 1, d_last, 0.0)
    d_a = running_sum(d_cum, True)
    sig = jax.nn.sigmoid(lifted)
    d_raw = through * jnp.where(dt > TINY, sig / jnp.maximum(dt, TINY), 1.0) + d_a * a_neg * sig
    d_raw = jnp.where(lane < hl, d_raw, 0.0)
    dproj[:, conv_width : conv_width + LANES] = d_raw.astype(BF)
    dvec[0:1, :] += jnp.sum(d_a * dt, axis=0, keepdims=True) * a_neg
    dvec[1:2, :] += jnp.sum(d_raw, axis=0, keepdims=True)

    valid = [spread(aux_v, 5 + tap) for tap in range(CONV - 1)]
    fold = lambda a: jnp.sum(a.reshape(BLOCK // 8, 8, LANES), axis=0)
    for lo in range(0, conv_width, LANES):
        hi = lo + LANES
        own = dwin[0:BLOCK, lo:hi]
        value = window[8 : 8 + BLOCK, lo:hi]
        grad = conv_w[CONV - 1 : CONV, lo:hi] * own
        dconv[CONV * 8 : CONV * 8 + 8, lo:hi] += fold(own)
        dconv[(CONV - 1) * 8 : CONV * 8, lo:hi] += fold(own * value)
        for tap in range(CONV - 1):
            ahead = CONV - 1 - tap
            moved = dwin[ahead : ahead + BLOCK, lo:hi] * valid[tap]
            grad += conv_w[tap : tap + 1, lo:hi] * moved
            dconv[tap * 8 : tap * 8 + 8, lo:hi] += fold(moved * value)
        dproj[:, lo:hi] = grad.astype(BF)
    dwin[BLOCK : BLOCK + 8, :] = dwin[0:8, :]


def segment_aux(segments):
    micro, length = segments.shape
    nb = length // BLOCK
    seg = segments.astype(F32)
    blocks = seg.reshape(micro, nb, BLOCK)
    prev = jnp.concatenate([jnp.full((micro, 1), -1.0, F32), blocks[:, :-1, -1]], axis=1)
    entry = (blocks == prev[:, :, None]).reshape(micro, length)
    end = (blocks == blocks[:, :, -1:]).reshape(micro, length)
    cols = []
    for tap in range(CONV - 1):
        back = CONV - 1 - tap
        cols.append(jnp.pad(seg, ((0, 0), (back, 0)), constant_values=-1.0)[:, :length] == seg)
    cols += [entry, end]
    for tap in range(CONV - 1):
        ahead = CONV - 1 - tap
        cols.append(jnp.pad(seg, ((0, 0), (0, ahead)), constant_values=-1.0)[:, ahead:] == seg)
    cols.append(seg)
    cols = [c.astype(F32) for c in cols] + [jnp.zeros_like(seg)] * 7
    aux = jnp.stack(cols, axis=-1).reshape(micro * length, 16)
    seg_row = jnp.broadcast_to(blocks.reshape(micro * nb, 1, BLOCK), (micro * nb, 8, BLOCK)).reshape(micro * nb * 8, BLOCK)
    return aux, seg_row


def scan_forward(place, proj, conv_w, rows, aux, seg_row, hl):
    tokens = proj.shape[0]
    nb = tokens // MICRO // BLOCK
    width = hl * HEADDIM
    conv_width = width + 2 * STATE
    held = lambda m, j, place: (m * nb + (j ^ place[0]), 0)
    at = lambda m, j, place: (m * nb + j, 0)
    whole = lambda m, j, place: (0, 0)
    grid_spec = pltpu.PrefetchScalarGridSpec(
        num_scalar_prefetch=1,
        grid=(MICRO, nb),
        in_specs=[
            pl.BlockSpec((BLOCK, conv_width + LANES), held),
            pl.BlockSpec((8, conv_width), whole),
            pl.BlockSpec(rows.shape, whole),
            pl.BlockSpec((BLOCK, 16), at),
            pl.BlockSpec((8, BLOCK), at),
        ],
        out_specs=[
            pl.BlockSpec((BLOCK, width), held),
            pl.BlockSpec((1, width, STATE), lambda m, j, place: (m * nb + j, 0, 0)),
        ],
        scratch_shapes=[
            pltpu.VMEM((BLOCK + 8, conv_width), F32),
            pltpu.VMEM((BLOCK, conv_width), BF),
            pltpu.VMEM((width, STATE), F32),
            pltpu.VMEM((gap_depth(hl), hl * BLOCK), BF),
            pltpu.VMEM((BLOCK, width), F32),
            pltpu.VMEM((2 * LANES, width), BF),
            pltpu.VMEM((BLOCK, width), F32),
        ],
    )
    return pl.pallas_call(
        functools.partial(forward_kernel, hl=hl),
        grid_spec=grid_spec,
        out_shape=[
            jax.ShapeDtypeStruct((tokens, width), BF),
            jax.ShapeDtypeStruct((MICRO * nb, width, STATE), BF),
        ],
        compiler_params=pltpu.CompilerParams(vmem_limit_bytes=VMEM, dimension_semantics=("arbitrary", "arbitrary")),
        name="scan_forward",
    )(place, proj, conv_w, rows, aux, seg_row)


def scan_backward(place, micro, proj, conv_w, rows, aux, seg_row, dy, states, hl, *done):
    tokens = proj.shape[0] // MICRO
    nb = tokens // BLOCK
    width = hl * HEADDIM
    conv_width = width + 2 * STATE
    full = conv_width + LANES
    first = micro * nb
    held = lambda j, place: (first + ((nb - 1 - j) ^ place[0]), 0)
    ahead_of = lambda j, place: ((first + (jnp.maximum(nb - 2 - j, 0) ^ place[0])) * (BLOCK // 16) + BLOCK // 16 - 1, 0)
    at = lambda j, place: (first + nb - 1 - j, 0)
    whole = lambda j, place: (0, 0)
    grid_spec = pltpu.PrefetchScalarGridSpec(
        num_scalar_prefetch=1,
        grid=(nb,),
        in_specs=[
            pl.BlockSpec((BLOCK, full), held),
            pl.BlockSpec((16, full), ahead_of),
            pl.BlockSpec((8, conv_width), whole),
            pl.BlockSpec(rows.shape, whole),
            pl.BlockSpec((BLOCK, 16), at),
            pl.BlockSpec((8, BLOCK), at),
            pl.BlockSpec((BLOCK, width), held),
            pl.BlockSpec((1, width, STATE), lambda j, place: (first + nb - 1 - j, 0, 0)),
        ]
        + [pl.BlockSpec(memory_space=pl.ANY)] * len(done),
        out_specs=[
            pl.BlockSpec((BLOCK, full), lambda j, place: ((nb - 1 - j) ^ place[0], 0)),
            pl.BlockSpec((8 * (CONV + 1), conv_width), whole),
            pl.BlockSpec((8, LANES), whole),
            pl.BlockSpec((8, width), whole),
        ],
        scratch_shapes=[
            pltpu.VMEM((BLOCK + 8, conv_width), F32),
            pltpu.VMEM((BLOCK, conv_width), BF),
            pltpu.VMEM((BLOCK + 8, conv_width), F32),
            pltpu.VMEM((width, STATE), F32),
            pltpu.VMEM((BLOCK, BLOCK), F32),
            pltpu.VMEM((LANES, BLOCK), F32),
            pltpu.VMEM((LANES, STATE), F32),
            pltpu.VMEM((gap_depth(hl), hl * BLOCK), BF),
            pltpu.VMEM((BLOCK, width), F32),
            pltpu.VMEM((BLOCK, width), F32),
            pltpu.VMEM((2 * LANES, width), BF),
            pltpu.VMEM((LANES, hl * BLOCK), BF),
            pltpu.VMEM((BLOCK, width), F32),
            pltpu.VMEM((BLOCK, width), F32),
            pltpu.VMEM((BLOCK, width), BF),
            pltpu.VMEM((BLOCK, width), BF),
        ],
    )
    return pl.pallas_call(
        functools.partial(backward_kernel, hl=hl),
        grid_spec=grid_spec,
        out_shape=[
            jax.ShapeDtypeStruct((tokens, full), BF),
            jax.ShapeDtypeStruct((8 * (CONV + 1), conv_width), F32),
            jax.ShapeDtypeStruct((8, LANES), F32),
            jax.ShapeDtypeStruct((8, width), F32),
        ],
        compiler_params=pltpu.CompilerParams(vmem_limit_bytes=VMEM, dimension_semantics=("arbitrary",)),
        name="scan_backward",
    )(place, proj, proj, conv_w, rows, aux, seg_row, dy, states, *done)


def scan_rows(a_log, skip, dt_bias, hl):
    width = max(hl * HEADDIM, LANES)
    pad = lambda v: jnp.pad(v, (0, width - v.shape[0]))
    return jnp.pad(jnp.stack([pad(dt_bias), pad(-jnp.exp(a_log)), pad(jnp.repeat(skip, HEADDIM))]), ((0, 5), (0, 0)))


def fetch(pieces, buffer, sems, step):
    @pl.when(step == 0)
    def _():
        pltpu.make_async_copy(pieces[0], buffer.at[0], sems.at[0]).start()

    for at in range(1, len(pieces)):

        @pl.when(step == at - 1)
        def _():
            pltpu.make_async_copy(pieces[at], buffer.at[at % 2], sems.at[at % 2]).start()

    slot = step % 2
    pltpu.make_async_copy(pieces[0], buffer.at[slot], sems.at[slot]).wait()
    return slot


def fixed(array):
    return pl.BlockSpec(array.shape, lambda i: (0, 0), pipeline_mode=pl.Buffered(1))


def by_rows(width):
    return pl.BlockSpec((BLOCK, width), lambda i: (i, 0))


def arbitrary(name):
    return dict(compiler_params=pltpu.CompilerParams(vmem_limit_bytes=VMEM, dimension_semantics=("arbitrary",)), name=name)


def in_kernel(*refs, count):
    pieces, w, (proj, hidden, buffer, sems) = refs[:count], refs[count], refs[-4:]
    slot = fetch(pieces, buffer, sems, pl.program_id(0))
    value = buffer[slot]
    hidden[...] = value
    proj[...] = dot(value, w[...], NN).astype(BF)


def in_project(pieces, w, *done):
    count = len(pieces)
    depth, width = w.shape
    return pl.pallas_call(
        functools.partial(in_kernel, count=count),
        grid=(count,),
        in_specs=[pl.BlockSpec(memory_space=pl.ANY)] * count + [fixed(w)] + [pl.BlockSpec(memory_space=pl.ANY)] * len(done),
        out_specs=[by_rows(width), by_rows(depth)],
        out_shape=[
            jax.ShapeDtypeStruct((count * BLOCK, width), BF),
            jax.ShapeDtypeStruct((count * BLOCK, depth), BF),
        ],
        scratch_shapes=[pltpu.VMEM((2, BLOCK, depth), BF), pltpu.SemaphoreType.DMA((2,))],
        **arbitrary("in_project"),
    )(*pieces, w, *done)


def gate_kernel(*refs, count):
    pieces, (hidden, w_z, w_o, y, gain, z_out, dn_out, cot_out, sums, buffer, sems) = refs[:count], refs[count:]
    slot = fetch(pieces, buffer, sems, pl.program_id(0))
    cot = buffer[slot]
    cot_out[...] = cot
    z = dot(hidden[...], w_z[...], NN).astype(BF)
    z_out[...] = z
    dn = dot(cot, w_o[...], NN)
    dn_out[...] = dn.astype(BF)
    z = z.astype(F32)
    gz = y[...].astype(F32) * (z * jax.nn.sigmoid(z))
    ones = jnp.ones((8, gz.shape[1]), BF)
    first = dot(ones, (gz * gz).astype(BF), NT)
    second = dot(ones, (dn * gain[0:1, :] * gz).astype(BF), NT)
    sums[...] = jnp.where(iota2((8, BLOCK), 0) == 0, first, second)


def gate_forward(pieces, hidden, w_z, w_o, y, gain):
    count = len(pieces)
    depth, width = w_z.shape
    return pl.pallas_call(
        functools.partial(gate_kernel, count=count),
        grid=(count,),
        in_specs=[pl.BlockSpec(memory_space=pl.ANY)] * count + [by_rows(depth), fixed(w_z), fixed(w_o), by_rows(width), fixed(gain)],
        out_specs=[by_rows(width), by_rows(width), by_rows(depth), pl.BlockSpec((8, BLOCK), lambda i: (i, 0))],
        out_shape=[
            jax.ShapeDtypeStruct((count * BLOCK, width), BF),
            jax.ShapeDtypeStruct((count * BLOCK, width), BF),
            jax.ShapeDtypeStruct((count * BLOCK, depth), BF),
            jax.ShapeDtypeStruct((count * 8, BLOCK), F32),
        ],
        scratch_shapes=[pltpu.VMEM((2, BLOCK, depth), BF), pltpu.SemaphoreType.DMA((2,))],
        **arbitrary("gate_forward"),
    )(*pieces, hidden, w_z, w_o, y, gain)


def out_kernel(z_in, dn_in, y_in, sums, gain, w_o, normed, dy, dz, out, dgain):
    @pl.when(pl.program_id(0) == 0)
    def _():
        dgain[...] = jnp.zeros(dgain.shape, F32)

    scale = lax.rsqrt(sums[0:1, :] / INNER + NORM_EPS)
    slope = scale * scale * scale * sums[1:2, :] / INNER
    row = iota2((LANES, BLOCK), 0)
    columns = jnp.where(row == 0, scale, jnp.where(row == 1, slope, 0.0)).T
    scale, slope = columns[:, 0:1], columns[:, 1:2]
    for lo in range(0, normed.shape[1], 2 * LANES):
        hi = lo + 2 * LANES
        z, y, dn = z_in[:, lo:hi].astype(F32), y_in[:, lo:hi].astype(F32), dn_in[:, lo:hi].astype(F32)
        sig = jax.nn.sigmoid(z)
        silu = z * sig
        gz = y * silu
        unit = gz * scale
        normed[:, lo:hi] = (unit * gain[0:1, lo:hi]).astype(BF)
        dgain[:, lo:hi] += jnp.sum((dn * unit).reshape(BLOCK // 8, 8, 2 * LANES), axis=0)
        d_gz = dn * gain[0:1, lo:hi] * scale - gz * slope
        dy[:, lo:hi] = (d_gz * silu).astype(BF)
        dz[:, lo:hi] = (d_gz * y * (sig + silu * (1.0 - sig))).astype(BF)
    out[...] = dot(normed[...], w_o[...], NT).astype(BF)


def out_project(z, dn, y, sums, gain, w_o):
    depth, width = w_o.shape
    tokens = z.shape[0]
    one = by_rows(width)
    return pl.pallas_call(
        out_kernel,
        grid=(tokens // BLOCK,),
        in_specs=[one, one, one, pl.BlockSpec((8, BLOCK), lambda i: (i, 0)), fixed(gain), fixed(w_o)],
        out_specs=[one, one, one, by_rows(depth), pl.BlockSpec((8, width), lambda i: (0, 0))],
        out_shape=[jax.ShapeDtypeStruct((tokens, width), BF)] * 3
        + [jax.ShapeDtypeStruct((tokens, depth), BF), jax.ShapeDtypeStruct((8, width), F32)],
        **arbitrary("out_project"),
    )(z, dn, y, sums, gain, w_o)


def back_kernel(dz, px, w_z, w_x, out):
    out[...] = (dot(dz[...], w_z[...], NT) + dot(px[...], w_x[...], NT)).astype(BF)


def back_project(micro, dz, px, w_z, w_x):
    tokens, width = px.shape
    depth = w_z.shape[0]
    first = micro * tokens // BLOCK
    return pl.pallas_call(
        back_kernel,
        grid=(tokens // BLOCK,),
        in_specs=[pl.BlockSpec((BLOCK, dz.shape[1]), lambda i: (first + i, 0)), by_rows(width), fixed(w_z), fixed(w_x)],
        out_specs=by_rows(depth),
        out_shape=jax.ShapeDtypeStruct((tokens, depth), BF),
        **arbitrary("back_project"),
    )(dz, px, w_z, w_x)

def swapped(value, axis, mask):
    return lax.ppermute(value, axis, [(i, i ^ mask) for i in range(lax.axis_size(axis))])


def axis_bits(axis):
    return [1 << i for i in range(lax.axis_size(axis).bit_length() - 1)]


def micro_order(micro, axis):
    bits = axis_bits(axis)
    return bits if micro % 2 == 0 else bits[::-1]


def nothing(*refs):
    pass


def after(values, *done):
    values = list(values)
    anywhere = pl.BlockSpec(memory_space=pl.ANY)
    held = pl.pallas_call(
        nothing,
        in_specs=[anywhere] * (len(values) + len(done)),
        out_specs=[anywhere] * len(values),
        out_shape=[jax.ShapeDtypeStruct(v.shape, v.dtype) for v in values],
        input_output_aliases={at: at for at in range(len(values))},
        name="after",
    )(*values, *done)
    return list(held)


def gather_stages(own):
    held = [{0: own[micro]} for micro in range(MICRO)]
    for turn in range(len(axis_bits("seq"))):
        got = []
        for micro in range(MICRO):
            bit = micro_order(micro, "seq")[turn]
            got.append({at ^ bit: swapped(held[micro][at], "seq", bit) for at in held[micro]})
        wait = yield [piece for one in got for piece in one.values()], [piece for one in held for piece in one.values()]
        for micro in range(MICRO):
            if wait is not None:
                got[micro] = dict(zip(got[micro], after(got[micro].values(), *wait)))
            held[micro].update(got[micro])
    yield [held[micro][at] for micro in range(MICRO) for at in range(len(held[micro]))]


def scatter_stages(parts):
    some, n, piece, width = parts.shape
    pick = lambda a, at: jnp.concatenate([a[:, k : k + 1] for k in at], axis=1)
    held = [parts[:, :, half * piece // 2 : (half + 1) * piece // 2] for half in range(2)]
    places = [list(range(n)) for half in range(2)]
    for turn in range(len(axis_bits("seq"))):
        sent = []
        for half in range(2):
            bit = micro_order(half, "seq")[turn]
            away = [at for at, place in enumerate(places[half]) if place & bit]
            stay = [at for at, place in enumerate(places[half]) if not place & bit]
            sent.append((pick(held[half], away), bit))
            held[half] = pick(held[half], stay)
            places[half] = [places[half][at] for at in stay]
        got = [swapped(one, "seq", bit) for one, bit in sent]
        wait = yield got, [one for one, _ in sent]
        if wait is not None:
            got = after(got, *wait)
        held = [(one.astype(F32) + more.astype(F32)).astype(BF) for one, more in zip(held, got)]
    yield jnp.concatenate([one[:, 0] for one in held], axis=1), None


def finish(stages, wait=None):
    last = None
    try:
        while True:
            last = stages.send(wait)
    except StopIteration:
        return last[0]


def turned(entries, rank):
    entries = list(entries)
    for bit in axis_bits("seq"):
        flip = (rank & bit) != 0
        entries = [jnp.where(flip, entries[at ^ bit], entries[at]) for at in range(len(entries))]
    return entries


def exchange(entries, rank):
    entries = turned(entries, rank)
    return entries, [swapped(one, "seq", mask) for mask, one in enumerate(entries) if mask]


def sum_all(value):
    for axis in ("dp", "seq"):
        for bit in axis_bits(axis):
            value = value + swapped(value, axis, bit)
    return value


def sum_pieces(value):
    n = value.shape[-2]
    total = value
    for mask in range(1, n):
        got = swapped(value, "seq", mask)
        total = total + jnp.concatenate([got[..., at ^ mask : (at ^ mask) + 1, :] for at in range(n)], axis=-2)
    return total


def adamw(master, gradient, first, second, clip, decay):
    clipped = gradient * clip
    first_new = BETA_ONE * first + (1.0 - BETA_ONE) * clipped
    second_new = BETA_TWO * second + (1.0 - BETA_TWO) * clipped * clipped
    update = first_new / FIX_ONE / (jnp.sqrt(second_new / FIX_TWO) + ADAM_EPS) + decay * master
    return (-LEARN_RATE * update, first_new, second_new)


def per_device(tokens, cotangent, segments, in_weight, in_m, in_v, conv_weight, conv_m, conv_v,
               out_weight, out_m, out_v, packed, packed_m, packed_v):
    n = lax.axis_size("seq")
    rank = lax.axis_index("seq")
    place = rank.astype(jnp.int32).reshape(1)
    ndev = n * lax.axis_size("dp")
    hl = HEADS // n
    xw = hl * HEADDIM
    rows = D // ndev
    piece = tokens.shape[1]
    count = MICRO * n * piece
    xs = INNER + INNER
    bc = 2 * STATE
    xc = xw + bc + LANES
    cw = conv_weight.shape[1]
    conv_cols = -(-(CONV + 1) * cw // rows)

    in_low = in_weight.astype(BF)
    out_low = out_weight.astype(BF).T
    conv_flat = conv_weight.astype(BF).reshape(-1)
    conv_flat = jnp.pad(conv_flat, (0, conv_cols * rows - conv_flat.shape[0])).reshape(rows, conv_cols)
    column = lambda a, q, width: a[:, q * width : (q + 1) * width]
    pad = jnp.zeros((rows, LANES - hl - conv_cols), BF)
    send_x = [
        jnp.concatenate(
            [column(in_low[:, INNER:xs], q, xw), in_low[:, xs : xs + bc], column(in_low[:, xs + bc :], q, hl), conv_flat, pad], axis=1
        )
        for q in range(n)
    ]
    gain_in = packed[3 * HEADS : 3 * HEADS + D]
    send_x = turned(send_x, rank)
    got_wx = [one if not mask else swapped(one, "seq", mask) for mask, one in enumerate(send_x)]
    tok = tokens.astype(F32)
    r_in = lax.rsqrt(jnp.mean(tok * tok, axis=-1, keepdims=True) + NORM_EPS)
    hidden_stages = gather_stages((tok * r_in * gain_in).astype(BF))
    arrived, sent = next(hidden_stages)
    got_wx = jnp.concatenate(turned(got_wx[:1] + after(got_wx[1:], *sent), rank), axis=0)
    w_x = lax.all_gather(got_wx, "dp", axis=0, tiled=True)
    send_zo = jnp.stack(turned([jnp.concatenate([column(in_low, q, xw), column(out_low, q, xw)], axis=1) for q in range(n)], rank))
    [send_zo] = after([send_zo], got_wx, *arrived)
    got_wzo = [send_zo[mask] if not mask else swapped(send_zo[mask], "seq", mask) for mask in range(n)]
    got_wzo = jnp.concatenate(turned(got_wzo, rank), axis=0)
    w_z = lax.all_gather(got_wzo[:, :xw], "dp", axis=0, tiled=True)
    w_o = lax.all_gather(got_wzo[:, xw:], "dp", axis=0, tiled=True)
    conv_full = w_x[:, xw + bc + hl : xw + bc + hl + conv_cols].reshape(ndev, rows * conv_cols)[:, : (CONV + 1) * cw]
    conv_full = conv_full.reshape(ndev, CONV + 1, cw).transpose(1, 0, 2).reshape(CONV + 1, CH)
    conv_loc = jnp.concatenate([lax.dynamic_slice_in_dim(conv_full, rank * xw, xw, 1), conv_full[:, INNER:]], axis=1).astype(F32)
    conv_loc = jnp.pad(conv_loc, ((0, 8 - CONV - 1), (0, 0)))

    a_log = lax.dynamic_slice_in_dim(packed, rank * hl, hl)
    skip = lax.dynamic_slice_in_dim(packed, HEADS + rank * hl, hl)
    dt_bias = lax.dynamic_slice_in_dim(packed, 2 * HEADS + rank * hl, hl)
    gain_out = lax.dynamic_slice_in_dim(packed, 3 * HEADS + D + rank * xw, xw)
    aux, seg_row = segment_aux(segments)
    scan_row = scan_rows(a_log, skip, dt_bias, hl)

    for _ in axis_bits("seq")[1:]:
        arrived, _ = hidden_stages.send(None)
    proj_x, hidden = in_project(hidden_stages.send(None), w_x, conv_loc)

    [cot] = after([cotangent], *arrived)
    cot_stages = gather_stages(cot)
    next(cot_stages)
    y, states = scan_forward(place, proj_x, conv_loc, scan_row, aux, seg_row, hl)
    for bit in axis_bits("seq"):
        cot = cot_stages.send([proj_x] if bit == 1 else [y])
    gain = jnp.broadcast_to(gain_out[None], (8, xw))
    z, dn, cot, sums = gate_forward(cot, hidden, w_z, w_o, y, gain)
    sums = sum_pieces(sums.reshape(MICRO, n, 8 * BLOCK)).reshape(-1, BLOCK)
    normed, dy, dz, out_part, d_gain_out = out_project(z, dn, y, sums, gain, w_o)
    d_gain_out = jnp.sum(d_gain_out, axis=0)

    scatter = lambda a: lax.psum_scatter(a, "dp", scatter_dimension=0, tiled=True)
    split = lambda a: [a[q * rows : (q + 1) * rows] for q in range(n)]
    out_stages = scatter_stages(out_part.reshape(MICRO, n, piece, D))
    _, sent = next(out_stages)
    [normed] = after([normed], *sent)
    part_o = dot(cot, normed, TN).astype(BF)
    part_z = dot(hidden, dz, TN).astype(BF)
    got_o, got_z = scatter(part_o), scatter(part_z)

    through_in = lambda micro, one: back_project(micro, dz, one, w_z, w_x).reshape(1, n, piece, D)
    scan_back = lambda micro, *done: scan_backward(place, micro, proj_x, conv_loc, scan_row, aux, seg_row, dy, states, hl, *done)

    px_0, conv_0, vec_0, skip_0 = scan_back(0, part_o, part_z)
    hid_0 = through_in(0, px_0)
    out_got, out_sent = out_stages.send([hid_0])
    stages_0 = scatter_stages(hid_0)
    hid_got, sent = next(stages_0)
    px_1, conv_1, vec_1, skip_1 = scan_back(1, *sent, *out_sent)
    [px_1] = after([px_1], *hid_got)
    part_x = dot(hidden, jnp.concatenate([px_0, px_1], axis=0), TN).astype(BF)
    got_x = scatter(part_x)
    hid_got, sent = stages_0.send([part_x])
    [px_1] = after([px_1], part_x, *sent, *out_got)
    hid_1 = through_in(1, px_1)
    [got_o, got_z] = after([got_o, got_z], part_x)
    sent_oz, got_oz = exchange(split(jnp.concatenate([got_o, got_z], axis=1)), rank)
    [hid_1] = after([hid_1], *got_oz, *hid_got)
    stages_1 = scatter_stages(hid_1)
    hid_got, hid_sent = next(stages_1)
    output = (tok + finish(out_stages, [part_x]).astype(F32)).astype(BF)

    d_conv = (conv_0 + conv_1).reshape(CONV + 1, 8, -1).sum(axis=1)
    d_skip = jnp.sum((skip_0 + skip_1).reshape(8, hl, HEADDIM), axis=(0, 2))
    d_vec = vec_0 + vec_1
    head_rows = jnp.concatenate([d_vec[0, :hl], d_skip, d_vec[1, :hl]])
    small = jnp.concatenate([d_conv.reshape(-1), d_gain_out, head_rows])
    small_size = small.shape[0]
    small = jnp.pad(small, (0, -small_size % 1024)).reshape(-1, LANES)
    [small] = after([small], *hid_sent)
    for bit in axis_bits("dp"):
        small = small + swapped(small, "dp", bit)
    small = jnp.stack(turned([small] + [swapped(small, "seq", mask) for mask in range(1, n)], rank)).reshape(n, -1)[:, :small_size]
    conv_all = small[:, : (CONV + 1) * (xw + bc)].reshape(n, CONV + 1, xw + bc)
    conv_tot = jnp.concatenate(
        [conv_all[:, :, :xw].transpose(1, 0, 2).reshape(CONV + 1, INNER), jnp.sum(conv_all[:, :, xw:], axis=0)], axis=1
    )
    gain_out_tot = small[:, (CONV + 1) * (xw + bc) : small_size - 3 * hl].reshape(-1)
    heads_tot = small[:, small_size - 3 * hl :].reshape(n, 3, hl).transpose(1, 0, 2).reshape(-1)

    [got_x] = after([got_x], conv_tot, *hid_got)
    sent_x, got_x = exchange(split(got_x), rank)
    d_hidden = jnp.concatenate([finish(stages_0, [hid_1]), finish(stages_1)], axis=0).astype(F32)
    got_oz, got_x = (turned(sent[:1] + got, rank) for sent, got in ((sent_oz, got_oz), (sent_x, got_x)))

    together = lambda parts, lo, hi: jnp.concatenate([one[:, lo:hi] for one in parts], axis=1).astype(F32)
    g_bc = sum(one[:, xw : xw + bc].astype(F32) for one in got_x)
    shard_in = jnp.concatenate(
        [together(got_oz, xw, 2 * xw), together(got_x, 0, xw), g_bc, together(got_x, xw + bc, xw + bc + hl)], axis=1
    )
    shard_out = together(got_oz, 0, xw).T

    dh = d_hidden * gain_in
    d_tok = r_in * (dh - tok * (r_in * r_in) * jnp.mean(dh * tok, axis=-1, keepdims=True))
    input_grad = (cotangent.astype(F32) + d_tok).astype(BF)

    own = lax.axis_index("dp") * n + rank
    own_gain = lax.dynamic_slice_in_dim(gain_in, own * rows, rows)
    d_gain_in = jnp.sum(in_low.astype(F32) * shard_in, axis=1) / own_gain
    partial_sq = jnp.sum(shard_in * shard_in) + jnp.sum(shard_out * shard_out)
    last = lax.dynamic_update_slice(jnp.zeros((D + 1024,), F32), d_gain_in, (own * rows,))
    last = lax.dynamic_update_slice(last, partial_sq[None], (D,))
    last = sum_all(last.reshape(-1, LANES)).reshape(-1)
    vec_tot = jnp.concatenate([heads_tot, last[:D], gain_out_tot])
    shard_conv = lax.dynamic_slice_in_dim(conv_tot, own * cw, cw, 1)
    grad_norm = jnp.sqrt(last[D] + jnp.sum(conv_tot * conv_tot) + jnp.sum(vec_tot * vec_tot))
    clip = jnp.minimum(1.0, CLIP_NORM / (grad_norm + 1e-06))
    in_new = adamw(in_weight, shard_in, in_m, in_v, clip, WEIGHT_DECAY)
    conv_new = adamw(conv_weight, shard_conv, conv_m, conv_v, clip, WEIGHT_DECAY)
    out_new = adamw(out_weight, shard_out, out_m, out_v, clip, WEIGHT_DECAY)
    vec_new = adamw(packed, vec_tot, packed_m, packed_v, clip, 0.0)
    return (
        output, input_grad, grad_norm,
        in_weight + in_new[0], in_new[1], in_new[2],
        conv_new[0], conv_new[1], conv_new[2],
        out_weight + out_new[0], out_new[1], out_new[2],
        vec_new[0], vec_new[1], vec_new[2],
    )


def solution(mesh):
    tok, col, row = P(None, ALL, None), P(None, ALL), P(ALL, None)
    return jax.shard_map(
        per_device,
        mesh=mesh,
        in_specs=(tok, tok, P(None, "dp"), row, row, row, col, col, col, col, col, col, P(), P(), P()),
        out_specs=(tok, tok, P(), row, row, row, col, col, col, col, col, col, P(), P(), P()),
        check_vma=False,
    )
```

```python
import functools

import jax
import jax.numpy as jnp
from jax import lax
from jax.experimental import pallas as pl
from jax.experimental.pallas import tpu as pltpu
from jax.sharding import PartitionSpec as P

D = 2048
HEADS = 64
HEADDIM = 64
STATE = 128
CONV = 4
BLOCK = 256
MICRO = 2
INNER = 4096
CH = 4352
NORM_EPS = 1e-05
LEARN_RATE = 0.004
BETA_ONE = 0.9
BETA_TWO = 0.95
FIX_ONE = 1.0 - 0.9**10
FIX_TWO = 1.0 - 0.95**10
ADAM_EPS = 1e-08
WEIGHT_DECAY = 0.1
CLIP_NORM = 1.0
BF = jnp.bfloat16
F32 = jnp.float32
ALL = ("dp", "seq")


def dot(a, b, dims, out=F32):
    return lax.dot_general(a, b, (dims, ((), ())), preferred_element_type=out)


NN = ((1,), (0,))
NT = ((1,), (1,))
TN = ((0,), (0,))
LANES = 128
PAIR = 2 * HEADDIM
VMEM = 56 * 1024 * 1024
SLOT = 16
TINY = 1e-37
CAP = 85.0


def iota2(shape, dim):
    return lax.broadcasted_iota(jnp.int32, shape, dim)


def tree(value, rows=8):
    while value.shape[0] > rows:
        half = value.shape[0] // 2
        value = value[:half] + value[half:]
    return value


def thirds(value):
    high = value.astype(BF).astype(F32)
    rest = value - high
    mid = rest.astype(BF).astype(F32)
    return high, mid, (rest - mid).astype(BF).astype(F32)


def running_sum(values, reverse):
    row, col = iota2((BLOCK, BLOCK), 0), iota2((BLOCK, BLOCK), 1)
    ones = jnp.where(row >= col if reverse else row <= col, 1.0, 0.0).astype(BF)
    sums = dot(jnp.concatenate(thirds(values), axis=0).astype(BF), ones, NN)
    return sums[:SLOT] + sums[SLOT : 2 * SLOT] + sums[2 * SLOT :]


def step_rows(raw, heads, masks):
    lifted = raw.astype(F32).T[:SLOT] + heads[:, 0:1]
    dt = jnp.maximum(lifted, 0.0) + jnp.log1p(jnp.exp(-jnp.abs(lifted)))
    cum = running_sum(dt * heads[:, 1:2], False)
    entry = jnp.exp(cum) * masks[1:2, :]
    dt_end = dt * jnp.exp(cum[:, BLOCK - 1 : BLOCK] - cum) * masks[2:3, :]
    return lifted, dt, cum, entry, dt_end


def two(value):
    high = value.astype(BF).astype(F32)
    return [high, value - high]


def as_columns(gap_rows, entry, dt_end):
    ones = jnp.where(iota2((SLOT, BLOCK), 0) < 3, 1.0, 0.0)
    return jnp.concatenate([*thirds(gap_rows), ones, *two(entry), *two(dt_end)], axis=0).T.astype(BF)


def gap_right_init(right, hl):
    row = iota2((3 * SLOT, BLOCK), 0)
    for h in range(hl):
        right[0 : 3 * SLOT, h * BLOCK : (h + 1) * BLOCK] = jnp.where((row & (SLOT - 1)) == h, 1.0, 0.0).astype(BF)


def gap_right_fill(right, values, hl):
    row = iota2((SLOT, BLOCK), 0)
    high, mid, low = thirds(values)
    for h in range(hl):
        one = slice(h, h + 1)
        slab = jnp.where(row == 0, high[one], jnp.where(row == 1, mid[one], jnp.where(row == 2, low[one], 0.0)))
        right[3 * SLOT :, h * BLOCK : (h + 1) * BLOCK] = slab.astype(BF)


def head_spread_init(spreads, hl):
    row, col = iota2(spreads.shape, 0), iota2(spreads.shape, 1)
    head = jnp.where(col < hl * HEADDIM, col, col - hl * HEADDIM) // HEADDIM
    slot = jnp.where(col < hl * HEADDIM, 2, 3)
    spreads[...] = jnp.where(((row & (SLOT - 1)) == head) & (row // (2 * SLOT) == slot), 1.0, 0.0).astype(BF)


def stacked(left, pair_values):
    zero = jnp.zeros_like(pair_values)
    return jnp.concatenate([jnp.where(left, pair_values, zero), jnp.where(left, zero, pair_values)], axis=0)


def conv_chunk(window, conv_w, valid, lo, hi):
    out = conv_w[CONV : CONV + 1, lo:hi] + conv_w[CONV - 1 : CONV, lo:hi] * window[8 : 8 + BLOCK, lo:hi]
    for tap in range(CONV - 1):
        out += conv_w[tap : tap + 1, lo:hi] * (window[5 + tap : 5 + tap + BLOCK, lo:hi] * valid[tap])
    return out


def spread(aux_v, at):
    return jnp.broadcast_to(aux_v[:, at : at + 1], (BLOCK, LANES))


def forward_kernel(place, proj, conv_w, skip, heads, aux, masks, y_out, s_out, act, slope, window, state, right, carried, spreads, *, hl):
    width = hl * HEADDIM
    conv_width = width + 2 * STATE

    @pl.when(pl.program_id(1) == 0)
    def _():
        window[0:8, :] = jnp.zeros((8, conv_width), F32)
        state[...] = jnp.zeros(state.shape, F32)
        gap_right_init(right, hl)
        head_spread_init(spreads, hl)

    aux_v = aux[...]
    valid = [spread(aux_v, tap) for tap in range(CONV - 1)]
    for lo in range(0, conv_width, LANES):
        hi = lo + LANES
        window[8 : 8 + BLOCK, lo:hi] = proj[:, lo:hi].astype(F32)
        out = conv_chunk(window, conv_w, valid, lo, hi)
        sig = jax.nn.sigmoid(out)
        silu = out * sig
        act[:, lo:hi] = silu.astype(BF)
        slope[:, lo:hi] = (sig + silu * (1.0 - sig)).astype(BF)
    window[0:8, :] = window[BLOCK : BLOCK + 8, :]

    _, dt, cum, entry, dt_end = step_rows(proj[:, conv_width : conv_width + LANES], heads[...], masks)
    columns = as_columns(cum, entry, dt_end)
    gaps = columns[:, : 4 * SLOT]
    gap_right_fill(right, jnp.log(jnp.maximum(dt, TINY)) - cum, hl)
    bm, cm = act[:, width : width + STATE], act[:, width + STATE :]
    same = (aux_v[:, 3:4] == masks[0:1, :]) & (iota2((BLOCK, BLOCK), 0) >= iota2((BLOCK, BLOCK), 1))
    inner = jnp.where(same, dot(cm, bm, NT), 0.0)
    left = iota2((BLOCK, PAIR), 1) < HEADDIM
    top = iota2((PAIR, STATE), 0) < HEADDIM
    last = entry[:, BLOCK - 1 : BLOCK]
    s_out[0] = state[...].astype(BF)
    carried[...] = dot(columns, spreads[...], NN)
    carried[:, :width] = carried[:, :width] * dot(cm, s_out[0], NT)
    for pair in range(hl // 2):
        first = 2 * pair
        lo, hi = pair * PAIR, (pair + 1) * PAIR
        xp = act[:, lo:hi]
        mix = []
        for h in (first, first + 1):
            decay = jnp.exp(jnp.minimum(dot(gaps, right[:, h * BLOCK : (h + 1) * BLOCK], NN), CAP))
            mix.append((inner * decay).astype(BF))
        xf = xp.astype(F32)
        y = dot(jnp.concatenate(mix, axis=1), stacked(left, xp), NN)
        y += carried[:, lo:hi] + skip[0:1, lo:hi] * xf
        y_out[:, lo:hi] = y.astype(BF)
        weighted = (xf * carried[:, width + lo : width + hi]).astype(BF)
        keep = jnp.where(top, last[first : first + 1], last[first + 1 : first + 2])
        state[lo:hi, :] = keep * state[lo:hi, :] + dot(weighted, bm, TN)


def backward_kernel(place, proj, conv_w, skip, heads, aux, masks, act, slope, dy, s_in, *refs, hl):
    dproj, dconv, dvec, dskip, dwin, grad_s, dcb, colsum, dkeep, right, carried, later_w, spreads, picks, sums, used, into = refs[-17:]
    width = hl * HEADDIM
    conv_width = width + 2 * STATE

    @pl.when(pl.program_id(0) == 0)
    def _():
        dconv[...] = jnp.zeros(dconv.shape, F32)
        dvec[...] = jnp.zeros(dvec.shape, F32)
        dskip[...] = jnp.zeros(dskip.shape, F32)
        dwin[BLOCK : BLOCK + 8, :] = jnp.zeros((8, conv_width), F32)
        grad_s[...] = jnp.zeros(grad_s.shape, F32)
        colsum[...] = jnp.zeros(colsum.shape, F32)
        dkeep[...] = jnp.zeros(dkeep.shape, F32)
        gap_right_init(right, hl)
        head_spread_init(spreads, hl)
        picks[...] = jnp.where(iota2(picks.shape, 0) == iota2(picks.shape, 1) // BLOCK, 1.0, 0.0).astype(BF)
        sums[...] = jnp.where(iota2(sums.shape, 0) == iota2(sums.shape, 1) // HEADDIM, 1.0, 0.0).astype(BF)

    aux_v = aux[...]
    lifted, dt, cum, entry, dt_end = step_rows(proj[:, conv_width : conv_width + LANES], heads[...], masks)
    a_neg = heads[:, 1:2]
    columns = as_columns(jnp.log(jnp.maximum(dt, TINY)) - cum, entry, dt_end)
    gaps = columns[:, : 4 * SLOT]
    gap_right_fill(right, cum, hl)
    bm, cm = act[:, width : width + STATE], act[:, width + STATE :]
    same = (aux_v[:, 3:4] == masks[0:1, :]) & (iota2((BLOCK, BLOCK), 0) <= iota2((BLOCK, BLOCK), 1))
    inner = jnp.where(same, dot(bm, cm, NT), 0.0)
    left = iota2((BLOCK, PAIR), 1) < HEADDIM
    top = iota2((PAIR, STATE), 0) < HEADDIM
    last = entry[:, BLOCK - 1 : BLOCK]
    d_row = jnp.zeros((SLOT, BLOCK), F32)
    d_b = jnp.zeros((BLOCK, STATE), F32)
    d_c = jnp.zeros((BLOCK, STATE), F32)
    spreaded = dot(columns, spreads[...], NN)
    carried[...] = spreaded
    later_w[:, :width] = dot(cm, s_in[0], NT)
    later_w[:, width:] = dot(bm, grad_s[...].astype(BF), NT)

    for pair in range(hl // 2):
        first = 2 * pair
        lo, hi = pair * PAIR, (pair + 1) * PAIR
        xp, dyp = act[:, lo:hi], dy[:, lo:hi]
        xf, dyf = xp.astype(F32), dyp.astype(F32)
        d_mix = dot(stacked(left, xp), dyp, NT)
        mix, pairwise = [], []
        d_inner = 0.0
        for at, h in enumerate((first, first + 1)):
            decay = jnp.exp(jnp.minimum(dot(gaps, right[:, h * BLOCK : (h + 1) * BLOCK], NN), CAP))
            mix.append((inner * decay).astype(BF))
            part = d_mix[at * BLOCK : (at + 1) * BLOCK] * decay
            d_inner += part
            part = (part * inner).astype(BF)
            pairwise.append(part)
            colsum[h : h + 1, :] = jnp.sum(tree(part.astype(F32)), axis=0, keepdims=True)
        d_row += dot(picks[:, first * BLOCK : (first + 2) * BLOCK], jnp.concatenate(pairwise, axis=1), NT)
        if pair == 0:
            dcb[...] = d_inner
        else:
            dcb[...] += d_inner
        later = grad_s[lo:hi, :]
        low = s_in[0, lo:hi, :]
        end_p = carried[:, width + lo : width + hi]
        from_end = later_w[:, width + lo : width + hi] * end_p
        dx = dot(jnp.concatenate(mix, axis=1), stacked(left, dyp), NN) + from_end + skip[0:1, lo:hi] * dyf
        dwin[0:BLOCK, lo:hi] = slope[:, lo:hi].astype(F32) * dx
        used[:, lo:hi] = (from_end * xf).astype(BF)
        entering = carried[:, lo:hi] * dyf
        into[:, lo:hi] = (entering * later_w[:, lo:hi]).astype(BF)
        entering = entering.astype(BF)
        dskip[:, lo:hi] += tree(xf * dyf)
        kept = later * low.astype(F32)
        dkeep[first : first + 1, :] = jnp.sum(tree(kept[:HEADDIM]), axis=0, keepdims=True)
        dkeep[first + 1 : first + 2, :] = jnp.sum(tree(kept[HEADDIM:]), axis=0, keepdims=True)
        weighted = (xf * end_p).astype(BF)
        d_b += dot(weighted, later.astype(BF), NN)
        d_c += dot(entering, low, NN)
        keep = jnp.where(top, last[first : first + 1], last[first + 1 : first + 2])
        grad_s[lo:hi, :] = dot(entering, cm, TN) + keep * later

    d_inner = jnp.where(same, dcb[...], 0.0).astype(BF)
    d_b += dot(d_inner, cm, NN)
    d_c += dot(d_inner, bm, TN)
    dwin[0:BLOCK, width : width + STATE] = slope[:, width : width + STATE].astype(F32) * d_b
    dwin[0:BLOCK, width + STATE :] = slope[:, width + STATE :].astype(F32) * d_c

    d_end = dot(sums[...], used[...], NT)
    through = d_row + d_end
    d_last = jnp.sum(d_end, axis=1, keepdims=True) + jnp.sum(dkeep[...], axis=1, keepdims=True) * last
    d_cum = dot(sums[...], into[...], NT) + colsum[...] - through
    d_cum += jnp.where(iota2((SLOT, BLOCK), 1) == BLOCK - 1, d_last, 0.0)
    d_a = running_sum(d_cum, True)
    sig = jax.nn.sigmoid(lifted)
    d_raw = through * jnp.where(dt > TINY, sig / jnp.maximum(dt, TINY), 1.0) + d_a * a_neg * sig
    d_raw = jnp.where(iota2((SLOT, BLOCK), 0) < hl, d_raw, 0.0)
    dproj[:, conv_width : conv_width + LANES] = jnp.concatenate([d_raw, jnp.zeros((LANES - SLOT, BLOCK), F32)], axis=0).T.astype(BF)
    lane = iota2((SLOT, LANES), 1)
    d_log = jnp.sum(d_a * dt, axis=1, keepdims=True) * a_neg
    dvec[...] += jnp.where(lane == 0, d_log, jnp.where(lane == 1, jnp.sum(d_raw, axis=1, keepdims=True), 0.0))

    valid = [spread(aux_v, 4 + tap) for tap in range(CONV - 1)]
    for lo in range(0, conv_width, LANES):
        hi = lo + LANES
        own = dwin[0:BLOCK, lo:hi]
        value = proj[:, lo:hi].astype(F32)
        grad = conv_w[CONV - 1 : CONV, lo:hi] * own
        dconv[CONV * 8 : CONV * 8 + 8, lo:hi] += tree(own)
        dconv[(CONV - 1) * 8 : CONV * 8, lo:hi] += tree(own * value)
        for tap in range(CONV - 1):
            ahead = CONV - 1 - tap
            moved = dwin[ahead : ahead + BLOCK, lo:hi] * valid[tap]
            grad += conv_w[tap : tap + 1, lo:hi] * moved
            dconv[tap * 8 : tap * 8 + 8, lo:hi] += tree(moved * value)
        dproj[:, lo:hi] = grad.astype(BF)
    dwin[BLOCK : BLOCK + 8, :] = dwin[0:8, :]


def segment_aux(segments):
    micro, length = segments.shape
    nb = length // BLOCK
    seg = segments.astype(F32)
    blocks = seg.reshape(micro, nb, BLOCK)
    prev = jnp.concatenate([jnp.full((micro, 1), -1.0, F32), blocks[:, :-1, -1]], axis=1)
    reach = range(CONV - 1, 0, -1)
    earlier = [jnp.pad(seg, ((0, 0), (by, 0)), constant_values=-1.0)[:, :length] == seg for by in reach]
    later = [jnp.pad(seg, ((0, 0), (0, by)), constant_values=-1.0)[:, by:] == seg for by in reach]
    columns = [c.astype(F32) for c in (*earlier, seg, *later, jnp.zeros_like(seg))]
    aux = jnp.stack(columns, axis=-1).reshape(micro * length, 8)
    zero = jnp.zeros_like(blocks)
    masks = [blocks, blocks == prev[:, :, None], blocks == blocks[:, :, -1:]] + [zero] * 5
    return aux, jnp.stack([m.astype(F32) for m in masks], axis=2).reshape(micro * nb * 8, BLOCK)


def head_columns(a_log, dt_bias):
    hl = a_log.shape[0]
    both = jnp.stack([dt_bias, -jnp.exp(a_log)], axis=1)
    return jnp.pad(both, ((0, SLOT - hl), (0, LANES - 2)))


def scan_forward(place, proj, conv_w, skip, heads, aux, masks, hl):
    tokens = proj.shape[0]
    nb = tokens // MICRO // BLOCK
    width = hl * HEADDIM
    conv_width = width + 2 * STATE
    held = lambda m, j, place: (m * nb + (j ^ place[0]), 0)
    at = lambda m, j, place: (m * nb + j, 0)
    whole = lambda m, j, place: (0, 0)
    grid_spec = pltpu.PrefetchScalarGridSpec(
        num_scalar_prefetch=1,
        grid=(MICRO, nb),
        in_specs=[
            pl.BlockSpec((BLOCK, conv_width + LANES), held),
            pl.BlockSpec((8, conv_width), whole),
            pl.BlockSpec(skip.shape, whole),
            pl.BlockSpec(heads.shape, whole),
            pl.BlockSpec((BLOCK, 8), at),
            pl.BlockSpec((8, BLOCK), at),
        ],
        out_specs=[
            pl.BlockSpec((BLOCK, width), held),
            pl.BlockSpec((1, width, STATE), lambda m, j, place: (m * nb + j, 0, 0)),
            pl.BlockSpec((BLOCK, conv_width), held),
            pl.BlockSpec((BLOCK, conv_width), held),
        ],
        scratch_shapes=[
            pltpu.VMEM((BLOCK + 8, conv_width), F32),
            pltpu.VMEM((width, STATE), F32),
            pltpu.VMEM((4 * SLOT, hl * BLOCK), BF),
            pltpu.VMEM((BLOCK, 2 * width), F32),
            pltpu.VMEM((LANES, 2 * width), BF),
        ],
    )
    return pl.pallas_call(
        functools.partial(forward_kernel, hl=hl),
        grid_spec=grid_spec,
        out_shape=[
            jax.ShapeDtypeStruct((tokens, width), BF),
            jax.ShapeDtypeStruct((MICRO * nb, width, STATE), BF),
            jax.ShapeDtypeStruct((tokens, conv_width), BF),
            jax.ShapeDtypeStruct((tokens, conv_width), BF),
        ],
        compiler_params=pltpu.CompilerParams(vmem_limit_bytes=VMEM, dimension_semantics=("arbitrary", "arbitrary")),
        name="scan_forward",
    )(place, proj, conv_w, skip, heads, aux, masks)


def scan_backward(place, micro, proj, conv_w, skip, heads, aux, masks, act, slope, dy, states, hl, *done):
    tokens = proj.shape[0] // MICRO
    nb = tokens // BLOCK
    width = hl * HEADDIM
    conv_width = width + 2 * STATE
    full = conv_width + LANES
    first = micro * nb
    held = lambda j, place: (first + ((nb - 1 - j) ^ place[0]), 0)
    at = lambda j, place: (first + nb - 1 - j, 0)
    whole = lambda j, place: (0, 0)
    grid_spec = pltpu.PrefetchScalarGridSpec(
        num_scalar_prefetch=1,
        grid=(nb,),
        in_specs=[
            pl.BlockSpec((BLOCK, full), held),
            pl.BlockSpec((8, conv_width), whole),
            pl.BlockSpec(skip.shape, whole),
            pl.BlockSpec(heads.shape, whole),
            pl.BlockSpec((BLOCK, 8), at),
            pl.BlockSpec((8, BLOCK), at),
            pl.BlockSpec((BLOCK, conv_width), held),
            pl.BlockSpec((BLOCK, conv_width), held),
            pl.BlockSpec((BLOCK, width), held),
            pl.BlockSpec((1, width, STATE), lambda j, place: (first + nb - 1 - j, 0, 0)),
        ]
        + [pl.BlockSpec(memory_space=pl.ANY)] * len(done),
        out_specs=[
            pl.BlockSpec((BLOCK, full), lambda j, place: ((nb - 1 - j) ^ place[0], 0)),
            pl.BlockSpec((8 * (CONV + 1), conv_width), whole),
            pl.BlockSpec((SLOT, LANES), whole),
            pl.BlockSpec((8, width), whole),
        ],
        scratch_shapes=[
            pltpu.VMEM((BLOCK + 8, conv_width), F32),
            pltpu.VMEM((width, STATE), F32),
            pltpu.VMEM((BLOCK, BLOCK), F32),
            pltpu.VMEM((SLOT, BLOCK), F32),
            pltpu.VMEM((SLOT, STATE), F32),
            pltpu.VMEM((4 * SLOT, hl * BLOCK), BF),
            pltpu.VMEM((BLOCK, 2 * width), F32),
            pltpu.VMEM((BLOCK, 2 * width), F32),
            pltpu.VMEM((LANES, 2 * width), BF),
            pltpu.VMEM((SLOT, hl * BLOCK), BF),
            pltpu.VMEM((SLOT, width), BF),
            pltpu.VMEM((BLOCK, width), BF),
            pltpu.VMEM((BLOCK, width), BF),
        ],
    )
    return pl.pallas_call(
        functools.partial(backward_kernel, hl=hl),
        grid_spec=grid_spec,
        out_shape=[
            jax.ShapeDtypeStruct((tokens, full), BF),
            jax.ShapeDtypeStruct((8 * (CONV + 1), conv_width), F32),
            jax.ShapeDtypeStruct((SLOT, LANES), F32),
            jax.ShapeDtypeStruct((8, width), F32),
        ],
        compiler_params=pltpu.CompilerParams(vmem_limit_bytes=VMEM, dimension_semantics=("arbitrary",)),
        name="scan_backward",
    )(place, proj, conv_w, skip, heads, aux, masks, act, slope, dy, states, *done)


def fetch(pieces, buffer, sems, step):
    @pl.when(step == 0)
    def _():
        pltpu.make_async_copy(pieces[0], buffer.at[0], sems.at[0]).start()

    for at in range(1, len(pieces)):

        @pl.when(step == at - 1)
        def _():
            pltpu.make_async_copy(pieces[at], buffer.at[at % 2], sems.at[at % 2]).start()

    slot = step % 2
    pltpu.make_async_copy(pieces[0], buffer.at[slot], sems.at[slot]).wait()
    return slot


def emit(value, targets, buffer, sems, micro, place, bits, step, steps):
    slot = step % 2
    rows = value.shape[0] // 2

    def waiting(at):
        for half in range(2):
            pltpu.make_async_copy(buffer.at[at, pl.ds(half * rows, rows)], targets[0].at[0, 0], sems.at[at, half]).wait()

    @pl.when(step >= 2)
    def _():
        waiting(slot)

    buffer[slot] = value
    for half, bit in enumerate(bits):
        index = place // (2 * bit) * bit + place % bit
        set_ = (place // bit) % 2
        for target, wanted in ((targets[2 * half], 1), (targets[2 * half + 1], 0)):

            @pl.when(set_ == wanted)
            def _():
                pltpu.make_async_copy(
                    buffer.at[slot, pl.ds(half * rows, rows)], target.at[micro, index], sems.at[slot, half]
                ).start()

    @pl.when(step == steps - 1)
    def _():
        waiting(0)
        waiting(1)


def emitted(some, n, depth):
    shapes = [jax.ShapeDtypeStruct((some, n // 2, BLOCK // 2, depth), BF)] * 4
    return shapes, [pl.BlockSpec(memory_space=pl.ANY)] * 4, [pltpu.VMEM((2, BLOCK, depth), BF), pltpu.SemaphoreType.DMA((2, 2))]


def fixed(array):
    return pl.BlockSpec(array.shape, lambda i: (0, 0), pipeline_mode=pl.Buffered(1))


def by_rows(width):
    return pl.BlockSpec((BLOCK, width), lambda i: (i, 0))


def arbitrary(name):
    return dict(compiler_params=pltpu.CompilerParams(vmem_limit_bytes=VMEM, dimension_semantics=("arbitrary",)), name=name)


def in_kernel(*refs, count):
    pieces, w, (proj, hidden, buffer, sems) = refs[1 : count + 1], refs[count + 1], refs[-4:]
    slot = fetch(pieces, buffer, sems, pl.program_id(0))
    value = buffer[slot]
    hidden[...] = value
    proj[...] = dot(value, w[...], NN).astype(BF)


def in_project(pieces, places, total, w, earlier=(), done=()):
    count = len(pieces)
    depth, width = w.shape
    anywhere = [pl.BlockSpec(memory_space=pl.ANY)]
    at = lambda i, table: (table[i], 0)
    return pl.pallas_call(
        functools.partial(in_kernel, count=count),
        grid_spec=pltpu.PrefetchScalarGridSpec(
            num_scalar_prefetch=1,
            grid=(count,),
            in_specs=anywhere * count
            + [pl.BlockSpec(w.shape, lambda i, table: (0, 0), pipeline_mode=pl.Buffered(1))]
            + anywhere * (len(earlier) + len(done)),
            out_specs=[pl.BlockSpec((BLOCK, width), at), pl.BlockSpec((BLOCK, depth), at)],
            scratch_shapes=[pltpu.VMEM((2, BLOCK, depth), BF), pltpu.SemaphoreType.DMA((2,))],
        ),
        out_shape=[
            jax.ShapeDtypeStruct((total * BLOCK, width), BF),
            jax.ShapeDtypeStruct((total * BLOCK, depth), BF),
        ],
        input_output_aliases={count + 2 + i: i for i in range(len(earlier))},
        **arbitrary("in_project"),
    )(jnp.array(places, jnp.int32), *pieces, w, *earlier, *done)


def gate_kernel(*refs, count):
    pieces, (z, w_o, y, gain, dn_out, cot_out, sums, buffer, sems) = refs[:count], refs[count:]
    slot = fetch(pieces, buffer, sems, pl.program_id(0))
    cot = buffer[slot]
    cot_out[...] = cot
    dn = dot(cot, w_o[...], NN)
    dn_out[...] = dn.astype(BF)
    zf = z[...].astype(F32)
    gz = y[...].astype(F32) * (zf * jax.nn.sigmoid(zf))
    ones = jnp.ones((8, gz.shape[1]), BF)
    first = dot(ones, (gz * gz).astype(BF), NT)
    second = dot(ones, (dn * gain[0:1, :] * gz).astype(BF), NT)
    sums[...] = jnp.where(iota2((8, BLOCK), 0) == 0, first, second)


def gate_forward(pieces, z, w_o, y, gain):
    count = len(pieces)
    depth, width = w_o.shape
    return pl.pallas_call(
        functools.partial(gate_kernel, count=count),
        grid=(count,),
        in_specs=[pl.BlockSpec(memory_space=pl.ANY)] * count + [by_rows(width), fixed(w_o), by_rows(width), fixed(gain)],
        out_specs=[by_rows(width), by_rows(depth), pl.BlockSpec((8, BLOCK), lambda i: (i, 0))],
        out_shape=[
            jax.ShapeDtypeStruct((count * BLOCK, width), BF),
            jax.ShapeDtypeStruct((count * BLOCK, depth), BF),
            jax.ShapeDtypeStruct((count * 8, BLOCK), F32),
        ],
        scratch_shapes=[pltpu.VMEM((2, BLOCK, depth), BF), pltpu.SemaphoreType.DMA((2,))],
        **arbitrary("gate_forward"),
    )(*pieces, z, w_o, y, gain)


def out_kernel(z_in, dn_in, y_in, sums, gain, w_o, normed, dy, dz, dgain, *refs, n, bits):
    step = pl.program_id(0)
    @pl.when(pl.program_id(0) == 0)
    def _():
        dgain[...] = jnp.zeros(dgain.shape, F32)

    scale = lax.rsqrt(sums[0:1, :] / INNER + NORM_EPS)
    slope = scale * scale * scale * sums[1:2, :] / INNER
    row = iota2((LANES, BLOCK), 0)
    columns = jnp.where(row == 0, scale, jnp.where(row == 1, slope, 0.0)).T
    scale, slope = columns[:, 0:1], columns[:, 1:2]
    for lo in range(0, normed.shape[1], 2 * LANES):
        hi = lo + 2 * LANES
        z, y, dn = z_in[:, lo:hi].astype(F32), y_in[:, lo:hi].astype(F32), dn_in[:, lo:hi].astype(F32)
        sig = jax.nn.sigmoid(z)
        silu = z * sig
        gz = y * silu
        unit = gz * scale
        normed[:, lo:hi] = (unit * gain[0:1, lo:hi]).astype(BF)
        dgain[:, lo:hi] += jnp.sum((dn * unit).reshape(BLOCK // 8, 8, 2 * LANES), axis=0)
        d_gz = dn * gain[0:1, lo:hi] * scale - gz * slope
        dy[:, lo:hi] = (d_gz * silu).astype(BF)
        dz[:, lo:hi] = (d_gz * y * (sig + silu * (1.0 - sig))).astype(BF)
    out = dot(normed[...], w_o[...], NT).astype(BF)
    emit(out, refs[:4], refs[4], refs[5], step // n, step % n, bits, step, MICRO * n)


def out_project(z, dn, y, sums, gain, w_o, bits):
    depth, width = w_o.shape
    tokens = z.shape[0]
    n = tokens // BLOCK // MICRO
    one = by_rows(width)
    shapes, places, scratch = emitted(MICRO, n, depth)
    return pl.pallas_call(
        functools.partial(out_kernel, n=n, bits=bits),
        grid=(tokens // BLOCK,),
        in_specs=[one, one, one, pl.BlockSpec((8, BLOCK), lambda i: (i, 0)), fixed(gain), fixed(w_o)],
        out_specs=[one, one, one, pl.BlockSpec((8, width), lambda i: (0, 0))] + places,
        out_shape=[jax.ShapeDtypeStruct((tokens, width), BF)] * 3 + [jax.ShapeDtypeStruct((8, width), F32)] + shapes,
        scratch_shapes=scratch,
        **arbitrary("out_project"),
    )(z, dn, y, sums, gain, w_o)


def back_kernel(dz, px, w_z, w_x, *refs, n, bits):
    step = pl.program_id(0)
    out = (dot(dz[...], w_z[...], NT) + dot(px[...], w_x[...], NT)).astype(BF)
    emit(out, refs[:4], refs[4], refs[5], 0, step, bits, step, n)


def back_project(micro, dz, px, w_z, w_x, bits):
    tokens, width = px.shape
    depth = w_z.shape[0]
    n = tokens // BLOCK
    shapes, places, scratch = emitted(1, n, depth)
    return pl.pallas_call(
        functools.partial(back_kernel, n=n, bits=bits),
        grid=(n,),
        in_specs=[pl.BlockSpec((BLOCK, dz.shape[1]), lambda i: (micro * n + i, 0)), by_rows(width), fixed(w_z), fixed(w_x)],
        out_specs=places,
        out_shape=shapes,
        scratch_shapes=scratch,
        **arbitrary("back_project"),
    )(dz, px, w_z, w_x)

def swapped(value, axis, mask):
    return lax.ppermute(value, axis, [(i, i ^ mask) for i in range(lax.axis_size(axis))])


def axis_bits(axis):
    return [1 << i for i in range(lax.axis_size(axis).bit_length() - 1)]


def micro_order(micro, axis):
    bits = axis_bits(axis)
    return bits if micro % 2 == 0 else bits[::-1]


def nothing(*refs):
    pass


def after(values, *done):
    values = list(values)
    anywhere = pl.BlockSpec(memory_space=pl.ANY)
    held = pl.pallas_call(
        nothing,
        in_specs=[anywhere] * (len(values) + len(done)),
        out_specs=[anywhere] * len(values),
        out_shape=[jax.ShapeDtypeStruct(v.shape, v.dtype) for v in values],
        input_output_aliases={at: at for at in range(len(values))},
        name="after",
    )(*values, *done)
    return list(held)


def gather_stages(own):
    held = [{0: own[micro]} for micro in range(MICRO)]
    for turn in range(len(axis_bits("seq"))):
        got = []
        for micro in range(MICRO):
            bit = micro_order(micro, "seq")[turn]
            got.append({at ^ bit: swapped(held[micro][at], "seq", bit) for at in held[micro]})
        wait = yield [piece for one in got for piece in one.values()], [piece for one in held for piece in one.values()]
        for micro in range(MICRO):
            if wait is not None:
                got[micro] = dict(zip(got[micro], after(got[micro].values(), *wait)))
            held[micro].update(got[micro])
    yield [held[micro][at] for micro in range(MICRO) for at in range(len(held[micro]))]


def scatter_stages(parts):
    n = 2 * parts[0].shape[1]
    away, stay = list(parts[0::2]), list(parts[1::2])
    places = [[at for at in range(n) if not at & micro_order(half, "seq")[0]] for half in range(2)]
    join = lambda one, more: (one.astype(F32) + more.astype(F32)).astype(BF)
    pick = lambda a, at: jnp.concatenate([a[:, k : k + 1] for k in at], axis=1)
    turns = len(axis_bits("seq"))
    for turn in range(turns):
        got = [swapped(away[half], "seq", micro_order(half, "seq")[turn]) for half in range(2)]
        wait = yield got, away
        if wait is not None:
            got = after(got, *wait)
        if turn == turns - 1:
            break
        held, away, stay = stay, [], []
        for half in range(2):
            bit = micro_order(half, "seq")[turn + 1]
            leave = [at for at, place in enumerate(places[half]) if place & bit]
            keep = [at for at, place in enumerate(places[half]) if not place & bit]
            away.append(join(pick(held[half], leave), pick(got[half], leave)))
            stay.append(join(pick(held[half], keep), pick(got[half], keep)))
            places[half] = [places[half][at] for at in keep]
    yield jnp.concatenate([join(one, more)[:, 0] for one, more in zip(stay, got)], axis=1), None


def finish(stages, wait=None):
    last = None
    try:
        while True:
            last = stages.send(wait)
    except StopIteration:
        return last[0]


def turned(entries, rank):
    entries = list(entries)
    for bit in axis_bits("seq"):
        flip = (rank & bit) != 0
        entries = [jnp.where(flip, entries[at ^ bit], entries[at]) for at in range(len(entries))]
    return entries


def exchange(entries, rank):
    entries = turned(entries, rank)
    return entries, [swapped(one, "seq", mask) for mask, one in enumerate(entries) if mask]


def sum_all(value):
    for axis in ("dp", "seq"):
        for bit in axis_bits(axis):
            value = value + swapped(value, axis, bit)
    return value


def sum_pieces(value):
    n = value.shape[-2]
    total = value
    for mask in range(1, n):
        got = swapped(value, "seq", mask)
        total = total + jnp.concatenate([got[..., at ^ mask : (at ^ mask) + 1, :] for at in range(n)], axis=-2)
    return total


def adamw(master, gradient, first, second, clip, decay):
    clipped = gradient * clip
    first_new = BETA_ONE * first + (1.0 - BETA_ONE) * clipped
    second_new = BETA_TWO * second + (1.0 - BETA_TWO) * clipped * clipped
    update = first_new / FIX_ONE / (jnp.sqrt(second_new / FIX_TWO) + ADAM_EPS) + decay * master
    return (-LEARN_RATE * update, first_new, second_new)


def per_device(tokens, cotangent, segments, in_weight, in_m, in_v, conv_weight, conv_m, conv_v,
               out_weight, out_m, out_v, packed, packed_m, packed_v):
    n = lax.axis_size("seq")
    rank = lax.axis_index("seq")
    place = rank.astype(jnp.int32).reshape(1)
    ndev = n * lax.axis_size("dp")
    hl = HEADS // n
    xw = hl * HEADDIM
    rows = D // ndev
    piece = tokens.shape[1]
    count = MICRO * n * piece
    xs = INNER + INNER
    bc = 2 * STATE
    xc = xw + bc + LANES
    cw = conv_weight.shape[1]
    conv_cols = -(-(CONV + 1) * cw // rows)

    in_low = in_weight.astype(BF)
    out_low = out_weight.astype(BF).T
    conv_flat = conv_weight.astype(BF).reshape(-1)
    conv_flat = jnp.pad(conv_flat, (0, conv_cols * rows - conv_flat.shape[0])).reshape(rows, conv_cols)
    column = lambda a, q, width: a[:, q * width : (q + 1) * width]
    pad = jnp.zeros((rows, LANES - hl - conv_cols), BF)
    send_x = [
        jnp.concatenate(
            [column(in_low[:, INNER:xs], q, xw), in_low[:, xs : xs + bc], column(in_low[:, xs + bc :], q, hl), conv_flat, pad], axis=1
        )
        for q in range(n)
    ]
    gain_in = packed[3 * HEADS : 3 * HEADS + D]
    send_x = turned(send_x, rank)
    got_wx = [one if not mask else swapped(one, "seq", mask) for mask, one in enumerate(send_x)]
    a_log = lax.dynamic_slice_in_dim(packed, rank * hl, hl)
    skip = lax.dynamic_slice_in_dim(packed, HEADS + rank * hl, hl)
    dt_bias = lax.dynamic_slice_in_dim(packed, 2 * HEADS + rank * hl, hl)
    gain_out = lax.dynamic_slice_in_dim(packed, 3 * HEADS + D + rank * xw, xw)
    aux, masks = segment_aux(segments)
    heads = head_columns(a_log, dt_bias)
    skip = jnp.broadcast_to(jnp.repeat(skip, HEADDIM)[None], (8, xw))

    tok = tokens.astype(F32)
    r_in = lax.rsqrt(jnp.mean(tok * tok, axis=-1, keepdims=True) + NORM_EPS)
    hidden_stages = gather_stages((tok * r_in * gain_in).astype(BF))
    arrived, sent = next(hidden_stages)
    more, _ = hidden_stages.send(None)
    got_wx = jnp.concatenate(turned(got_wx[:1] + after(got_wx[1:], *sent), rank), axis=0)
    w_x = lax.all_gather(got_wx, "dp", axis=0, tiled=True)
    send_zo = jnp.stack(turned([jnp.concatenate([column(in_low, q, xw), column(out_low, q, xw)], axis=1) for q in range(n)], rank))
    [send_zo] = after([send_zo], got_wx, more[0], more[2])
    got_wzo = [send_zo[mask] if not mask else swapped(send_zo[mask], "seq", mask) for mask in range(n)]
    got_wzo = jnp.concatenate(turned(got_wzo, rank), axis=0)
    w_z = lax.all_gather(got_wzo[:, :xw], "dp", axis=0, tiled=True)
    w_o = lax.all_gather(got_wzo[:, xw:], "dp", axis=0, tiled=True)
    conv_full = w_x[:, xw + bc + hl : xw + bc + hl + conv_cols].reshape(ndev, rows * conv_cols)[:, : (CONV + 1) * cw]
    conv_full = conv_full.reshape(ndev, CONV + 1, cw).transpose(1, 0, 2).reshape(CONV + 1, CH)
    conv_loc = jnp.concatenate([lax.dynamic_slice_in_dim(conv_full, rank * xw, xw, 1), conv_full[:, INNER:]], axis=1).astype(F32)
    conv_loc = jnp.pad(conv_loc, ((0, 8 - CONV - 1), (0, 0)))

    for _ in axis_bits("seq")[1:]:
        arrived, more = more, hidden_stages.send(None)
        more = more[0] if isinstance(more, tuple) else more
    late = [micro * n + at for micro in range(MICRO) for at in range(n) if at & (last := micro_order(micro, "seq")[-1]) and at != last]
    soon = [at for at in range(MICRO * n) if at not in late]
    soon.sort(key=lambda at: (at % n).bit_count())
    earlier = in_project([more[at] for at in soon], soon, MICRO * n, w_x, done=(aux, masks))
    late_pieces = after([more[at] for at in late], earlier[0])
    proj_x, hidden = in_project(late_pieces, late, MICRO * n, w_x, earlier)

    cot_stages = gather_stages(after([cotangent[micro] for micro in range(MICRO)], *late_pieces))
    next(cot_stages)
    y, states, act, slope = scan_forward(place, proj_x, conv_loc, skip, heads, aux, masks, hl)
    for bit in axis_bits("seq"):
        cot = cot_stages.send([proj_x] if bit == 1 else [y])
    gain = jnp.broadcast_to(gain_out[None], (8, xw))
    [w_z] = after([w_z], y)
    z = dot(hidden, w_z, NN).astype(BF)
    dn, cot, sums = gate_forward(cot, z, w_o, y, gain)
    sums = sum_pieces(sums.reshape(MICRO, n, 8 * BLOCK)).reshape(-1, BLOCK)
    first_bits = tuple(micro_order(half, "seq")[0] for half in range(2))
    normed, dy, dz, d_gain_out, *out_part = out_project(z, dn, y, sums, gain, w_o, first_bits)
    d_gain_out = jnp.sum(d_gain_out, axis=0)

    scatter = lambda a: lax.psum_scatter(a, "dp", scatter_dimension=0, tiled=True)
    split = lambda a: [a[q * rows : (q + 1) * rows] for q in range(n)]
    out_stages = scatter_stages(out_part)
    next(out_stages)
    part_o = dot(cot, normed, TN).astype(BF)
    part_z = dot(hidden, dz, TN).astype(BF)
    got_o, got_z = scatter(part_o), scatter(part_z)

    through_in = lambda micro, one: back_project(micro, dz, one, w_z, w_x, first_bits)
    scan_back = lambda micro, *done: scan_backward(
        place, micro, proj_x, conv_loc, skip, heads, aux, masks, act, slope, dy, states, hl, *done
    )

    px_0, conv_0, vec_0, skip_0 = scan_back(0, part_o, part_z)
    hid_0 = through_in(0, px_0)
    out_got, out_sent = out_stages.send([hid_0[0]])
    stages_0 = scatter_stages(hid_0)
    hid_got, sent = next(stages_0)
    px_1, conv_1, vec_1, skip_1 = scan_back(1, *sent, *out_sent)
    [px_1] = after([px_1], *hid_got, *out_got)
    part_x = dot(hidden, jnp.concatenate([px_0, px_1], axis=0), TN).astype(BF)
    got_x = scatter(part_x)
    hid_got, sent = stages_0.send([part_x])
    [got_o, got_z] = after([got_o, got_z], px_1)
    sent_oz, got_oz = exchange(split(jnp.concatenate([got_o, got_z], axis=1)), rank)
    [px_1] = after([px_1], part_x, *sent, *got_oz)
    hid_1 = after(through_in(1, px_1), *hid_got)
    stages_1 = scatter_stages(hid_1)
    hid_got, hid_sent = next(stages_1)
    output = (tok + finish(out_stages, [hid_1[0]]).astype(F32)).astype(BF)

    d_conv = (conv_0 + conv_1).reshape(CONV + 1, 8, -1).sum(axis=1)
    d_skip = jnp.sum((skip_0 + skip_1).reshape(8, hl, HEADDIM), axis=(0, 2))
    d_vec = vec_0 + vec_1
    head_rows = jnp.concatenate([d_vec[:hl, 0], d_skip, d_vec[:hl, 1]])
    small = jnp.concatenate([d_conv.reshape(-1), d_gain_out, head_rows])
    small_size = small.shape[0]
    small = jnp.pad(small, (0, -small_size % 1024)).reshape(-1, LANES)
    [small] = after([small], hid_1[0])
    for bit in axis_bits("dp"):
        small = small + swapped(small, "dp", bit)
    small = [small] + after([swapped(small, "seq", mask) for mask in range(1, n)], *hid_got)
    small = jnp.stack(turned(small, rank)).reshape(n, -1)[:, :small_size]
    conv_all = small[:, : (CONV + 1) * (xw + bc)].reshape(n, CONV + 1, xw + bc)
    conv_tot = jnp.concatenate(
        [conv_all[:, :, :xw].transpose(1, 0, 2).reshape(CONV + 1, INNER), jnp.sum(conv_all[:, :, xw:], axis=0)], axis=1
    )
    gain_out_tot = small[:, (CONV + 1) * (xw + bc) : small_size - 3 * hl].reshape(-1)
    heads_tot = small[:, small_size - 3 * hl :].reshape(n, 3, hl).transpose(1, 0, 2).reshape(-1)

    [got_x] = after([got_x], conv_tot, output)
    sent_x, got_x = exchange(split(got_x), rank)
    d_hidden = jnp.concatenate([finish(stages_0, [hid_1[0]]), finish(stages_1, sent_x)], axis=0).astype(F32)
    dh = d_hidden * gain_in
    d_tok = r_in * (dh - tok * (r_in * r_in) * jnp.mean(dh * tok, axis=-1, keepdims=True))
    input_grad = (cotangent.astype(F32) + d_tok).astype(BF)
    got_x = after(got_x, input_grad)
    got_oz, got_x = (turned(sent[:1] + got, rank) for sent, got in ((sent_oz, got_oz), (sent_x, got_x)))

    together = lambda parts, lo, hi: jnp.concatenate([one[:, lo:hi] for one in parts], axis=1).astype(F32)
    g_bc = sum(one[:, xw : xw + bc].astype(F32) for one in got_x)
    shard_in = jnp.concatenate(
        [together(got_oz, xw, 2 * xw), together(got_x, 0, xw), g_bc, together(got_x, xw + bc, xw + bc + hl)], axis=1
    )
    shard_out = together(got_oz, 0, xw).T

    own = lax.axis_index("dp") * n + rank
    own_gain = lax.dynamic_slice_in_dim(gain_in, own * rows, rows)
    d_gain_in = jnp.sum(in_low.astype(F32) * shard_in, axis=1) / own_gain
    partial_sq = jnp.sum(shard_in * shard_in) + jnp.sum(shard_out * shard_out)
    last = lax.dynamic_update_slice(jnp.zeros((D + 1024,), F32), d_gain_in, (own * rows,))
    last = lax.dynamic_update_slice(last, partial_sq[None], (D,))
    last = sum_all(last.reshape(-1, LANES)).reshape(-1)
    vec_tot = jnp.concatenate([heads_tot, last[:D], gain_out_tot])
    shard_conv = lax.dynamic_slice_in_dim(conv_tot, own * cw, cw, 1)
    grad_norm = jnp.sqrt(last[D] + jnp.sum(conv_tot * conv_tot) + jnp.sum(vec_tot * vec_tot))
    clip = jnp.minimum(1.0, CLIP_NORM / (grad_norm + 1e-06))
    in_new = adamw(in_weight, shard_in, in_m, in_v, clip, WEIGHT_DECAY)
    conv_new = adamw(conv_weight, shard_conv, conv_m, conv_v, clip, WEIGHT_DECAY)
    out_new = adamw(out_weight, shard_out, out_m, out_v, clip, WEIGHT_DECAY)
    vec_new = adamw(packed, vec_tot, packed_m, packed_v, clip, 0.0)
    return (
        output, input_grad, grad_norm,
        in_weight + in_new[0], in_new[1], in_new[2],
        conv_new[0], conv_new[1], conv_new[2],
        out_weight + out_new[0], out_new[1], out_new[2],
        vec_new[0], vec_new[1], vec_new[2],
    )


def solution(mesh):
    tok, col, row = P(None, ALL, None), P(None, ALL), P(ALL, None)
    return jax.shard_map(
        per_device,
        mesh=mesh,
        in_specs=(tok, tok, P(None, "dp"), row, row, row, col, col, col, col, col, col, P(), P(), P()),
        out_specs=(tok, tok, P(), row, row, row, col, col, col, col, col, col, P(), P(), P()),
        check_vma=False,
    )
```

```python
import functools

import jax
import jax.numpy as jnp
from jax import lax
from jax.experimental import pallas as pl
from jax.experimental.pallas import tpu as pltpu
from jax.sharding import PartitionSpec as P

D = 2048
HEADS = 64
HEADDIM = 64
STATE = 128
CONV = 4
BLOCK = 256
MICRO = 2
INNER = 4096
CH = 4352
NORM_EPS = 1e-05
LEARN_RATE = 0.004
BETA_ONE = 0.9
BETA_TWO = 0.95
FIX_ONE = 1.0 - 0.9**10
FIX_TWO = 1.0 - 0.95**10
ADAM_EPS = 1e-08
WEIGHT_DECAY = 0.1
CLIP_NORM = 1.0
BF = jnp.bfloat16
F32 = jnp.float32
ALL = ("dp", "seq")


def dot(a, b, dims, out=F32):
    return lax.dot_general(a, b, (dims, ((), ())), preferred_element_type=out)


NN = ((1,), (0,))
NT = ((1,), (1,))
TN = ((0,), (0,))
LANES = 128
PAIR = 2 * HEADDIM
VMEM = 56 * 1024 * 1024
SLOT = 16
TINY = 1e-37
CAP = 85.0


def iota2(shape, dim):
    return lax.broadcasted_iota(jnp.int32, shape, dim)


def tree(value, rows=8):
    while value.shape[0] > rows:
        half = value.shape[0] // 2
        value = value[:half] + value[half:]
    return value


def thirds(value):
    high = value.astype(BF).astype(F32)
    rest = value - high
    mid = rest.astype(BF).astype(F32)
    return high, mid, (rest - mid).astype(BF).astype(F32)


def running_sum(values, reverse):
    row, col = iota2((BLOCK, BLOCK), 0), iota2((BLOCK, BLOCK), 1)
    ones = jnp.where(row >= col if reverse else row <= col, 1.0, 0.0).astype(BF)
    sums = dot(jnp.concatenate(thirds(values), axis=0).astype(BF), ones, NN)
    return sums[:SLOT] + sums[SLOT : 2 * SLOT] + sums[2 * SLOT :]


def step_rows(raw, heads, masks):
    lifted = raw.astype(F32).T[:SLOT] + heads[:, 0:1]
    dt = jnp.maximum(lifted, 0.0) + jnp.log1p(jnp.exp(-jnp.abs(lifted)))
    cum = running_sum(dt * heads[:, 1:2], False)
    entry = jnp.exp(cum) * masks[1:2, :]
    dt_end = dt * jnp.exp(cum[:, BLOCK - 1 : BLOCK] - cum) * masks[2:3, :]
    return lifted, dt, cum, entry, dt_end


def two(value):
    high = value.astype(BF).astype(F32)
    return [high, value - high]


def as_columns(gap_rows, entry, dt_end):
    ones = jnp.where(iota2((SLOT, BLOCK), 0) < 3, 1.0, 0.0)
    return jnp.concatenate([*thirds(gap_rows), ones, *two(entry), *two(dt_end)], axis=0).T.astype(BF)


def gap_right_init(right, hl):
    row = iota2((3 * SLOT, BLOCK), 0)
    for h in range(hl):
        right[0 : 3 * SLOT, h * BLOCK : (h + 1) * BLOCK] = jnp.where((row & (SLOT - 1)) == h, 1.0, 0.0).astype(BF)


def gap_right_fill(right, values, hl):
    row = iota2((SLOT, BLOCK), 0)
    high, mid, low = thirds(values)
    for h in range(hl):
        one = slice(h, h + 1)
        slab = jnp.where(row == 0, high[one], jnp.where(row == 1, mid[one], jnp.where(row == 2, low[one], 0.0)))
        right[3 * SLOT :, h * BLOCK : (h + 1) * BLOCK] = slab.astype(BF)


def head_spread_init(spreads, hl):
    row, col = iota2(spreads.shape, 0), iota2(spreads.shape, 1)
    head = jnp.where(col < hl * HEADDIM, col, col - hl * HEADDIM) // HEADDIM
    slot = jnp.where(col < hl * HEADDIM, 2, 3)
    spreads[...] = jnp.where(((row & (SLOT - 1)) == head) & (row // (2 * SLOT) == slot), 1.0, 0.0).astype(BF)


def stacked(left, pair_values):
    zero = jnp.zeros_like(pair_values)
    return jnp.concatenate([jnp.where(left, pair_values, zero), jnp.where(left, zero, pair_values)], axis=0)


def conv_chunk(window, conv_w, valid, lo, hi):
    out = conv_w[CONV : CONV + 1, lo:hi] + conv_w[CONV - 1 : CONV, lo:hi] * window[8 : 8 + BLOCK, lo:hi]
    for tap in range(CONV - 1):
        out += conv_w[tap : tap + 1, lo:hi] * (window[5 + tap : 5 + tap + BLOCK, lo:hi] * valid[tap])
    return out


def spread(aux_v, at):
    return jnp.broadcast_to(aux_v[:, at : at + 1], (BLOCK, LANES))


def forward_kernel(place, proj, conv_w, skip, heads, aux, masks, y_out, s_out, act, slope, window, state, right, carried, spreads, *, hl):
    width = hl * HEADDIM
    conv_width = width + 2 * STATE

    @pl.when(pl.program_id(1) == 0)
    def _():
        window[0:8, :] = jnp.zeros((8, conv_width), F32)
        state[...] = jnp.zeros(state.shape, F32)
        gap_right_init(right, hl)
        head_spread_init(spreads, hl)

    aux_v = aux[...]
    valid = [spread(aux_v, tap) for tap in range(CONV - 1)]
    for lo in range(0, conv_width, LANES):
        hi = lo + LANES
        window[8 : 8 + BLOCK, lo:hi] = proj[:, lo:hi].astype(F32)
        out = conv_chunk(window, conv_w, valid, lo, hi)
        sig = jax.nn.sigmoid(out)
        silu = out * sig
        act[:, lo:hi] = silu.astype(BF)
        slope[:, lo:hi] = (sig + silu * (1.0 - sig)).astype(BF)
    window[0:8, :] = window[BLOCK : BLOCK + 8, :]

    _, dt, cum, entry, dt_end = step_rows(proj[:, conv_width : conv_width + LANES], heads[...], masks)
    columns = as_columns(cum, entry, dt_end)
    gaps = columns[:, : 4 * SLOT]
    gap_right_fill(right, jnp.log(jnp.maximum(dt, TINY)) - cum, hl)
    bm, cm = act[:, width : width + STATE], act[:, width + STATE :]
    same = (aux_v[:, 3:4] == masks[0:1, :]) & (iota2((BLOCK, BLOCK), 0) >= iota2((BLOCK, BLOCK), 1))
    inner = jnp.where(same, dot(cm, bm, NT), 0.0)
    left = iota2((BLOCK, PAIR), 1) < HEADDIM
    top = iota2((PAIR, STATE), 0) < HEADDIM
    last = entry[:, BLOCK - 1 : BLOCK]
    s_out[0] = state[...].astype(BF)
    carried[...] = dot(columns, spreads[...], NN)
    carried[:, :width] = carried[:, :width] * dot(cm, s_out[0], NT)
    for pair in range(hl // 2):
        first = 2 * pair
        lo, hi = pair * PAIR, (pair + 1) * PAIR
        xp = act[:, lo:hi]
        mix = []
        for h in (first, first + 1):
            decay = jnp.exp(jnp.minimum(dot(gaps, right[:, h * BLOCK : (h + 1) * BLOCK], NN), CAP))
            mix.append((inner * decay).astype(BF))
        xf = xp.astype(F32)
        y = dot(jnp.concatenate(mix, axis=1), stacked(left, xp), NN)
        y += carried[:, lo:hi] + skip[0:1, lo:hi] * xf
        y_out[:, lo:hi] = y.astype(BF)
        weighted = (xf * carried[:, width + lo : width + hi]).astype(BF)
        keep = jnp.where(top, last[first : first + 1], last[first + 1 : first + 2])
        state[lo:hi, :] = keep * state[lo:hi, :] + dot(weighted, bm, TN)


def backward_kernel(place, proj, conv_w, skip, heads, aux, masks, act, slope, dy, s_in, *refs, hl):
    dproj, dconv, dvec, dskip, dwin, grad_s, dcb, colsum, dkeep, right, carried, later_w, spreads, picks, sums, used, into = refs[-17:]
    width = hl * HEADDIM
    conv_width = width + 2 * STATE

    @pl.when(pl.program_id(0) == 0)
    def _():
        dconv[...] = jnp.zeros(dconv.shape, F32)
        dvec[...] = jnp.zeros(dvec.shape, F32)
        dskip[...] = jnp.zeros(dskip.shape, F32)
        dwin[BLOCK : BLOCK + 8, :] = jnp.zeros((8, conv_width), F32)
        grad_s[...] = jnp.zeros(grad_s.shape, F32)
        colsum[...] = jnp.zeros(colsum.shape, F32)
        dkeep[...] = jnp.zeros(dkeep.shape, F32)
        gap_right_init(right, hl)
        head_spread_init(spreads, hl)
        picks[...] = jnp.where(iota2(picks.shape, 0) == iota2(picks.shape, 1) // BLOCK, 1.0, 0.0).astype(BF)
        sums[...] = jnp.where(iota2(sums.shape, 0) == iota2(sums.shape, 1) // HEADDIM, 1.0, 0.0).astype(BF)

    aux_v = aux[...]
    lifted, dt, cum, entry, dt_end = step_rows(proj[:, conv_width : conv_width + LANES], heads[...], masks)
    a_neg = heads[:, 1:2]
    columns = as_columns(jnp.log(jnp.maximum(dt, TINY)) - cum, entry, dt_end)
    gaps = columns[:, : 4 * SLOT]
    gap_right_fill(right, cum, hl)
    bm, cm = act[:, width : width + STATE], act[:, width + STATE :]
    same = (aux_v[:, 3:4] == masks[0:1, :]) & (iota2((BLOCK, BLOCK), 0) <= iota2((BLOCK, BLOCK), 1))
    inner = jnp.where(same, dot(bm, cm, NT), 0.0)
    left = iota2((BLOCK, PAIR), 1) < HEADDIM
    top = iota2((PAIR, STATE), 0) < HEADDIM
    last = entry[:, BLOCK - 1 : BLOCK]
    d_row = jnp.zeros((SLOT, BLOCK), F32)
    d_b = jnp.zeros((BLOCK, STATE), F32)
    d_c = jnp.zeros((BLOCK, STATE), F32)
    spreaded = dot(columns, spreads[...], NN)
    carried[...] = spreaded
    later_w[:, :width] = dot(cm, s_in[0], NT)
    later_w[:, width:] = dot(bm, grad_s[...].astype(BF), NT)

    for pair in range(hl // 2):
        first = 2 * pair
        lo, hi = pair * PAIR, (pair + 1) * PAIR
        xp, dyp = act[:, lo:hi], dy[:, lo:hi]
        xf, dyf = xp.astype(F32), dyp.astype(F32)
        d_mix = dot(stacked(left, xp), dyp, NT)
        mix, pairwise = [], []
        d_inner = 0.0
        for at, h in enumerate((first, first + 1)):
            decay = jnp.exp(jnp.minimum(dot(gaps, right[:, h * BLOCK : (h + 1) * BLOCK], NN), CAP))
            mix.append((inner * decay).astype(BF))
            part = d_mix[at * BLOCK : (at + 1) * BLOCK] * decay
            d_inner += part
            part = (part * inner).astype(BF)
            pairwise.append(part)
            colsum[h : h + 1, :] = jnp.sum(tree(part.astype(F32)), axis=0, keepdims=True)
        d_row += dot(picks[:, first * BLOCK : (first + 2) * BLOCK], jnp.concatenate(pairwise, axis=1), NT)
        if pair == 0:
            dcb[...] = d_inner
        else:
            dcb[...] += d_inner
        later = grad_s[lo:hi, :]
        low = s_in[0, lo:hi, :]
        end_p = carried[:, width + lo : width + hi]
        from_end = later_w[:, width + lo : width + hi] * end_p
        dx = dot(jnp.concatenate(mix, axis=1), stacked(left, dyp), NN) + from_end + skip[0:1, lo:hi] * dyf
        dwin[0:BLOCK, lo:hi] = slope[:, lo:hi].astype(F32) * dx
        used[:, lo:hi] = (from_end * xf).astype(BF)
        entering = carried[:, lo:hi] * dyf
        into[:, lo:hi] = (entering * later_w[:, lo:hi]).astype(BF)
        entering = entering.astype(BF)
        dskip[:, lo:hi] += tree(xf * dyf)
        kept = later * low.astype(F32)
        dkeep[first : first + 1, :] = jnp.sum(tree(kept[:HEADDIM]), axis=0, keepdims=True)
        dkeep[first + 1 : first + 2, :] = jnp.sum(tree(kept[HEADDIM:]), axis=0, keepdims=True)
        weighted = (xf * end_p).astype(BF)
        d_b += dot(weighted, later.astype(BF), NN)
        d_c += dot(entering, low, NN)
        keep = jnp.where(top, last[first : first + 1], last[first + 1 : first + 2])
        grad_s[lo:hi, :] = dot(entering, cm, TN) + keep * later

    d_inner = jnp.where(same, dcb[...], 0.0).astype(BF)
    d_b += dot(d_inner, cm, NN)
    d_c += dot(d_inner, bm, TN)
    dwin[0:BLOCK, width : width + STATE] = slope[:, width : width + STATE].astype(F32) * d_b
    dwin[0:BLOCK, width + STATE :] = slope[:, width + STATE :].astype(F32) * d_c

    d_end = dot(sums[...], used[...], NT)
    through = d_row + d_end
    d_last = jnp.sum(d_end, axis=1, keepdims=True) + jnp.sum(dkeep[...], axis=1, keepdims=True) * last
    d_cum = dot(sums[...], into[...], NT) + colsum[...] - through
    d_cum += jnp.where(iota2((SLOT, BLOCK), 1) == BLOCK - 1, d_last, 0.0)
    d_a = running_sum(d_cum, True)
    sig = jax.nn.sigmoid(lifted)
    d_raw = through * jnp.where(dt > TINY, sig / jnp.maximum(dt, TINY), 1.0) + d_a * a_neg * sig
    d_raw = jnp.where(iota2((SLOT, BLOCK), 0) < hl, d_raw, 0.0)
    dproj[:, conv_width : conv_width + LANES] = jnp.concatenate([d_raw, jnp.zeros((LANES - SLOT, BLOCK), F32)], axis=0).T.astype(BF)
    lane = iota2((SLOT, LANES), 1)
    d_log = jnp.sum(d_a * dt, axis=1, keepdims=True) * a_neg
    dvec[...] += jnp.where(lane == 0, d_log, jnp.where(lane == 1, jnp.sum(d_raw, axis=1, keepdims=True), 0.0))

    valid = [spread(aux_v, 4 + tap) for tap in range(CONV - 1)]
    for lo in range(0, conv_width, LANES):
        hi = lo + LANES
        own = dwin[0:BLOCK, lo:hi]
        value = proj[:, lo:hi].astype(F32)
        grad = conv_w[CONV - 1 : CONV, lo:hi] * own
        dconv[CONV * 8 : CONV * 8 + 8, lo:hi] += tree(own)
        dconv[(CONV - 1) * 8 : CONV * 8, lo:hi] += tree(own * value)
        for tap in range(CONV - 1):
            ahead = CONV - 1 - tap
            moved = dwin[ahead : ahead + BLOCK, lo:hi] * valid[tap]
            grad += conv_w[tap : tap + 1, lo:hi] * moved
            dconv[tap * 8 : tap * 8 + 8, lo:hi] += tree(moved * value)
        dproj[:, lo:hi] = grad.astype(BF)
    dwin[BLOCK : BLOCK + 8, :] = dwin[0:8, :]


def segment_aux(segments):
    micro, length = segments.shape
    nb = length // BLOCK
    seg = segments.astype(F32)
    blocks = seg.reshape(micro, nb, BLOCK)
    prev = jnp.concatenate([jnp.full((micro, 1), -1.0, F32), blocks[:, :-1, -1]], axis=1)
    reach = range(CONV - 1, 0, -1)
    earlier = [jnp.pad(seg, ((0, 0), (by, 0)), constant_values=-1.0)[:, :length] == seg for by in reach]
    later = [jnp.pad(seg, ((0, 0), (0, by)), constant_values=-1.0)[:, by:] == seg for by in reach]
    columns = [c.astype(F32) for c in (*earlier, seg, *later, jnp.zeros_like(seg))]
    aux = jnp.stack(columns, axis=-1).reshape(micro * length, 8)
    zero = jnp.zeros_like(blocks)
    masks = [blocks, blocks == prev[:, :, None], blocks == blocks[:, :, -1:]] + [zero] * 5
    return aux, jnp.stack([m.astype(F32) for m in masks], axis=2).reshape(micro * nb * 8, BLOCK)


def head_columns(a_log, dt_bias):
    hl = a_log.shape[0]
    both = jnp.stack([dt_bias, -jnp.exp(a_log)], axis=1)
    return jnp.pad(both, ((0, SLOT - hl), (0, LANES - 2)))


def scan_forward(place, proj, conv_w, skip, heads, aux, masks, hl):
    tokens = proj.shape[0]
    nb = tokens // MICRO // BLOCK
    width = hl * HEADDIM
    conv_width = width + 2 * STATE
    held = lambda m, j, place: (m * nb + (j ^ place[0]), 0)
    at = lambda m, j, place: (m * nb + j, 0)
    whole = lambda m, j, place: (0, 0)
    grid_spec = pltpu.PrefetchScalarGridSpec(
        num_scalar_prefetch=1,
        grid=(MICRO, nb),
        in_specs=[
            pl.BlockSpec((BLOCK, conv_width + LANES), held),
            pl.BlockSpec((8, conv_width), whole),
            pl.BlockSpec(skip.shape, whole),
            pl.BlockSpec(heads.shape, whole),
            pl.BlockSpec((BLOCK, 8), at),
            pl.BlockSpec((8, BLOCK), at),
        ],
        out_specs=[
            pl.BlockSpec((BLOCK, width), held),
            pl.BlockSpec((1, width, STATE), lambda m, j, place: (m * nb + j, 0, 0)),
            pl.BlockSpec((BLOCK, conv_width), held),
            pl.BlockSpec((BLOCK, conv_width), held),
        ],
        scratch_shapes=[
            pltpu.VMEM((BLOCK + 8, conv_width), F32),
            pltpu.VMEM((width, STATE), F32),
            pltpu.VMEM((4 * SLOT, hl * BLOCK), BF),
            pltpu.VMEM((BLOCK, 2 * width), F32),
            pltpu.VMEM((LANES, 2 * width), BF),
        ],
    )
    return pl.pallas_call(
        functools.partial(forward_kernel, hl=hl),
        grid_spec=grid_spec,
        out_shape=[
            jax.ShapeDtypeStruct((tokens, width), BF),
            jax.ShapeDtypeStruct((MICRO * nb, width, STATE), BF),
            jax.ShapeDtypeStruct((tokens, conv_width), BF),
            jax.ShapeDtypeStruct((tokens, conv_width), BF),
        ],
        compiler_params=pltpu.CompilerParams(vmem_limit_bytes=VMEM, dimension_semantics=("arbitrary", "arbitrary")),
        name="scan_forward",
    )(place, proj, conv_w, skip, heads, aux, masks)


def scan_backward(place, micro, proj, conv_w, skip, heads, aux, masks, act, slope, dy, states, hl, *done):
    tokens = proj.shape[0] // MICRO
    nb = tokens // BLOCK
    width = hl * HEADDIM
    conv_width = width + 2 * STATE
    full = conv_width + LANES
    first = micro * nb
    held = lambda j, place: (first + ((nb - 1 - j) ^ place[0]), 0)
    at = lambda j, place: (first + nb - 1 - j, 0)
    whole = lambda j, place: (0, 0)
    grid_spec = pltpu.PrefetchScalarGridSpec(
        num_scalar_prefetch=1,
        grid=(nb,),
        in_specs=[
            pl.BlockSpec((BLOCK, full), held),
            pl.BlockSpec((8, conv_width), whole),
            pl.BlockSpec(skip.shape, whole),
            pl.BlockSpec(heads.shape, whole),
            pl.BlockSpec((BLOCK, 8), at),
            pl.BlockSpec((8, BLOCK), at),
            pl.BlockSpec((BLOCK, conv_width), held),
            pl.BlockSpec((BLOCK, conv_width), held),
            pl.BlockSpec((BLOCK, width), held),
            pl.BlockSpec((1, width, STATE), lambda j, place: (first + nb - 1 - j, 0, 0)),
        ]
        + [pl.BlockSpec(memory_space=pl.ANY)] * len(done),
        out_specs=[
            pl.BlockSpec((BLOCK, full), lambda j, place: ((nb - 1 - j) ^ place[0], 0)),
            pl.BlockSpec((8 * (CONV + 1), conv_width), whole),
            pl.BlockSpec((SLOT, LANES), whole),
            pl.BlockSpec((8, width), whole),
        ],
        scratch_shapes=[
            pltpu.VMEM((BLOCK + 8, conv_width), F32),
            pltpu.VMEM((width, STATE), F32),
            pltpu.VMEM((BLOCK, BLOCK), F32),
            pltpu.VMEM((SLOT, BLOCK), F32),
            pltpu.VMEM((SLOT, STATE), F32),
            pltpu.VMEM((4 * SLOT, hl * BLOCK), BF),
            pltpu.VMEM((BLOCK, 2 * width), F32),
            pltpu.VMEM((BLOCK, 2 * width), F32),
            pltpu.VMEM((LANES, 2 * width), BF),
            pltpu.VMEM((SLOT, hl * BLOCK), BF),
            pltpu.VMEM((SLOT, width), BF),
            pltpu.VMEM((BLOCK, width), BF),
            pltpu.VMEM((BLOCK, width), BF),
        ],
    )
    return pl.pallas_call(
        functools.partial(backward_kernel, hl=hl),
        grid_spec=grid_spec,
        out_shape=[
            jax.ShapeDtypeStruct((tokens, full), BF),
            jax.ShapeDtypeStruct((8 * (CONV + 1), conv_width), F32),
            jax.ShapeDtypeStruct((SLOT, LANES), F32),
            jax.ShapeDtypeStruct((8, width), F32),
        ],
        compiler_params=pltpu.CompilerParams(vmem_limit_bytes=VMEM, dimension_semantics=("arbitrary",)),
        name="scan_backward",
    )(place, proj, conv_w, skip, heads, aux, masks, act, slope, dy, states, *done)


def fetch(pieces, buffer, sems, step):
    @pl.when(step == 0)
    def _():
        pltpu.make_async_copy(pieces[0], buffer.at[0], sems.at[0]).start()

    for at in range(1, len(pieces)):

        @pl.when(step == at - 1)
        def _():
            pltpu.make_async_copy(pieces[at], buffer.at[at % 2], sems.at[at % 2]).start()

    slot = step % 2
    pltpu.make_async_copy(pieces[0], buffer.at[slot], sems.at[slot]).wait()
    return slot


def emit(value, targets, buffer, sems, micro, place, bits, step, steps):
    slot = step % 2
    rows = value.shape[0] // 2

    def waiting(at):
        for half in range(2):
            pltpu.make_async_copy(buffer.at[at, pl.ds(half * rows, rows)], targets[0].at[0, 0], sems.at[at, half]).wait()

    @pl.when(step >= 2)
    def _():
        waiting(slot)

    buffer[slot] = value
    for half, bit in enumerate(bits):
        index = place // (2 * bit) * bit + place % bit
        set_ = (place // bit) % 2
        for target, wanted in ((targets[2 * half], 1), (targets[2 * half + 1], 0)):

            @pl.when(set_ == wanted)
            def _():
                pltpu.make_async_copy(
                    buffer.at[slot, pl.ds(half * rows, rows)], target.at[micro, index], sems.at[slot, half]
                ).start()

    @pl.when(step == steps - 1)
    def _():
        waiting(0)
        waiting(1)


def emitted(some, n, depth):
    shapes = [jax.ShapeDtypeStruct((some, n // 2, BLOCK // 2, depth), BF)] * 4
    return shapes, [pl.BlockSpec(memory_space=pl.ANY)] * 4, [pltpu.VMEM((2, BLOCK, depth), BF), pltpu.SemaphoreType.DMA((2, 2))]


def fixed(array):
    return pl.BlockSpec(array.shape, lambda i: (0, 0), pipeline_mode=pl.Buffered(1))


def by_rows(width):
    return pl.BlockSpec((BLOCK, width), lambda i: (i, 0))


def arbitrary(name):
    return dict(compiler_params=pltpu.CompilerParams(vmem_limit_bytes=VMEM, dimension_semantics=("arbitrary",)), name=name)


def in_kernel(*refs, count):
    pieces, w, (proj, hidden, buffer, sems) = refs[1 : count + 1], refs[count + 1], refs[-4:]
    slot = fetch(pieces, buffer, sems, pl.program_id(0))
    value = buffer[slot]
    hidden[...] = value
    proj[...] = dot(value, w[...], NN).astype(BF)


def in_project(pieces, places, total, w, earlier=(), done=()):
    count = len(pieces)
    depth, width = w.shape
    anywhere = [pl.BlockSpec(memory_space=pl.ANY)]
    at = lambda i, table: (table[i], 0)
    return pl.pallas_call(
        functools.partial(in_kernel, count=count),
        grid_spec=pltpu.PrefetchScalarGridSpec(
            num_scalar_prefetch=1,
            grid=(count,),
            in_specs=anywhere * count
            + [pl.BlockSpec(w.shape, lambda i, table: (0, 0), pipeline_mode=pl.Buffered(1))]
            + anywhere * (len(earlier) + len(done)),
            out_specs=[pl.BlockSpec((BLOCK, width), at), pl.BlockSpec((BLOCK, depth), at)],
            scratch_shapes=[pltpu.VMEM((2, BLOCK, depth), BF), pltpu.SemaphoreType.DMA((2,))],
        ),
        out_shape=[
            jax.ShapeDtypeStruct((total * BLOCK, width), BF),
            jax.ShapeDtypeStruct((total * BLOCK, depth), BF),
        ],
        input_output_aliases={count + 2 + i: i for i in range(len(earlier))},
        **arbitrary("in_project"),
    )(jnp.array(places, jnp.int32), *pieces, w, *earlier, *done)


def gate_kernel(*refs, count):
    pieces, (z, w_o, y, gain, dn_out, cot_out, sums, buffer, sems) = refs[:count], refs[count:]
    slot = fetch(pieces, buffer, sems, pl.program_id(0))
    cot = buffer[slot]
    cot_out[...] = cot
    dn = dot(cot, w_o[...], NN)
    dn_out[...] = dn.astype(BF)
    zf = z[...].astype(F32)
    gz = y[...].astype(F32) * (zf * jax.nn.sigmoid(zf))
    ones = jnp.ones((8, gz.shape[1]), BF)
    first = dot(ones, (gz * gz).astype(BF), NT)
    second = dot(ones, (dn * gain[0:1, :] * gz).astype(BF), NT)
    sums[...] = jnp.where(iota2((8, BLOCK), 0) == 0, first, second)


def gate_forward(pieces, z, w_o, y, gain):
    count = len(pieces)
    depth, width = w_o.shape
    return pl.pallas_call(
        functools.partial(gate_kernel, count=count),
        grid=(count,),
        in_specs=[pl.BlockSpec(memory_space=pl.ANY)] * count + [by_rows(width), fixed(w_o), by_rows(width), fixed(gain)],
        out_specs=[by_rows(width), by_rows(depth), pl.BlockSpec((8, BLOCK), lambda i: (i, 0))],
        out_shape=[
            jax.ShapeDtypeStruct((count * BLOCK, width), BF),
            jax.ShapeDtypeStruct((count * BLOCK, depth), BF),
            jax.ShapeDtypeStruct((count * 8, BLOCK), F32),
        ],
        scratch_shapes=[pltpu.VMEM((2, BLOCK, depth), BF), pltpu.SemaphoreType.DMA((2,))],
        **arbitrary("gate_forward"),
    )(*pieces, z, w_o, y, gain)


def out_kernel(z_in, dn_in, y_in, sums, gain, w_o, normed, dy, dz, dgain, *refs, n, bits):
    step = pl.program_id(0)
    @pl.when(pl.program_id(0) == 0)
    def _():
        dgain[...] = jnp.zeros(dgain.shape, F32)

    scale = lax.rsqrt(sums[0:1, :] / INNER + NORM_EPS)
    slope = scale * scale * scale * sums[1:2, :] / INNER
    row = iota2((LANES, BLOCK), 0)
    columns = jnp.where(row == 0, scale, jnp.where(row == 1, slope, 0.0)).T
    scale, slope = columns[:, 0:1], columns[:, 1:2]
    for lo in range(0, normed.shape[1], 2 * LANES):
        hi = lo + 2 * LANES
        z, y, dn = z_in[:, lo:hi].astype(F32), y_in[:, lo:hi].astype(F32), dn_in[:, lo:hi].astype(F32)
        sig = jax.nn.sigmoid(z)
        silu = z * sig
        gz = y * silu
        unit = gz * scale
        normed[:, lo:hi] = (unit * gain[0:1, lo:hi]).astype(BF)
        dgain[:, lo:hi] += jnp.sum((dn * unit).reshape(BLOCK // 8, 8, 2 * LANES), axis=0)
        d_gz = dn * gain[0:1, lo:hi] * scale - gz * slope
        dy[:, lo:hi] = (d_gz * silu).astype(BF)
        dz[:, lo:hi] = (d_gz * y * (sig + silu * (1.0 - sig))).astype(BF)
    out = dot(normed[...], w_o[...], NT).astype(BF)
    emit(out, refs[:4], refs[4], refs[5], step // n, step % n, bits, step, MICRO * n)


def out_project(z, dn, y, sums, gain, w_o, bits):
    depth, width = w_o.shape
    tokens = z.shape[0]
    n = tokens // BLOCK // MICRO
    one = by_rows(width)
    shapes, places, scratch = emitted(MICRO, n, depth)
    return pl.pallas_call(
        functools.partial(out_kernel, n=n, bits=bits),
        grid=(tokens // BLOCK,),
        in_specs=[one, one, one, pl.BlockSpec((8, BLOCK), lambda i: (i, 0)), fixed(gain), fixed(w_o)],
        out_specs=[one, one, one, pl.BlockSpec((8, width), lambda i: (0, 0))] + places,
        out_shape=[jax.ShapeDtypeStruct((tokens, width), BF)] * 3 + [jax.ShapeDtypeStruct((8, width), F32)] + shapes,
        scratch_shapes=scratch,
        **arbitrary("out_project"),
    )(z, dn, y, sums, gain, w_o)


def back_kernel(dz, px, w_z, w_x, *refs, n, bits):
    step = pl.program_id(0)
    out = (dot(dz[...], w_z[...], NT) + dot(px[...], w_x[...], NT)).astype(BF)
    emit(out, refs[:4], refs[4], refs[5], 0, step, bits, step, n)


def back_project(micro, dz, px, w_z, w_x, bits):
    tokens, width = px.shape
    depth = w_z.shape[0]
    n = tokens // BLOCK
    shapes, places, scratch = emitted(1, n, depth)
    return pl.pallas_call(
        functools.partial(back_kernel, n=n, bits=bits),
        grid=(n,),
        in_specs=[pl.BlockSpec((BLOCK, dz.shape[1]), lambda i: (micro * n + i, 0)), by_rows(width), fixed(w_z), fixed(w_x)],
        out_specs=places,
        out_shape=shapes,
        scratch_shapes=scratch,
        **arbitrary("back_project"),
    )(dz, px, w_z, w_x)


def shard_kernel(spot, *refs, n, hl):
    fronts, backs, (weight, gain, shard_in, shard_out, last) = refs[:n], refs[n : 2 * n], refs[2 * n :]
    rank, own = spot[0], spot[1]
    width = hl * HEADDIM
    rows = weight.shape[0]
    lane = iota2((rows, LANES), 1)
    square = jnp.zeros((rows, LANES), F32)
    scaled = jnp.zeros((rows, LANES), F32)
    shared = [jnp.zeros((rows, LANES), F32) for _ in range(2 * STATE // LANES + 1)]
    for mask in range(n):
        at = (rank ^ mask) * width
        for lo in range(0, width, LANES):
            spot_z = pl.multiple_of(at + lo, LANES)
            spot_x = pl.multiple_of(INNER + at + lo, LANES)
            out = fronts[mask][:, lo : lo + LANES].astype(F32)
            z = fronts[mask][:, width + lo : width + lo + LANES].astype(F32)
            x = backs[mask][:, lo : lo + LANES].astype(F32)
            shard_out[:, pl.ds(spot_z, LANES)] = out
            shard_in[:, pl.ds(spot_z, LANES)] = z
            shard_in[:, pl.ds(spot_x, LANES)] = x
            square += out * out + z * z + x * x
            scaled += weight[:, pl.ds(spot_z, LANES)].astype(BF).astype(F32) * z
            scaled += weight[:, pl.ds(spot_x, LANES)].astype(BF).astype(F32) * x
        for at_lane in range(2 * STATE // LANES):
            lo = width + at_lane * LANES
            shared[at_lane] += backs[mask][:, lo : lo + LANES].astype(F32)
        steps = jnp.where(lane < hl, backs[mask][:, width + 2 * STATE :].astype(F32), 0.0)
        shared[-1] += pltpu.roll(steps, (rank ^ mask) * hl, 1)
    for at_lane, one in enumerate(shared):
        lo = 2 * INNER + at_lane * LANES
        wide = min(LANES, weight.shape[1] - lo)
        one = one[:, :wide]
        shard_in[:, lo : lo + wide] = one
        square += jnp.concatenate([one * one, jnp.zeros((rows, LANES - wide), F32)], axis=1) if wide < LANES else one * one
        part = weight[:, lo : lo + wide].astype(BF).astype(F32) * one
        scaled += jnp.concatenate([part, jnp.zeros((rows, LANES - wide), F32)], axis=1) if wide < LANES else part
    d_gain = jnp.sum(scaled, axis=1, keepdims=True) / gain[:, 0:1]
    start = own * rows
    line = jnp.sum(jnp.where(lane == start % LANES + iota2((rows, LANES), 0), d_gain, 0.0), axis=0, keepdims=True)
    total = jnp.sum(jnp.sum(square, axis=0, keepdims=True), axis=1, keepdims=True)
    row, col = iota2(last.shape, 0), iota2(last.shape, 1)
    last[...] = jnp.where(row == start // LANES, line, 0.0) + jnp.where((row == D // LANES) & (col == 0), total, 0.0)


def shards(spot, fronts, backs, weight, gain, hl):
    rows = weight.shape[0]
    return pl.pallas_call(
        functools.partial(shard_kernel, n=len(fronts), hl=hl),
        grid_spec=pltpu.PrefetchScalarGridSpec(
            num_scalar_prefetch=1,
            grid=(1,),
            in_specs=[pl.BlockSpec(one.shape, lambda i, spot: (0, 0)) for one in (*fronts, *backs, weight, gain)],
            out_specs=[
                pl.BlockSpec(weight.shape, lambda i, spot: (0, 0)),
                pl.BlockSpec((rows, INNER), lambda i, spot: (0, 0)),
                pl.BlockSpec((D // LANES + 8, LANES), lambda i, spot: (0, 0)),
            ],
        ),
        out_shape=[
            jax.ShapeDtypeStruct(weight.shape, F32),
            jax.ShapeDtypeStruct((rows, INNER), F32),
            jax.ShapeDtypeStruct((D // LANES + 8, LANES), F32),
        ],
        **arbitrary("shards"),
    )(spot, *fronts, *backs, weight, gain)


def small_kernel(conv_0, conv_1, vec_0, vec_1, skip_0, skip_1, gain, out):
    width = gain.shape[1]
    out[...] = jnp.zeros(out.shape, F32)
    for tap in range(CONV + 1):
        rows = slice(tap * 8, tap * 8 + 8)
        out[tap : tap + 1, :] = jnp.sum(conv_0[rows, :] + conv_1[rows, :], axis=0, keepdims=True)
    out[5:6, :width] = jnp.sum(gain[...], axis=0, keepdims=True)
    out[6:7, :width] = jnp.sum(skip_0[...] + skip_1[...], axis=0, keepdims=True)
    vec = vec_0[...] + vec_1[...]
    head, lane = iota2((SLOT, LANES), 0), iota2((SLOT, LANES), 1)
    line = jnp.where(lane == head, vec[:, 0:1], jnp.where(lane == SLOT + head, vec[:, 1:2], 0.0))
    out[7:8, :LANES] = jnp.sum(line, axis=0, keepdims=True)


def small_gradients(*parts):
    return pl.pallas_call(
        small_kernel,
        out_shape=jax.ShapeDtypeStruct((8, parts[0].shape[1]), F32),
        name="small_gradients",
    )(*parts)


def place_kernel(spot, *refs, width):
    *pieces, out = refs
    shared = 0.0
    for mask, piece in enumerate(pieces):
        at = (spot[0] ^ mask) * width
        for lo in range(0, width, LANES):
            out[:, pl.ds(pl.multiple_of(at + lo, LANES), LANES)] = piece[:, lo : lo + LANES]
        shared = shared + piece[:, width:]
    out[:, INNER:] = shared


def place_small(spot, pieces, width):
    return pl.pallas_call(
        functools.partial(place_kernel, width=width),
        grid_spec=pltpu.PrefetchScalarGridSpec(
            num_scalar_prefetch=1,
            grid=(1,),
            in_specs=[pl.BlockSpec(one.shape, lambda i, spot: (0, 0)) for one in pieces],
            out_specs=pl.BlockSpec((8, CH), lambda i, spot: (0, 0)),
        ),
        out_shape=jax.ShapeDtypeStruct((8, CH), F32),
        **arbitrary("place_small"),
    )(spot, *pieces)

def swapped(value, axis, mask):
    return lax.ppermute(value, axis, [(i, i ^ mask) for i in range(lax.axis_size(axis))])


def axis_bits(axis):
    return [1 << i for i in range(lax.axis_size(axis).bit_length() - 1)]


def micro_order(micro, axis):
    bits = axis_bits(axis)
    return bits if micro % 2 == 0 else bits[::-1]


def nothing(*refs):
    pass


def after(values, *done):
    values = list(values)
    anywhere = pl.BlockSpec(memory_space=pl.ANY)
    held = pl.pallas_call(
        nothing,
        in_specs=[anywhere] * (len(values) + len(done)),
        out_specs=[anywhere] * len(values),
        out_shape=[jax.ShapeDtypeStruct(v.shape, v.dtype) for v in values],
        input_output_aliases={at: at for at in range(len(values))},
        name="after",
    )(*values, *done)
    return list(held)


def gather_stages(own):
    held = [{0: own[micro]} for micro in range(MICRO)]
    for turn in range(len(axis_bits("seq"))):
        got = []
        for micro in range(MICRO):
            bit = micro_order(micro, "seq")[turn]
            got.append({at ^ bit: swapped(held[micro][at], "seq", bit) for at in held[micro]})
        wait = yield [piece for one in got for piece in one.values()], [piece for one in held for piece in one.values()]
        for micro in range(MICRO):
            if wait is not None:
                got[micro] = dict(zip(got[micro], after(got[micro].values(), *wait)))
            held[micro].update(got[micro])
    yield [held[micro][at] for micro in range(MICRO) for at in range(len(held[micro]))]


def scatter_stages(parts):
    n = 2 * parts[0].shape[1]
    away, stay = list(parts[0::2]), list(parts[1::2])
    places = [[at for at in range(n) if not at & micro_order(half, "seq")[0]] for half in range(2)]
    join = lambda one, more: (one.astype(F32) + more.astype(F32)).astype(BF)
    pick = lambda a, at: jnp.concatenate([a[:, k : k + 1] for k in at], axis=1)
    turns = len(axis_bits("seq"))
    for turn in range(turns):
        got = [swapped(away[half], "seq", micro_order(half, "seq")[turn]) for half in range(2)]
        wait = yield got, away
        if wait is not None:
            got = after(got, *wait)
        if turn == turns - 1:
            break
        held, away, stay = stay, [], []
        for half in range(2):
            bit = micro_order(half, "seq")[turn + 1]
            leave = [at for at, place in enumerate(places[half]) if place & bit]
            keep = [at for at, place in enumerate(places[half]) if not place & bit]
            away.append(join(pick(held[half], leave), pick(got[half], leave)))
            stay.append(join(pick(held[half], keep), pick(got[half], keep)))
            places[half] = [places[half][at] for at in keep]
    yield jnp.concatenate([join(one, more)[:, 0] for one, more in zip(stay, got)], axis=1), None


def finish(stages, wait=None):
    last = None
    try:
        while True:
            last = stages.send(wait)
    except StopIteration:
        return last[0]


def turned(entries, rank):
    entries = list(entries)
    for bit in axis_bits("seq"):
        flip = (rank & bit) != 0
        entries = [jnp.where(flip, entries[at ^ bit], entries[at]) for at in range(len(entries))]
    return entries


def exchange(entries, rank):
    entries = turned(entries, rank)
    return entries, [swapped(one, "seq", mask) for mask, one in enumerate(entries) if mask]


def sum_pieces(value):
    n = value.shape[-2]
    total = value
    for mask in range(1, n):
        got = swapped(value, "seq", mask)
        total = total + jnp.concatenate([got[..., at ^ mask : (at ^ mask) + 1, :] for at in range(n)], axis=-2)
    return total


def adamw(master, gradient, first, second, clip, decay):
    clipped = gradient * clip
    first_new = BETA_ONE * first + (1.0 - BETA_ONE) * clipped
    second_new = BETA_TWO * second + (1.0 - BETA_TWO) * clipped * clipped
    update = first_new / FIX_ONE / (jnp.sqrt(second_new / FIX_TWO) + ADAM_EPS) + decay * master
    return (-LEARN_RATE * update, first_new, second_new)


def per_device(tokens, cotangent, segments, in_weight, in_m, in_v, conv_weight, conv_m, conv_v,
               out_weight, out_m, out_v, packed, packed_m, packed_v):
    n = lax.axis_size("seq")
    rank = lax.axis_index("seq")
    own = lax.axis_index("dp") * n + rank
    place = rank.astype(jnp.int32).reshape(1)
    ndev = n * lax.axis_size("dp")
    hl = HEADS // n
    xw = hl * HEADDIM
    rows = D // ndev
    piece = tokens.shape[1]
    count = MICRO * n * piece
    xs = INNER + INNER
    bc = 2 * STATE
    xc = xw + bc + LANES
    cw = conv_weight.shape[1]
    conv_cols = -(-(CONV + 1) * cw // rows)

    in_low = in_weight.astype(BF)
    out_low = out_weight.astype(BF).T
    conv_flat = conv_weight.astype(BF).reshape(-1)
    conv_flat = jnp.pad(conv_flat, (0, conv_cols * rows - conv_flat.shape[0])).reshape(rows, conv_cols)
    column = lambda a, q, width: a[:, q * width : (q + 1) * width]
    pad = jnp.zeros((rows, LANES - hl - conv_cols), BF)
    send_x = [
        jnp.concatenate(
            [column(in_low[:, INNER:xs], q, xw), in_low[:, xs : xs + bc], column(in_low[:, xs + bc :], q, hl), conv_flat, pad], axis=1
        )
        for q in range(n)
    ]
    gain_in = packed[3 * HEADS : 3 * HEADS + D]
    send_x = turned(send_x, rank)
    got_wx = [one if not mask else swapped(one, "seq", mask) for mask, one in enumerate(send_x)]
    a_log = lax.dynamic_slice_in_dim(packed, rank * hl, hl)
    skip = lax.dynamic_slice_in_dim(packed, HEADS + rank * hl, hl)
    dt_bias = lax.dynamic_slice_in_dim(packed, 2 * HEADS + rank * hl, hl)
    gain_out = lax.dynamic_slice_in_dim(packed, 3 * HEADS + D + rank * xw, xw)
    aux, masks = segment_aux(segments)
    heads = head_columns(a_log, dt_bias)
    skip = jnp.broadcast_to(jnp.repeat(skip, HEADDIM)[None], (8, xw))

    tok = tokens.astype(F32)
    r_in = lax.rsqrt(jnp.mean(tok * tok, axis=-1, keepdims=True) + NORM_EPS)
    hidden_stages = gather_stages((tok * r_in * gain_in).astype(BF))
    arrived, sent = next(hidden_stages)
    more, _ = hidden_stages.send(None)
    got_wx = jnp.concatenate(turned(got_wx[:1] + after(got_wx[1:], *sent), rank), axis=0)
    w_x = lax.all_gather(got_wx, "dp", axis=0, tiled=True)
    send_zo = jnp.stack(turned([jnp.concatenate([column(in_low, q, xw), column(out_low, q, xw)], axis=1) for q in range(n)], rank))
    [send_zo] = after([send_zo], got_wx, more[0], more[2])
    got_wzo = [send_zo[mask] if not mask else swapped(send_zo[mask], "seq", mask) for mask in range(n)]
    got_wzo = jnp.concatenate(turned(got_wzo, rank), axis=0)
    w_z = lax.all_gather(got_wzo[:, :xw], "dp", axis=0, tiled=True)
    w_o = lax.all_gather(got_wzo[:, xw:], "dp", axis=0, tiled=True)
    conv_full = w_x[:, xw + bc + hl : xw + bc + hl + conv_cols].reshape(ndev, rows * conv_cols)[:, : (CONV + 1) * cw]
    conv_full = conv_full.reshape(ndev, CONV + 1, cw).transpose(1, 0, 2).reshape(CONV + 1, CH)
    conv_loc = jnp.concatenate([lax.dynamic_slice_in_dim(conv_full, rank * xw, xw, 1), conv_full[:, INNER:]], axis=1).astype(F32)
    conv_loc = jnp.pad(conv_loc, ((0, 8 - CONV - 1), (0, 0)))

    for _ in axis_bits("seq")[1:]:
        arrived, more = more, hidden_stages.send(None)
        more = more[0] if isinstance(more, tuple) else more
    late = [micro * n + at for micro in range(MICRO) for at in range(n) if at & (last := micro_order(micro, "seq")[-1]) and at != last]
    soon = [at for at in range(MICRO * n) if at not in late]
    soon.sort(key=lambda at: (at % n).bit_count())
    earlier = in_project([more[at] for at in soon], soon, MICRO * n, w_x, done=(aux, masks, conv_loc))
    late_pieces = after([more[at] for at in late], earlier[0])
    proj_x, hidden = in_project(late_pieces, late, MICRO * n, w_x, earlier)

    cot_stages = gather_stages(after([cotangent[micro] for micro in range(MICRO)], *late_pieces))
    next(cot_stages)
    y, states, act, slope = scan_forward(place, proj_x, conv_loc, skip, heads, aux, masks, hl)
    for bit in axis_bits("seq"):
        cot = cot_stages.send([proj_x] if bit == 1 else [y])
    gain = jnp.broadcast_to(gain_out[None], (8, xw))
    [w_z] = after([w_z], y)
    z = dot(hidden, w_z, NN).astype(BF)
    dn, cot, sums = gate_forward(cot, z, w_o, y, gain)
    sums = sum_pieces(sums.reshape(MICRO, n, 8 * BLOCK)).reshape(-1, BLOCK)
    first_bits = tuple(micro_order(half, "seq")[0] for half in range(2))
    normed, dy, dz, d_gain_out, *out_part = out_project(z, dn, y, sums, gain, w_o, first_bits)

    scatter = lambda a: lax.psum_scatter(a, "dp", scatter_dimension=0, tiled=True)
    split = lambda a: [a[q * rows : (q + 1) * rows] for q in range(n)]
    out_stages = scatter_stages(out_part)
    next(out_stages)
    part_o = dot(cot, normed, TN).astype(BF)
    part_z = dot(hidden, dz, TN).astype(BF)
    got_o, got_z = scatter(part_o), scatter(part_z)

    through_in = lambda micro, one: back_project(micro, dz, one, w_z, w_x, first_bits)
    scan_back = lambda micro, *done: scan_backward(
        place, micro, proj_x, conv_loc, skip, heads, aux, masks, act, slope, dy, states, hl, *done
    )

    px_0, conv_0, vec_0, skip_0 = scan_back(0, part_o, part_z)
    hid_0 = through_in(0, px_0)
    out_got, out_sent = out_stages.send([hid_0[0]])
    stages_0 = scatter_stages(hid_0)
    hid_got, sent = next(stages_0)
    px_1, conv_1, vec_1, skip_1 = scan_back(1, *sent, *out_sent)
    [px_1] = after([px_1], *hid_got, *out_got)
    part_x = dot(hidden, jnp.concatenate([px_0, px_1], axis=0), TN).astype(BF)
    got_x = scatter(part_x)
    hid_got, sent = stages_0.send([part_x])
    spot = jnp.stack([rank, own]).astype(jnp.int32)
    own_gain = lax.dynamic_slice_in_dim(gain_in, own * rows, rows)[:, None]
    first_bit, *more_bits = axis_bits("dp")
    small = small_gradients(conv_0, conv_1, vec_0, vec_1, skip_0, skip_1, d_gain_out)
    small = small + swapped(small, "dp", first_bit)
    [px_1] = after([px_1], part_x, *sent, small)
    hid_1 = through_in(1, px_1)
    [got_o, got_z] = after([got_o, got_z], part_x)
    sent_oz, got_oz = exchange(split(jnp.concatenate([got_o, got_z], axis=1)), rank)
    [small] = after([small], hid_1[0], *got_oz)
    for bit in more_bits:
        small = small + swapped(small, "dp", bit)
    small = [small] + [swapped(small, "seq", mask) for mask in range(1, n)]
    hid_1 = after(hid_1, *hid_got, *small[1:])
    stages_1 = scatter_stages(hid_1)
    hid_got, hid_sent = next(stages_1)
    small = place_small(spot, small, xw)
    conv_tot, gain_out_tot = small[: CONV + 1], small[5, :INNER]
    skip_tot = jnp.sum(small[6, :INNER].reshape(HEADS, HEADDIM), axis=1)
    by_head = small[7, :INNER].reshape(n, xw)
    a_log_tot, dt_bias_tot = by_head[:, :hl].reshape(-1), by_head[:, SLOT : SLOT + hl].reshape(-1)
    shard_conv = lax.dynamic_slice_in_dim(conv_tot, own * cw, cw, 1)
    conv_sq = jnp.sum(conv_tot * conv_tot)

    [got_x] = after([got_x], small)
    sent_x, got_x = exchange(split(got_x), rank)
    shard_in, shard_out, last = shards(spot, sent_oz[:1] + got_oz, sent_x[:1] + got_x, in_weight, own_gain, hl)
    shard_out = shard_out.T
    output = (tok + finish(out_stages, [small]).astype(F32)).astype(BF)
    d_hidden = jnp.concatenate([finish(stages_0, [hid_1[0]]), finish(stages_1, got_x)], axis=0).astype(F32)
    dh = d_hidden * gain_in
    d_tok = r_in * (dh - tok * (r_in * r_in) * jnp.mean(dh * tok, axis=-1, keepdims=True))
    input_grad = (cotangent.astype(F32) + d_tok).astype(BF)

    stages = [(axis, bit) for axis in ("dp", "seq") for bit in axis_bits(axis)]
    for axis, bit in stages[:-1]:
        last = last + swapped(last, axis, bit)
    [last] = after([last], input_grad)
    last = last + swapped(last, *stages[-1])
    vec_tot = jnp.concatenate([a_log_tot, skip_tot, dt_bias_tot, last[: D // LANES].reshape(-1), gain_out_tot])
    grad_norm = jnp.sqrt(last[D // LANES, 0] + conv_sq + jnp.sum(vec_tot * vec_tot))
    clip = jnp.minimum(1.0, CLIP_NORM / (grad_norm + 1e-06))
    in_new = adamw(in_weight, shard_in, in_m, in_v, clip, WEIGHT_DECAY)
    conv_new = adamw(conv_weight, shard_conv, conv_m, conv_v, clip, WEIGHT_DECAY)
    out_new = adamw(out_weight, shard_out, out_m, out_v, clip, WEIGHT_DECAY)
    vec_new = adamw(packed, vec_tot, packed_m, packed_v, clip, 0.0)
    return (
        output, input_grad, grad_norm,
        in_weight + in_new[0], in_new[1], in_new[2],
        conv_new[0], conv_new[1], conv_new[2],
        out_weight + out_new[0], out_new[1], out_new[2],
        vec_new[0], vec_new[1], vec_new[2],
    )


def solution(mesh):
    tok, col, row = P(None, ALL, None), P(None, ALL), P(ALL, None)
    return jax.shard_map(
        per_device,
        mesh=mesh,
        in_specs=(tok, tok, P(None, "dp"), row, row, row, col, col, col, col, col, col, P(), P(), P()),
        out_specs=(tok, tok, P(), row, row, row, col, col, col, col, col, col, P(), P(), P()),
        check_vma=False,
    )
```

```python
import functools

import jax
import jax.numpy as jnp
from jax import lax
from jax.experimental import pallas as pl
from jax.experimental.pallas import tpu as pltpu
from jax.sharding import PartitionSpec as P

D = 2048
HEADS = 64
HEADDIM = 64
STATE = 128
CONV = 4
BLOCK = 256
MICRO = 2
INNER = 4096
CH = 4352
NORM_EPS = 1e-05
LEARN_RATE = 0.004
BETA_ONE = 0.9
BETA_TWO = 0.95
FIX_ONE = 1.0 - 0.9**10
FIX_TWO = 1.0 - 0.95**10
ADAM_EPS = 1e-08
WEIGHT_DECAY = 0.1
CLIP_NORM = 1.0
BF = jnp.bfloat16
F32 = jnp.float32
ALL = ("dp", "seq")


def dot(a, b, dims, out=F32):
    return lax.dot_general(a, b, (dims, ((), ())), preferred_element_type=out)


NN = ((1,), (0,))
NT = ((1,), (1,))
TN = ((0,), (0,))
LANES = 128
PAIR = 2 * HEADDIM
VMEM = 56 * 1024 * 1024
SLOT = 16
TINY = 1e-37
CAP = 85.0


def iota2(shape, dim):
    return lax.broadcasted_iota(jnp.int32, shape, dim)


def tree(value, rows=8):
    while value.shape[0] > rows:
        half = value.shape[0] // 2
        value = value[:half] + value[half:]
    return value


def thirds(value):
    high = value.astype(BF).astype(F32)
    rest = value - high
    mid = rest.astype(BF).astype(F32)
    return high, mid, (rest - mid).astype(BF).astype(F32)


def running_sum(values, reverse):
    row, col = iota2((BLOCK, BLOCK), 0), iota2((BLOCK, BLOCK), 1)
    ones = jnp.where(row >= col if reverse else row <= col, 1.0, 0.0).astype(BF)
    sums = dot(jnp.concatenate(thirds(values), axis=0).astype(BF), ones, NN)
    return sums[:SLOT] + sums[SLOT : 2 * SLOT] + sums[2 * SLOT :]


def step_rows(raw, heads, masks):
    lifted = raw.astype(F32).T[:SLOT] + heads[:, 0:1]
    dt = jnp.maximum(lifted, 0.0) + jnp.log1p(jnp.exp(-jnp.abs(lifted)))
    cum = running_sum(dt * heads[:, 1:2], False)
    entry = jnp.exp(cum) * masks[1:2, :]
    dt_end = dt * jnp.exp(cum[:, BLOCK - 1 : BLOCK] - cum) * masks[2:3, :]
    return lifted, dt, cum, entry, dt_end


def two(value):
    high = value.astype(BF).astype(F32)
    return [high, value - high]


def as_columns(gap_rows, entry, dt_end):
    ones = jnp.where(iota2((SLOT, BLOCK), 0) < 3, 1.0, 0.0)
    return jnp.concatenate([*thirds(gap_rows), ones, *two(entry), *two(dt_end)], axis=0).T.astype(BF)


def gap_right_init(right, hl):
    row = iota2((3 * SLOT, BLOCK), 0)
    for h in range(hl):
        right[0 : 3 * SLOT, h * BLOCK : (h + 1) * BLOCK] = jnp.where((row & (SLOT - 1)) == h, 1.0, 0.0).astype(BF)


def gap_right_fill(right, values, hl):
    row = iota2((SLOT, BLOCK), 0)
    high, mid, low = thirds(values)
    for h in range(hl):
        one = slice(h, h + 1)
        slab = jnp.where(row == 0, high[one], jnp.where(row == 1, mid[one], jnp.where(row == 2, low[one], 0.0)))
        right[3 * SLOT :, h * BLOCK : (h + 1) * BLOCK] = slab.astype(BF)


def head_spread_init(spreads, hl):
    row, col = iota2(spreads.shape, 0), iota2(spreads.shape, 1)
    head = jnp.where(col < hl * HEADDIM, col, col - hl * HEADDIM) // HEADDIM
    slot = jnp.where(col < hl * HEADDIM, 2, 3)
    spreads[...] = jnp.where(((row & (SLOT - 1)) == head) & (row // (2 * SLOT) == slot), 1.0, 0.0).astype(BF)


def stacked(left, pair_values):
    zero = jnp.zeros_like(pair_values)
    return jnp.concatenate([jnp.where(left, pair_values, zero), jnp.where(left, zero, pair_values)], axis=0)


def conv_chunk(window, conv_w, valid, lo, hi):
    out = conv_w[CONV : CONV + 1, lo:hi] + conv_w[CONV - 1 : CONV, lo:hi] * window[8 : 8 + BLOCK, lo:hi]
    for tap in range(CONV - 1):
        out += conv_w[tap : tap + 1, lo:hi] * (window[5 + tap : 5 + tap + BLOCK, lo:hi] * valid[tap])
    return out


def spread(aux_v, at):
    return jnp.broadcast_to(aux_v[:, at : at + 1], (BLOCK, LANES))


def forward_kernel(place, proj, conv_w, skip, heads, aux, masks, y_out, s_out, act, slope, window, state, right, carried, spreads, *, hl):
    width = hl * HEADDIM
    conv_width = width + 2 * STATE

    @pl.when(pl.program_id(1) == 0)
    def _():
        window[0:8, :] = jnp.zeros((8, conv_width), F32)
        state[...] = jnp.zeros(state.shape, F32)
        gap_right_init(right, hl)
        head_spread_init(spreads, hl)

    aux_v = aux[...]
    valid = [spread(aux_v, tap) for tap in range(CONV - 1)]
    for lo in range(0, conv_width, LANES):
        hi = lo + LANES
        window[8 : 8 + BLOCK, lo:hi] = proj[:, lo:hi].astype(F32)
        out = conv_chunk(window, conv_w, valid, lo, hi)
        sig = jax.nn.sigmoid(out)
        silu = out * sig
        act[:, lo:hi] = silu.astype(BF)
        slope[:, lo:hi] = (sig + silu * (1.0 - sig)).astype(BF)
    window[0:8, :] = window[BLOCK : BLOCK + 8, :]

    _, dt, cum, entry, dt_end = step_rows(proj[:, conv_width : conv_width + LANES], heads[...], masks)
    columns = as_columns(cum, entry, dt_end)
    gaps = columns[:, : 4 * SLOT]
    gap_right_fill(right, jnp.log(jnp.maximum(dt, TINY)) - cum, hl)
    bm, cm = act[:, width : width + STATE], act[:, width + STATE :]
    same = (aux_v[:, 3:4] == masks[0:1, :]) & (iota2((BLOCK, BLOCK), 0) >= iota2((BLOCK, BLOCK), 1))
    inner = jnp.where(same, dot(cm, bm, NT), 0.0)
    left = iota2((BLOCK, PAIR), 1) < HEADDIM
    top = iota2((PAIR, STATE), 0) < HEADDIM
    last = entry[:, BLOCK - 1 : BLOCK]
    s_out[0] = state[...].astype(BF)
    carried[...] = dot(columns, spreads[...], NN)
    carried[:, :width] = carried[:, :width] * dot(cm, s_out[0], NT)
    for pair in range(hl // 2):
        first = 2 * pair
        lo, hi = pair * PAIR, (pair + 1) * PAIR
        xp = act[:, lo:hi]
        mix = []
        for h in (first, first + 1):
            decay = jnp.exp(jnp.minimum(dot(gaps, right[:, h * BLOCK : (h + 1) * BLOCK], NN), CAP))
            mix.append((inner * decay).astype(BF))
        xf = xp.astype(F32)
        y = dot(jnp.concatenate(mix, axis=1), stacked(left, xp), NN)
        y += carried[:, lo:hi] + skip[0:1, lo:hi] * xf
        y_out[:, lo:hi] = y.astype(BF)
        weighted = (xf * carried[:, width + lo : width + hi]).astype(BF)
        keep = jnp.where(top, last[first : first + 1], last[first + 1 : first + 2])
        state[lo:hi, :] = keep * state[lo:hi, :] + dot(weighted, bm, TN)


def backward_kernel(place, proj, conv_w, skip, heads, aux, masks, act, slope, dy, s_in, *refs, hl):
    dproj, dco, dvec, dskip, dwin, grad_s, dcb, colsum, dkeep, right, carried, later_w, spreads, picks, sums, used, into = refs[-17:]
    width = hl * HEADDIM
    conv_width = width + 2 * STATE

    @pl.when(pl.program_id(0) == 0)
    def _():
        dvec[...] = jnp.zeros(dvec.shape, F32)
        dskip[...] = jnp.zeros(dskip.shape, F32)
        dwin[BLOCK : BLOCK + 8, :] = jnp.zeros((8, conv_width), F32)
        grad_s[...] = jnp.zeros(grad_s.shape, F32)
        colsum[...] = jnp.zeros(colsum.shape, F32)
        dkeep[...] = jnp.zeros(dkeep.shape, F32)
        gap_right_init(right, hl)
        head_spread_init(spreads, hl)
        picks[...] = jnp.where(iota2(picks.shape, 0) == iota2(picks.shape, 1) // BLOCK, 1.0, 0.0).astype(BF)
        sums[...] = jnp.where(iota2(sums.shape, 0) == iota2(sums.shape, 1) // HEADDIM, 1.0, 0.0).astype(BF)

    aux_v = aux[...]
    lifted, dt, cum, entry, dt_end = step_rows(proj[:, conv_width : conv_width + LANES], heads[...], masks)
    a_neg = heads[:, 1:2]
    columns = as_columns(jnp.log(jnp.maximum(dt, TINY)) - cum, entry, dt_end)
    gaps = columns[:, : 4 * SLOT]
    gap_right_fill(right, cum, hl)
    bm, cm = act[:, width : width + STATE], act[:, width + STATE :]
    same = (aux_v[:, 3:4] == masks[0:1, :]) & (iota2((BLOCK, BLOCK), 0) <= iota2((BLOCK, BLOCK), 1))
    inner = jnp.where(same, dot(bm, cm, NT), 0.0)
    left = iota2((BLOCK, PAIR), 1) < HEADDIM
    top = iota2((PAIR, STATE), 0) < HEADDIM
    last = entry[:, BLOCK - 1 : BLOCK]
    d_row = jnp.zeros((SLOT, BLOCK), F32)
    d_b = jnp.zeros((BLOCK, STATE), F32)
    d_c = jnp.zeros((BLOCK, STATE), F32)
    spreaded = dot(columns, spreads[...], NN)
    carried[...] = spreaded
    later_w[:, :width] = dot(cm, s_in[0], NT)
    later_w[:, width:] = dot(bm, grad_s[...].astype(BF), NT)

    for pair in range(hl // 2):
        first = 2 * pair
        lo, hi = pair * PAIR, (pair + 1) * PAIR
        xp, dyp = act[:, lo:hi], dy[:, lo:hi]
        xf, dyf = xp.astype(F32), dyp.astype(F32)
        d_mix = dot(stacked(left, xp), dyp, NT)
        mix, pairwise = [], []
        d_inner = 0.0
        for at, h in enumerate((first, first + 1)):
            decay = jnp.exp(jnp.minimum(dot(gaps, right[:, h * BLOCK : (h + 1) * BLOCK], NN), CAP))
            mix.append((inner * decay).astype(BF))
            part = d_mix[at * BLOCK : (at + 1) * BLOCK] * decay
            d_inner += part
            part = (part * inner).astype(BF)
            pairwise.append(part)
            colsum[h : h + 1, :] = jnp.sum(tree(part.astype(F32)), axis=0, keepdims=True)
        d_row += dot(picks[:, first * BLOCK : (first + 2) * BLOCK], jnp.concatenate(pairwise, axis=1), NT)
        if pair == 0:
            dcb[...] = d_inner
        else:
            dcb[...] += d_inner
        later = grad_s[lo:hi, :]
        low = s_in[0, lo:hi, :]
        end_p = carried[:, width + lo : width + hi]
        from_end = later_w[:, width + lo : width + hi] * end_p
        dx = dot(jnp.concatenate(mix, axis=1), stacked(left, dyp), NN) + from_end + skip[0:1, lo:hi] * dyf
        dwin[0:BLOCK, lo:hi] = slope[:, lo:hi].astype(F32) * dx
        used[:, lo:hi] = (from_end * xf).astype(BF)
        entering = carried[:, lo:hi] * dyf
        into[:, lo:hi] = (entering * later_w[:, lo:hi]).astype(BF)
        entering = entering.astype(BF)
        dskip[:, lo:hi] += tree(xf * dyf)
        kept = later * low.astype(F32)
        dkeep[first : first + 1, :] = jnp.sum(tree(kept[:HEADDIM]), axis=0, keepdims=True)
        dkeep[first + 1 : first + 2, :] = jnp.sum(tree(kept[HEADDIM:]), axis=0, keepdims=True)
        weighted = (xf * end_p).astype(BF)
        d_b += dot(weighted, later.astype(BF), NN)
        d_c += dot(entering, low, NN)
        keep = jnp.where(top, last[first : first + 1], last[first + 1 : first + 2])
        grad_s[lo:hi, :] = dot(entering, cm, TN) + keep * later

    d_inner = jnp.where(same, dcb[...], 0.0).astype(BF)
    d_b += dot(d_inner, cm, NN)
    d_c += dot(d_inner, bm, TN)
    dwin[0:BLOCK, width : width + STATE] = slope[:, width : width + STATE].astype(F32) * d_b
    dwin[0:BLOCK, width + STATE :] = slope[:, width + STATE :].astype(F32) * d_c

    d_end = dot(sums[...], used[...], NT)
    through = d_row + d_end
    d_last = jnp.sum(d_end, axis=1, keepdims=True) + jnp.sum(dkeep[...], axis=1, keepdims=True) * last
    d_cum = dot(sums[...], into[...], NT) + colsum[...] - through
    d_cum += jnp.where(iota2((SLOT, BLOCK), 1) == BLOCK - 1, d_last, 0.0)
    d_a = running_sum(d_cum, True)
    sig = jax.nn.sigmoid(lifted)
    d_raw = through * jnp.where(dt > TINY, sig / jnp.maximum(dt, TINY), 1.0) + d_a * a_neg * sig
    d_raw = jnp.where(iota2((SLOT, BLOCK), 0) < hl, d_raw, 0.0)
    dproj[:, conv_width : conv_width + LANES] = jnp.concatenate([d_raw, jnp.zeros((LANES - SLOT, BLOCK), F32)], axis=0).T.astype(BF)
    lane = iota2((SLOT, LANES), 1)
    d_log = jnp.sum(d_a * dt, axis=1, keepdims=True) * a_neg
    dvec[...] += jnp.where(lane == 0, d_log, jnp.where(lane == 1, jnp.sum(d_raw, axis=1, keepdims=True), 0.0))

    valid = [spread(aux_v, 4 + tap) for tap in range(CONV - 1)]
    for lo in range(0, conv_width, LANES):
        hi = lo + LANES
        own = dwin[0:BLOCK, lo:hi]
        dco[:, lo:hi] = own.astype(BF)
        grad = conv_w[CONV - 1 : CONV, lo:hi] * own
        for tap in range(CONV - 1):
            ahead = CONV - 1 - tap
            grad += conv_w[tap : tap + 1, lo:hi] * (dwin[ahead : ahead + BLOCK, lo:hi] * valid[tap])
        dproj[:, lo:hi] = grad.astype(BF)
    dwin[BLOCK : BLOCK + 8, :] = dwin[0:8, :]


def taps_kernel(place, proj, aux, dco, dconv, dwin):
    conv_width = dco.shape[1]

    @pl.when(pl.program_id(0) == 0)
    def _():
        dconv[...] = jnp.zeros(dconv.shape, F32)
        dwin[BLOCK : BLOCK + 8, :] = jnp.zeros((8, conv_width), F32)

    aux_v = aux[...]
    valid = [spread(aux_v, 4 + tap) for tap in range(CONV - 1)]
    for lo in range(0, conv_width, LANES):
        hi = lo + LANES
        own = dco[:, lo:hi].astype(F32)
        dwin[0:BLOCK, lo:hi] = own
        value = proj[:, lo:hi].astype(F32)
        dconv[CONV * 8 : CONV * 8 + 8, lo:hi] += tree(own)
        dconv[(CONV - 1) * 8 : CONV * 8, lo:hi] += tree(own * value)
        for tap in range(CONV - 1):
            ahead = CONV - 1 - tap
            moved = dwin[ahead : ahead + BLOCK, lo:hi] * valid[tap]
            dconv[tap * 8 : tap * 8 + 8, lo:hi] += tree(moved * value)
    dwin[BLOCK : BLOCK + 8, :] = dwin[0:8, :]


def segment_aux(segments):
    micro, length = segments.shape
    nb = length // BLOCK
    seg = segments.astype(F32)
    blocks = seg.reshape(micro, nb, BLOCK)
    prev = jnp.concatenate([jnp.full((micro, 1), -1.0, F32), blocks[:, :-1, -1]], axis=1)
    reach = range(CONV - 1, 0, -1)
    earlier = [jnp.pad(seg, ((0, 0), (by, 0)), constant_values=-1.0)[:, :length] == seg for by in reach]
    later = [jnp.pad(seg, ((0, 0), (0, by)), constant_values=-1.0)[:, by:] == seg for by in reach]
    columns = [c.astype(F32) for c in (*earlier, seg, *later, jnp.zeros_like(seg))]
    aux = jnp.stack(columns, axis=-1).reshape(micro * length, 8)
    zero = jnp.zeros_like(blocks)
    masks = [blocks, blocks == prev[:, :, None], blocks == blocks[:, :, -1:]] + [zero] * 5
    return aux, jnp.stack([m.astype(F32) for m in masks], axis=2).reshape(micro * nb * 8, BLOCK)


def head_columns(a_log, dt_bias):
    hl = a_log.shape[0]
    both = jnp.stack([dt_bias, -jnp.exp(a_log)], axis=1)
    return jnp.pad(both, ((0, SLOT - hl), (0, LANES - 2)))


def scan_forward(place, proj, conv_w, skip, heads, aux, masks, hl):
    tokens = proj.shape[0]
    nb = tokens // MICRO // BLOCK
    width = hl * HEADDIM
    conv_width = width + 2 * STATE
    held = lambda m, j, place: (m * nb + (j ^ place[0]), 0)
    at = lambda m, j, place: (m * nb + j, 0)
    whole = lambda m, j, place: (0, 0)
    grid_spec = pltpu.PrefetchScalarGridSpec(
        num_scalar_prefetch=1,
        grid=(MICRO, nb),
        in_specs=[
            pl.BlockSpec((BLOCK, conv_width + LANES), held),
            pl.BlockSpec((8, conv_width), whole),
            pl.BlockSpec(skip.shape, whole),
            pl.BlockSpec(heads.shape, whole),
            pl.BlockSpec((BLOCK, 8), at),
            pl.BlockSpec((8, BLOCK), at),
        ],
        out_specs=[
            pl.BlockSpec((BLOCK, width), held),
            pl.BlockSpec((1, width, STATE), lambda m, j, place: (m * nb + j, 0, 0)),
            pl.BlockSpec((BLOCK, conv_width), held),
            pl.BlockSpec((BLOCK, conv_width), held),
        ],
        scratch_shapes=[
            pltpu.VMEM((BLOCK + 8, conv_width), F32),
            pltpu.VMEM((width, STATE), F32),
            pltpu.VMEM((4 * SLOT, hl * BLOCK), BF),
            pltpu.VMEM((BLOCK, 2 * width), F32),
            pltpu.VMEM((LANES, 2 * width), BF),
        ],
    )
    return pl.pallas_call(
        functools.partial(forward_kernel, hl=hl),
        grid_spec=grid_spec,
        out_shape=[
            jax.ShapeDtypeStruct((tokens, width), BF),
            jax.ShapeDtypeStruct((MICRO * nb, width, STATE), BF),
            jax.ShapeDtypeStruct((tokens, conv_width), BF),
            jax.ShapeDtypeStruct((tokens, conv_width), BF),
        ],
        compiler_params=pltpu.CompilerParams(vmem_limit_bytes=VMEM, dimension_semantics=("arbitrary", "arbitrary")),
        name="scan_forward",
    )(place, proj, conv_w, skip, heads, aux, masks)


def scan_backward(place, micro, proj, conv_w, skip, heads, aux, masks, act, slope, dy, states, hl, *done):
    tokens = proj.shape[0] // MICRO
    nb = tokens // BLOCK
    width = hl * HEADDIM
    conv_width = width + 2 * STATE
    full = conv_width + LANES
    first = micro * nb
    held = lambda j, place: (first + ((nb - 1 - j) ^ place[0]), 0)
    at = lambda j, place: (first + nb - 1 - j, 0)
    whole = lambda j, place: (0, 0)
    grid_spec = pltpu.PrefetchScalarGridSpec(
        num_scalar_prefetch=1,
        grid=(nb,),
        in_specs=[
            pl.BlockSpec((BLOCK, full), held),
            pl.BlockSpec((8, conv_width), whole),
            pl.BlockSpec(skip.shape, whole),
            pl.BlockSpec(heads.shape, whole),
            pl.BlockSpec((BLOCK, 8), at),
            pl.BlockSpec((8, BLOCK), at),
            pl.BlockSpec((BLOCK, conv_width), held),
            pl.BlockSpec((BLOCK, conv_width), held),
            pl.BlockSpec((BLOCK, width), held),
            pl.BlockSpec((1, width, STATE), lambda j, place: (first + nb - 1 - j, 0, 0)),
        ]
        + [pl.BlockSpec(memory_space=pl.ANY)] * len(done),
        out_specs=[
            pl.BlockSpec((BLOCK, full), lambda j, place: ((nb - 1 - j) ^ place[0], 0)),
            pl.BlockSpec((BLOCK, conv_width), lambda j, place: ((nb - 1 - j) ^ place[0], 0)),
            pl.BlockSpec((SLOT, LANES), whole),
            pl.BlockSpec((8, width), whole),
        ],
        scratch_shapes=[
            pltpu.VMEM((BLOCK + 8, conv_width), F32),
            pltpu.VMEM((width, STATE), F32),
            pltpu.VMEM((BLOCK, BLOCK), F32),
            pltpu.VMEM((SLOT, BLOCK), F32),
            pltpu.VMEM((SLOT, STATE), F32),
            pltpu.VMEM((4 * SLOT, hl * BLOCK), BF),
            pltpu.VMEM((BLOCK, 2 * width), F32),
            pltpu.VMEM((BLOCK, 2 * width), F32),
            pltpu.VMEM((LANES, 2 * width), BF),
            pltpu.VMEM((SLOT, hl * BLOCK), BF),
            pltpu.VMEM((SLOT, width), BF),
            pltpu.VMEM((BLOCK, width), BF),
            pltpu.VMEM((BLOCK, width), BF),
        ],
    )
    return pl.pallas_call(
        functools.partial(backward_kernel, hl=hl),
        grid_spec=grid_spec,
        out_shape=[
            jax.ShapeDtypeStruct((tokens, full), BF),
            jax.ShapeDtypeStruct((tokens, conv_width), BF),
            jax.ShapeDtypeStruct((SLOT, LANES), F32),
            jax.ShapeDtypeStruct((8, width), F32),
        ],
        compiler_params=pltpu.CompilerParams(vmem_limit_bytes=VMEM, dimension_semantics=("arbitrary",)),
        name="scan_backward",
    )(place, proj, conv_w, skip, heads, aux, masks, act, slope, dy, states, *done)


def tap_gradients(place, micro, proj, aux, dco):
    tokens, conv_width = dco.shape
    nb = tokens // BLOCK
    grid_spec = pltpu.PrefetchScalarGridSpec(
        num_scalar_prefetch=1,
        grid=(nb,),
        in_specs=[
            pl.BlockSpec((BLOCK, proj.shape[1]), lambda j, place: (micro * nb + ((nb - 1 - j) ^ place[0]), 0)),
            pl.BlockSpec((BLOCK, 8), lambda j, place: (micro * nb + nb - 1 - j, 0)),
            pl.BlockSpec((BLOCK, conv_width), lambda j, place: ((nb - 1 - j) ^ place[0], 0)),
        ],
        out_specs=pl.BlockSpec((8 * (CONV + 1), conv_width), lambda j, place: (0, 0)),
        scratch_shapes=[pltpu.VMEM((BLOCK + 8, conv_width), F32)],
    )
    return pl.pallas_call(
        taps_kernel,
        grid_spec=grid_spec,
        out_shape=jax.ShapeDtypeStruct((8 * (CONV + 1), conv_width), F32),
        compiler_params=pltpu.CompilerParams(vmem_limit_bytes=VMEM, dimension_semantics=("arbitrary",)),
        name="tap_gradients",
    )(place, proj, aux, dco)


def fetch(pieces, buffer, sems, step):
    @pl.when(step == 0)
    def _():
        pltpu.make_async_copy(pieces[0], buffer.at[0], sems.at[0]).start()

    for at in range(1, len(pieces)):

        @pl.when(step == at - 1)
        def _():
            pltpu.make_async_copy(pieces[at], buffer.at[at % 2], sems.at[at % 2]).start()

    slot = step % 2
    pltpu.make_async_copy(pieces[0], buffer.at[slot], sems.at[slot]).wait()
    return slot


def emit(value, targets, buffer, sems, micro, place, bits, step, steps):
    slot = step % 2
    rows = value.shape[0] // 2

    def waiting(at):
        for half in range(2):
            pltpu.make_async_copy(buffer.at[at, pl.ds(half * rows, rows)], targets[0].at[0, 0], sems.at[at, half]).wait()

    @pl.when(step >= 2)
    def _():
        waiting(slot)

    buffer[slot] = value
    for half, bit in enumerate(bits):
        index = place // (2 * bit) * bit + place % bit
        set_ = (place // bit) % 2
        for target, wanted in ((targets[2 * half], 1), (targets[2 * half + 1], 0)):

            @pl.when(set_ == wanted)
            def _():
                pltpu.make_async_copy(
                    buffer.at[slot, pl.ds(half * rows, rows)], target.at[micro, index], sems.at[slot, half]
                ).start()

    @pl.when(step == steps - 1)
    def _():
        waiting(0)
        waiting(1)


def emitted(some, n, depth):
    shapes = [jax.ShapeDtypeStruct((some, n // 2, BLOCK // 2, depth), BF)] * 4
    return shapes, [pl.BlockSpec(memory_space=pl.ANY)] * 4, [pltpu.VMEM((2, BLOCK, depth), BF), pltpu.SemaphoreType.DMA((2, 2))]


def fixed(array):
    return pl.BlockSpec(array.shape, lambda i: (0, 0), pipeline_mode=pl.Buffered(1))


def by_rows(width):
    return pl.BlockSpec((BLOCK, width), lambda i: (i, 0))


def arbitrary(name):
    return dict(compiler_params=pltpu.CompilerParams(vmem_limit_bytes=VMEM, dimension_semantics=("arbitrary",)), name=name)


def in_kernel(*refs, count):
    pieces, w, (proj, hidden, buffer, sems) = refs[1 : count + 1], refs[count + 1], refs[-4:]
    slot = fetch(pieces, buffer, sems, pl.program_id(0))
    value = buffer[slot]
    hidden[...] = value
    proj[...] = dot(value, w[...], NN).astype(BF)


def in_project(pieces, places, total, w, earlier=(), done=()):
    count = len(pieces)
    depth, width = w.shape
    anywhere = [pl.BlockSpec(memory_space=pl.ANY)]
    at = lambda i, table: (table[i], 0)
    return pl.pallas_call(
        functools.partial(in_kernel, count=count),
        grid_spec=pltpu.PrefetchScalarGridSpec(
            num_scalar_prefetch=1,
            grid=(count,),
            in_specs=anywhere * count
            + [pl.BlockSpec(w.shape, lambda i, table: (0, 0), pipeline_mode=pl.Buffered(1))]
            + anywhere * (len(earlier) + len(done)),
            out_specs=[pl.BlockSpec((BLOCK, width), at), pl.BlockSpec((BLOCK, depth), at)],
            scratch_shapes=[pltpu.VMEM((2, BLOCK, depth), BF), pltpu.SemaphoreType.DMA((2,))],
        ),
        out_shape=[
            jax.ShapeDtypeStruct((total * BLOCK, width), BF),
            jax.ShapeDtypeStruct((total * BLOCK, depth), BF),
        ],
        input_output_aliases={count + 2 + i: i for i in range(len(earlier))},
        **arbitrary("in_project"),
    )(jnp.array(places, jnp.int32), *pieces, w, *earlier, *done)


def gate_kernel(*refs, count):
    pieces, (z, w_o, y, gain, dn_out, cot_out, sums, buffer, sems) = refs[:count], refs[count:]
    slot = fetch(pieces, buffer, sems, pl.program_id(0))
    cot = buffer[slot]
    cot_out[...] = cot
    dn = dot(cot, w_o[...], NN)
    dn_out[...] = dn.astype(BF)
    zf = z[...].astype(F32)
    gz = y[...].astype(F32) * (zf * jax.nn.sigmoid(zf))
    ones = jnp.ones((8, gz.shape[1]), BF)
    first = dot(ones, (gz * gz).astype(BF), NT)
    second = dot(ones, (dn * gain[0:1, :] * gz).astype(BF), NT)
    sums[...] = jnp.where(iota2((8, BLOCK), 0) == 0, first, second)


def gate_forward(pieces, z, w_o, y, gain):
    count = len(pieces)
    depth, width = w_o.shape
    return pl.pallas_call(
        functools.partial(gate_kernel, count=count),
        grid=(count,),
        in_specs=[pl.BlockSpec(memory_space=pl.ANY)] * count + [by_rows(width), fixed(w_o), by_rows(width), fixed(gain)],
        out_specs=[by_rows(width), by_rows(depth), pl.BlockSpec((8, BLOCK), lambda i: (i, 0))],
        out_shape=[
            jax.ShapeDtypeStruct((count * BLOCK, width), BF),
            jax.ShapeDtypeStruct((count * BLOCK, depth), BF),
            jax.ShapeDtypeStruct((count * 8, BLOCK), F32),
        ],
        scratch_shapes=[pltpu.VMEM((2, BLOCK, depth), BF), pltpu.SemaphoreType.DMA((2,))],
        **arbitrary("gate_forward"),
    )(*pieces, z, w_o, y, gain)


def out_kernel(z_in, dn_in, y_in, sums, gain, w_o, normed, dy, dz, dgain, *refs, n, bits):
    step = pl.program_id(0)
    @pl.when(pl.program_id(0) == 0)
    def _():
        dgain[...] = jnp.zeros(dgain.shape, F32)

    scale = lax.rsqrt(sums[0:1, :] / INNER + NORM_EPS)
    slope = scale * scale * scale * sums[1:2, :] / INNER
    row = iota2((LANES, BLOCK), 0)
    columns = jnp.where(row == 0, scale, jnp.where(row == 1, slope, 0.0)).T
    scale, slope = columns[:, 0:1], columns[:, 1:2]
    for lo in range(0, normed.shape[1], 2 * LANES):
        hi = lo + 2 * LANES
        z, y, dn = z_in[:, lo:hi].astype(F32), y_in[:, lo:hi].astype(F32), dn_in[:, lo:hi].astype(F32)
        sig = jax.nn.sigmoid(z)
        silu = z * sig
        gz = y * silu
        unit = gz * scale
        normed[:, lo:hi] = (unit * gain[0:1, lo:hi]).astype(BF)
        dgain[:, lo:hi] += jnp.sum((dn * unit).reshape(BLOCK // 8, 8, 2 * LANES), axis=0)
        d_gz = dn * gain[0:1, lo:hi] * scale - gz * slope
        dy[:, lo:hi] = (d_gz * silu).astype(BF)
        dz[:, lo:hi] = (d_gz * y * (sig + silu * (1.0 - sig))).astype(BF)
    out = dot(normed[...], w_o[...], NT).astype(BF)
    emit(out, refs[:4], refs[4], refs[5], step // n, step % n, bits, step, MICRO * n)


def out_project(z, dn, y, sums, gain, w_o, bits):
    depth, width = w_o.shape
    tokens = z.shape[0]
    n = tokens // BLOCK // MICRO
    one = by_rows(width)
    shapes, places, scratch = emitted(MICRO, n, depth)
    return pl.pallas_call(
        functools.partial(out_kernel, n=n, bits=bits),
        grid=(tokens // BLOCK,),
        in_specs=[one, one, one, pl.BlockSpec((8, BLOCK), lambda i: (i, 0)), fixed(gain), fixed(w_o)],
        out_specs=[one, one, one, pl.BlockSpec((8, width), lambda i: (0, 0))] + places,
        out_shape=[jax.ShapeDtypeStruct((tokens, width), BF)] * 3 + [jax.ShapeDtypeStruct((8, width), F32)] + shapes,
        scratch_shapes=scratch,
        **arbitrary("out_project"),
    )(z, dn, y, sums, gain, w_o)


def back_kernel(dz, px, w_z, w_x, *refs, n, bits):
    step = pl.program_id(0)
    out = (dot(dz[...], w_z[...], NT) + dot(px[...], w_x[...], NT)).astype(BF)
    emit(out, refs[:4], refs[4], refs[5], 0, step, bits, step, n)


def back_project(micro, dz, px, w_z, w_x, bits):
    tokens, width = px.shape
    depth = w_z.shape[0]
    n = tokens // BLOCK
    shapes, places, scratch = emitted(1, n, depth)
    return pl.pallas_call(
        functools.partial(back_kernel, n=n, bits=bits),
        grid=(n,),
        in_specs=[pl.BlockSpec((BLOCK, dz.shape[1]), lambda i: (micro * n + i, 0)), by_rows(width), fixed(w_z), fixed(w_x)],
        out_specs=places,
        out_shape=shapes,
        scratch_shapes=scratch,
        **arbitrary("back_project"),
    )(dz, px, w_z, w_x)


def shard_kernel(spot, *refs, n, hl):
    fronts, backs, (weight, gain, shard_in, shard_out, last) = refs[:n], refs[n : 2 * n], refs[2 * n :]
    rank, own = spot[0], spot[1]
    width = hl * HEADDIM
    rows = weight.shape[0]
    lane = iota2((rows, LANES), 1)
    square = jnp.zeros((rows, LANES), F32)
    scaled = jnp.zeros((rows, LANES), F32)
    shared = [jnp.zeros((rows, LANES), F32) for _ in range(2 * STATE // LANES + 1)]
    for mask in range(n):
        at = (rank ^ mask) * width
        for lo in range(0, width, LANES):
            spot_z = pl.multiple_of(at + lo, LANES)
            spot_x = pl.multiple_of(INNER + at + lo, LANES)
            out = fronts[mask][:, lo : lo + LANES].astype(F32)
            z = fronts[mask][:, width + lo : width + lo + LANES].astype(F32)
            x = backs[mask][:, lo : lo + LANES].astype(F32)
            shard_out[:, pl.ds(spot_z, LANES)] = out
            shard_in[:, pl.ds(spot_z, LANES)] = z
            shard_in[:, pl.ds(spot_x, LANES)] = x
            square += out * out + z * z + x * x
            scaled += weight[:, pl.ds(spot_z, LANES)].astype(BF).astype(F32) * z
            scaled += weight[:, pl.ds(spot_x, LANES)].astype(BF).astype(F32) * x
        for at_lane in range(2 * STATE // LANES):
            lo = width + at_lane * LANES
            shared[at_lane] += backs[mask][:, lo : lo + LANES].astype(F32)
        steps = jnp.where(lane < hl, backs[mask][:, width + 2 * STATE :].astype(F32), 0.0)
        shared[-1] += pltpu.roll(steps, (rank ^ mask) * hl, 1)
    for at_lane, one in enumerate(shared):
        lo = 2 * INNER + at_lane * LANES
        wide = min(LANES, weight.shape[1] - lo)
        one = one[:, :wide]
        shard_in[:, lo : lo + wide] = one
        square += jnp.concatenate([one * one, jnp.zeros((rows, LANES - wide), F32)], axis=1) if wide < LANES else one * one
        part = weight[:, lo : lo + wide].astype(BF).astype(F32) * one
        scaled += jnp.concatenate([part, jnp.zeros((rows, LANES - wide), F32)], axis=1) if wide < LANES else part
    d_gain = jnp.sum(scaled, axis=1, keepdims=True) / gain[:, 0:1]
    start = own * rows
    line = jnp.sum(jnp.where(lane == start % LANES + iota2((rows, LANES), 0), d_gain, 0.0), axis=0, keepdims=True)
    total = jnp.sum(jnp.sum(square, axis=0, keepdims=True), axis=1, keepdims=True)
    row, col = iota2(last.shape, 0), iota2(last.shape, 1)
    last[...] = jnp.where(row == start // LANES, line, 0.0) + jnp.where((row == D // LANES) & (col == 0), total, 0.0)


def shards(spot, fronts, backs, weight, gain, hl):
    rows = weight.shape[0]
    return pl.pallas_call(
        functools.partial(shard_kernel, n=len(fronts), hl=hl),
        grid_spec=pltpu.PrefetchScalarGridSpec(
            num_scalar_prefetch=1,
            grid=(1,),
            in_specs=[pl.BlockSpec(one.shape, lambda i, spot: (0, 0)) for one in (*fronts, *backs, weight, gain)],
            out_specs=[
                pl.BlockSpec(weight.shape, lambda i, spot: (0, 0)),
                pl.BlockSpec((rows, INNER), lambda i, spot: (0, 0)),
                pl.BlockSpec((D // LANES + 8, LANES), lambda i, spot: (0, 0)),
            ],
        ),
        out_shape=[
            jax.ShapeDtypeStruct(weight.shape, F32),
            jax.ShapeDtypeStruct((rows, INNER), F32),
            jax.ShapeDtypeStruct((D // LANES + 8, LANES), F32),
        ],
        **arbitrary("shards"),
    )(spot, *fronts, *backs, weight, gain)


def small_kernel(conv_0, conv_1, vec_0, vec_1, skip_0, skip_1, gain, out):
    width = gain.shape[1]
    out[...] = jnp.zeros(out.shape, F32)
    for tap in range(CONV + 1):
        rows = slice(tap * 8, tap * 8 + 8)
        out[tap : tap + 1, :] = jnp.sum(conv_0[rows, :] + conv_1[rows, :], axis=0, keepdims=True)
    out[5:6, :width] = jnp.sum(gain[...], axis=0, keepdims=True)
    out[6:7, :width] = jnp.sum(skip_0[...] + skip_1[...], axis=0, keepdims=True)
    vec = vec_0[...] + vec_1[...]
    head, lane = iota2((SLOT, LANES), 0), iota2((SLOT, LANES), 1)
    line = jnp.where(lane == head, vec[:, 0:1], jnp.where(lane == SLOT + head, vec[:, 1:2], 0.0))
    out[7:8, :LANES] = jnp.sum(line, axis=0, keepdims=True)


def small_gradients(*parts):
    return pl.pallas_call(
        small_kernel,
        out_shape=jax.ShapeDtypeStruct((8, parts[0].shape[1]), F32),
        name="small_gradients",
    )(*parts)


def place_kernel(spot, *refs, width):
    *pieces, out = refs
    shared = 0.0
    for mask, piece in enumerate(pieces):
        at = (spot[0] ^ mask) * width
        for lo in range(0, width, LANES):
            out[:, pl.ds(pl.multiple_of(at + lo, LANES), LANES)] = piece[:, lo : lo + LANES]
        shared = shared + piece[:, width:]
    out[:, INNER:] = shared


def place_small(spot, pieces, width):
    return pl.pallas_call(
        functools.partial(place_kernel, width=width),
        grid_spec=pltpu.PrefetchScalarGridSpec(
            num_scalar_prefetch=1,
            grid=(1,),
            in_specs=[pl.BlockSpec(one.shape, lambda i, spot: (0, 0)) for one in pieces],
            out_specs=pl.BlockSpec((8, CH), lambda i, spot: (0, 0)),
        ),
        out_shape=jax.ShapeDtypeStruct((8, CH), F32),
        **arbitrary("place_small"),
    )(spot, *pieces)

def swapped(value, axis, mask):
    return lax.ppermute(value, axis, [(i, i ^ mask) for i in range(lax.axis_size(axis))])


def axis_bits(axis):
    return [1 << i for i in range(lax.axis_size(axis).bit_length() - 1)]


def micro_order(micro, axis):
    bits = axis_bits(axis)
    return bits if micro % 2 == 0 else bits[::-1]


def nothing(*refs):
    pass


def after(values, *done):
    values = list(values)
    anywhere = pl.BlockSpec(memory_space=pl.ANY)
    held = pl.pallas_call(
        nothing,
        in_specs=[anywhere] * (len(values) + len(done)),
        out_specs=[anywhere] * len(values),
        out_shape=[jax.ShapeDtypeStruct(v.shape, v.dtype) for v in values],
        input_output_aliases={at: at for at in range(len(values))},
        name="after",
    )(*values, *done)
    return list(held)


def gather_stages(own):
    held = [{0: own[micro]} for micro in range(MICRO)]
    for turn in range(len(axis_bits("seq"))):
        got = []
        for micro in range(MICRO):
            bit = micro_order(micro, "seq")[turn]
            got.append({at ^ bit: swapped(held[micro][at], "seq", bit) for at in held[micro]})
        wait = yield [piece for one in got for piece in one.values()], [piece for one in held for piece in one.values()]
        for micro in range(MICRO):
            if wait is not None:
                got[micro] = dict(zip(got[micro], after(got[micro].values(), *wait)))
            held[micro].update(got[micro])
    yield [held[micro][at] for micro in range(MICRO) for at in range(len(held[micro]))]


def scatter_stages(parts):
    n = 2 * parts[0].shape[1]
    away, stay = list(parts[0::2]), list(parts[1::2])
    places = [[at for at in range(n) if not at & micro_order(half, "seq")[0]] for half in range(2)]
    join = lambda one, more: (one.astype(F32) + more.astype(F32)).astype(BF)
    pick = lambda a, at: jnp.concatenate([a[:, k : k + 1] for k in at], axis=1)
    turns = len(axis_bits("seq"))
    for turn in range(turns):
        got = [swapped(away[half], "seq", micro_order(half, "seq")[turn]) for half in range(2)]
        wait = yield got, away
        if wait is not None:
            got = after(got, *wait)
        if turn == turns - 1:
            break
        held, away, stay = stay, [], []
        for half in range(2):
            bit = micro_order(half, "seq")[turn + 1]
            leave = [at for at, place in enumerate(places[half]) if place & bit]
            keep = [at for at, place in enumerate(places[half]) if not place & bit]
            away.append(join(pick(held[half], leave), pick(got[half], leave)))
            stay.append(join(pick(held[half], keep), pick(got[half], keep)))
            places[half] = [places[half][at] for at in keep]
    yield jnp.concatenate([join(one, more)[:, 0] for one, more in zip(stay, got)], axis=1), None


def finish(stages, wait=None):
    last = None
    try:
        while True:
            last = stages.send(wait)
    except StopIteration:
        return last[0]


def turned(entries, rank):
    entries = list(entries)
    for bit in axis_bits("seq"):
        flip = (rank & bit) != 0
        entries = [jnp.where(flip, entries[at ^ bit], entries[at]) for at in range(len(entries))]
    return entries


def exchange(entries, rank):
    entries = turned(entries, rank)
    return entries, [swapped(one, "seq", mask) for mask, one in enumerate(entries) if mask]


def sum_pieces(value):
    n = value.shape[-2]
    total = value
    for mask in range(1, n):
        got = swapped(value, "seq", mask)
        total = total + jnp.concatenate([got[..., at ^ mask : (at ^ mask) + 1, :] for at in range(n)], axis=-2)
    return total


def adamw(master, gradient, first, second, clip, decay):
    clipped = gradient * clip
    first_new = BETA_ONE * first + (1.0 - BETA_ONE) * clipped
    second_new = BETA_TWO * second + (1.0 - BETA_TWO) * clipped * clipped
    update = first_new / FIX_ONE / (jnp.sqrt(second_new / FIX_TWO) + ADAM_EPS) + decay * master
    return (-LEARN_RATE * update, first_new, second_new)


def per_device(tokens, cotangent, segments, in_weight, in_m, in_v, conv_weight, conv_m, conv_v,
               out_weight, out_m, out_v, packed, packed_m, packed_v):
    n = lax.axis_size("seq")
    rank = lax.axis_index("seq")
    own = lax.axis_index("dp") * n + rank
    place = rank.astype(jnp.int32).reshape(1)
    ndev = n * lax.axis_size("dp")
    hl = HEADS // n
    xw = hl * HEADDIM
    rows = D // ndev
    piece = tokens.shape[1]
    count = MICRO * n * piece
    xs = INNER + INNER
    bc = 2 * STATE
    xc = xw + bc + LANES
    cw = conv_weight.shape[1]
    conv_cols = -(-(CONV + 1) * cw // rows)

    in_low = in_weight.astype(BF)
    out_low = out_weight.astype(BF).T
    conv_flat = conv_weight.astype(BF).reshape(-1)
    conv_flat = jnp.pad(conv_flat, (0, conv_cols * rows - conv_flat.shape[0])).reshape(rows, conv_cols)
    column = lambda a, q, width: a[:, q * width : (q + 1) * width]
    pad = jnp.zeros((rows, LANES - hl - conv_cols), BF)
    send_x = [
        jnp.concatenate(
            [column(in_low[:, INNER:xs], q, xw), in_low[:, xs : xs + bc], column(in_low[:, xs + bc :], q, hl), conv_flat, pad], axis=1
        )
        for q in range(n)
    ]
    gain_in = packed[3 * HEADS : 3 * HEADS + D]
    send_x = turned(send_x, rank)
    got_wx = [one if not mask else swapped(one, "seq", mask) for mask, one in enumerate(send_x)]
    a_log = lax.dynamic_slice_in_dim(packed, rank * hl, hl)
    skip = lax.dynamic_slice_in_dim(packed, HEADS + rank * hl, hl)
    dt_bias = lax.dynamic_slice_in_dim(packed, 2 * HEADS + rank * hl, hl)
    gain_out = lax.dynamic_slice_in_dim(packed, 3 * HEADS + D + rank * xw, xw)
    aux, masks = segment_aux(segments)
    heads = head_columns(a_log, dt_bias)
    skip = jnp.broadcast_to(jnp.repeat(skip, HEADDIM)[None], (8, xw))

    tok = tokens.astype(F32)
    r_in = lax.rsqrt(jnp.mean(tok * tok, axis=-1, keepdims=True) + NORM_EPS)
    hidden_stages = gather_stages((tok * r_in * gain_in).astype(BF))
    arrived, sent = next(hidden_stages)
    more, _ = hidden_stages.send(None)
    got_wx = jnp.concatenate(turned(got_wx[:1] + after(got_wx[1:], *sent), rank), axis=0)
    w_x = lax.all_gather(got_wx, "dp", axis=0, tiled=True)
    send_zo = jnp.stack(turned([jnp.concatenate([column(in_low, q, xw), column(out_low, q, xw)], axis=1) for q in range(n)], rank))
    [send_zo] = after([send_zo], got_wx, more[0], more[2])
    got_wzo = [send_zo[mask] if not mask else swapped(send_zo[mask], "seq", mask) for mask in range(n)]
    got_wzo = jnp.concatenate(turned(got_wzo, rank), axis=0)
    w_z = lax.all_gather(got_wzo[:, :xw], "dp", axis=0, tiled=True)
    w_o = lax.all_gather(got_wzo[:, xw:], "dp", axis=0, tiled=True)
    conv_full = w_x[:, xw + bc + hl : xw + bc + hl + conv_cols].reshape(ndev, rows * conv_cols)[:, : (CONV + 1) * cw]
    conv_full = conv_full.reshape(ndev, CONV + 1, cw).transpose(1, 0, 2).reshape(CONV + 1, CH)
    conv_loc = jnp.concatenate([lax.dynamic_slice_in_dim(conv_full, rank * xw, xw, 1), conv_full[:, INNER:]], axis=1).astype(F32)
    conv_loc = jnp.pad(conv_loc, ((0, 8 - CONV - 1), (0, 0)))

    for _ in axis_bits("seq")[1:]:
        arrived, more = more, hidden_stages.send(None)
        more = more[0] if isinstance(more, tuple) else more
    late = [micro * n + at for micro in range(MICRO) for at in range(n) if at & (last := micro_order(micro, "seq")[-1]) and at != last]
    soon = [at for at in range(MICRO * n) if at not in late]
    soon.sort(key=lambda at: (at % n).bit_count())
    earlier = in_project([more[at] for at in soon], soon, MICRO * n, w_x, done=(aux, masks, conv_loc))
    late_pieces = after([more[at] for at in late], earlier[0])
    proj_x, hidden = in_project(late_pieces, late, MICRO * n, w_x, earlier)

    cot_stages = gather_stages(after([cotangent[micro] for micro in range(MICRO)], *late_pieces))
    next(cot_stages)
    y, states, act, slope = scan_forward(place, proj_x, conv_loc, skip, heads, aux, masks, hl)
    for bit in axis_bits("seq"):
        cot = cot_stages.send([proj_x] if bit == 1 else [y])
    gain = jnp.broadcast_to(gain_out[None], (8, xw))
    [w_z] = after([w_z], y)
    z = dot(hidden, w_z, NN).astype(BF)
    dn, cot, sums = gate_forward(cot, z, w_o, y, gain)
    sums = sum_pieces(sums.reshape(MICRO, n, 8 * BLOCK)).reshape(-1, BLOCK)
    first_bits = tuple(micro_order(half, "seq")[0] for half in range(2))
    normed, dy, dz, d_gain_out, *out_part = out_project(z, dn, y, sums, gain, w_o, first_bits)

    scatter = lambda a: lax.psum_scatter(a, "dp", scatter_dimension=0, tiled=True)
    split = lambda a: [a[q * rows : (q + 1) * rows] for q in range(n)]
    out_stages = scatter_stages(out_part)
    next(out_stages)
    part_o = dot(cot, normed, TN).astype(BF)
    part_z = dot(hidden, dz, TN).astype(BF)
    got_o, got_z = scatter(part_o), scatter(part_z)

    through_in = lambda micro, one: back_project(micro, dz, one, w_z, w_x, first_bits)
    scan_back = lambda micro, *done: scan_backward(
        place, micro, proj_x, conv_loc, skip, heads, aux, masks, act, slope, dy, states, hl, *done
    )

    px_0, dco_0, vec_0, skip_0 = scan_back(0, part_o, part_z)
    hid_0 = through_in(0, px_0)
    out_got, out_sent = out_stages.send([hid_0[0]])
    stages_0 = scatter_stages(hid_0)
    hid_got, sent = next(stages_0)
    px_1, dco_1, vec_1, skip_1 = scan_back(1, *sent, *out_sent)
    [px_1] = after([px_1], *hid_got, *out_got)
    part_x = dot(hidden, jnp.concatenate([px_0, px_1], axis=0), TN).astype(BF)
    got_x = scatter(part_x)
    hid_got, sent = stages_0.send([part_x])
    spot = jnp.stack([rank, own]).astype(jnp.int32)
    own_gain = lax.dynamic_slice_in_dim(gain_in, own * rows, rows)[:, None]
    [px_1] = after([px_1], part_x, *sent)
    hid_1 = through_in(1, px_1)
    [got_o, got_z] = after([got_o, got_z], part_x)
    sent_oz, got_oz = exchange(split(jnp.concatenate([got_o, got_z], axis=1)), rank)
    dco_0, dco_1 = after([dco_0, dco_1], hid_1[0], *got_oz)
    conv_0, conv_1 = (tap_gradients(place, micro, proj_x, aux, one) for micro, one in enumerate((dco_0, dco_1)))
    stages_1 = scatter_stages(after(hid_1, *hid_got))
    hid_got, _ = next(stages_1)
    small = small_gradients(conv_0, conv_1, vec_0, vec_1, skip_0, skip_1, d_gain_out)
    [small] = after([small], *hid_got)
    for bit in axis_bits("dp"):
        small = small + swapped(small, "dp", bit)
    _, hid_sent = stages_1.send(None)
    [got_x] = after([got_x], small, *hid_sent)
    sent_x, got_x = exchange(split(got_x), rank)
    [small] = after([small], *sent_x)
    small = [small] + after([swapped(small, "seq", mask) for mask in range(1, n)], *got_x)
    small = place_small(spot, small, xw)
    conv_tot, gain_out_tot = small[: CONV + 1], small[5, :INNER]
    skip_tot = jnp.sum(small[6, :INNER].reshape(HEADS, HEADDIM), axis=1)
    by_head = small[7, :INNER].reshape(n, xw)
    a_log_tot, dt_bias_tot = by_head[:, :hl].reshape(-1), by_head[:, SLOT : SLOT + hl].reshape(-1)
    shard_conv = lax.dynamic_slice_in_dim(conv_tot, own * cw, cw, 1)
    conv_sq = jnp.sum(conv_tot * conv_tot)
    shard_in, shard_out, last = shards(spot, sent_oz[:1] + got_oz, sent_x[:1] + got_x, in_weight, own_gain, hl)
    shard_out = shard_out.T
    output = (tok + finish(out_stages, got_x).astype(F32)).astype(BF)
    d_hidden = jnp.concatenate([finish(stages_0, [hid_1[0]]), finish(stages_1)], axis=0).astype(F32)
    dh = d_hidden * gain_in
    d_tok = r_in * (dh - tok * (r_in * r_in) * jnp.mean(dh * tok, axis=-1, keepdims=True))
    input_grad = (cotangent.astype(F32) + d_tok).astype(BF)

    stages = [(axis, bit) for axis in ("seq", "dp") for bit in axis_bits(axis)]
    for axis, bit in stages:
        last = last + swapped(last, axis, bit)
    vec_tot = jnp.concatenate([a_log_tot, skip_tot, dt_bias_tot, last[: D // LANES].reshape(-1), gain_out_tot])
    grad_norm = jnp.sqrt(last[D // LANES, 0] + conv_sq + jnp.sum(vec_tot * vec_tot))
    clip = jnp.minimum(1.0, CLIP_NORM / (grad_norm + 1e-06))
    in_new = adamw(in_weight, shard_in, in_m, in_v, clip, WEIGHT_DECAY)
    conv_new = adamw(conv_weight, shard_conv, conv_m, conv_v, clip, WEIGHT_DECAY)
    out_new = adamw(out_weight, shard_out, out_m, out_v, clip, WEIGHT_DECAY)
    vec_new = adamw(packed, vec_tot, packed_m, packed_v, clip, 0.0)
    return (
        output, input_grad, grad_norm,
        in_weight + in_new[0], in_new[1], in_new[2],
        conv_new[0], conv_new[1], conv_new[2],
        out_weight + out_new[0], out_new[1], out_new[2],
        vec_new[0], vec_new[1], vec_new[2],
    )


def solution(mesh):
    tok, col, row = P(None, ALL, None), P(None, ALL), P(ALL, None)
    return jax.shard_map(
        per_device,
        mesh=mesh,
        in_specs=(tok, tok, P(None, "dp"), row, row, row, col, col, col, col, col, col, P(), P(), P()),
        out_specs=(tok, tok, P(), row, row, row, col, col, col, col, col, col, P(), P(), P()),
        check_vma=False,
    )
```

```python
import functools

import jax
import jax.numpy as jnp
from jax import lax
from jax.experimental import pallas as pl
from jax.experimental.pallas import tpu as pltpu
from jax.sharding import PartitionSpec as P

D = 2048
HEADS = 64
HEADDIM = 64
STATE = 128
CONV = 4
BLOCK = 256
MICRO = 2
INNER = 4096
CH = 4352
NORM_EPS = 1e-05
LEARN_RATE = 0.004
BETA_ONE = 0.9
BETA_TWO = 0.95
FIX_ONE = 1.0 - 0.9**10
FIX_TWO = 1.0 - 0.95**10
ADAM_EPS = 1e-08
WEIGHT_DECAY = 0.1
CLIP_NORM = 1.0
BF = jnp.bfloat16
F32 = jnp.float32
ALL = ("dp", "seq")


def dot(a, b, dims, out=F32):
    return lax.dot_general(a, b, (dims, ((), ())), preferred_element_type=out)


NN = ((1,), (0,))
NT = ((1,), (1,))
TN = ((0,), (0,))
LANES = 128
PAIR = 2 * HEADDIM
VMEM = 56 * 1024 * 1024
SLOT = 16
TINY = 1e-37
CAP = 85.0


def iota2(shape, dim):
    return lax.broadcasted_iota(jnp.int32, shape, dim)


def tree(value, rows=8):
    while value.shape[0] > rows:
        half = value.shape[0] // 2
        value = value[:half] + value[half:]
    return value


def thirds(value):
    high = value.astype(BF).astype(F32)
    rest = value - high
    mid = rest.astype(BF).astype(F32)
    return high, mid, (rest - mid).astype(BF).astype(F32)


def running_sum(values, reverse):
    row, col = iota2((BLOCK, BLOCK), 0), iota2((BLOCK, BLOCK), 1)
    ones = jnp.where(row >= col if reverse else row <= col, 1.0, 0.0).astype(BF)
    sums = dot(jnp.concatenate(thirds(values), axis=0).astype(BF), ones, NN)
    return sums[:SLOT] + sums[SLOT : 2 * SLOT] + sums[2 * SLOT :]


def step_rows(raw, heads, masks):
    lifted = raw.astype(F32).T[:SLOT] + heads[:, 0:1]
    dt = jnp.maximum(lifted, 0.0) + jnp.log1p(jnp.exp(-jnp.abs(lifted)))
    cum = running_sum(dt * heads[:, 1:2], False)
    entry = jnp.exp(cum) * masks[1:2, :]
    dt_end = dt * jnp.exp(cum[:, BLOCK - 1 : BLOCK] - cum) * masks[2:3, :]
    return lifted, dt, cum, entry, dt_end


def two(value):
    high = value.astype(BF).astype(F32)
    return [high, value - high]


def as_columns(gap_rows, entry, dt_end):
    ones = jnp.where(iota2((SLOT, BLOCK), 0) < 3, 1.0, 0.0)
    return jnp.concatenate([*thirds(gap_rows), ones, *two(entry), *two(dt_end)], axis=0).T.astype(BF)


def gap_right_init(right, hl):
    row = iota2((3 * SLOT, BLOCK), 0)
    for h in range(hl):
        right[0 : 3 * SLOT, h * BLOCK : (h + 1) * BLOCK] = jnp.where((row & (SLOT - 1)) == h, 1.0, 0.0).astype(BF)


def gap_right_fill(right, values, hl):
    row = iota2((SLOT, BLOCK), 0)
    high, mid, low = thirds(values)
    for h in range(hl):
        one = slice(h, h + 1)
        slab = jnp.where(row == 0, high[one], jnp.where(row == 1, mid[one], jnp.where(row == 2, low[one], 0.0)))
        right[3 * SLOT :, h * BLOCK : (h + 1) * BLOCK] = slab.astype(BF)


def head_spread_init(spreads, hl):
    row, col = iota2(spreads.shape, 0), iota2(spreads.shape, 1)
    head = jnp.where(col < hl * HEADDIM, col, col - hl * HEADDIM) // HEADDIM
    slot = jnp.where(col < hl * HEADDIM, 2, 3)
    spreads[...] = jnp.where(((row & (SLOT - 1)) == head) & (row // (2 * SLOT) == slot), 1.0, 0.0).astype(BF)


def stacked(left, pair_values):
    zero = jnp.zeros_like(pair_values)
    return jnp.concatenate([jnp.where(left, pair_values, zero), jnp.where(left, zero, pair_values)], axis=0)


def conv_chunk(window, conv_w, valid, lo, hi):
    out = conv_w[CONV : CONV + 1, lo:hi] + conv_w[CONV - 1 : CONV, lo:hi] * window[8 : 8 + BLOCK, lo:hi]
    for tap in range(CONV - 1):
        out += conv_w[tap : tap + 1, lo:hi] * (window[5 + tap : 5 + tap + BLOCK, lo:hi] * valid[tap])
    return out


def spread(aux_v, at):
    return jnp.broadcast_to(aux_v[:, at : at + 1], (BLOCK, LANES))


def forward_kernel(place, proj, conv_w, skip, heads, aux, masks, y_out, s_out, act, slope, window, state, right, carried, spreads, *, hl):
    width = hl * HEADDIM
    conv_width = width + 2 * STATE

    @pl.when(pl.program_id(1) == 0)
    def _():
        window[0:8, :] = jnp.zeros((8, conv_width), F32)
        state[...] = jnp.zeros(state.shape, F32)
        gap_right_init(right, hl)
        head_spread_init(spreads, hl)

    aux_v = aux[...]
    valid = [spread(aux_v, tap) for tap in range(CONV - 1)]
    for lo in range(0, conv_width, LANES):
        hi = lo + LANES
        window[8 : 8 + BLOCK, lo:hi] = proj[:, lo:hi].astype(F32)
        out = conv_chunk(window, conv_w, valid, lo, hi)
        sig = jax.nn.sigmoid(out)
        silu = out * sig
        act[:, lo:hi] = silu.astype(BF)
        slope[:, lo:hi] = (sig + silu * (1.0 - sig)).astype(BF)
    window[0:8, :] = window[BLOCK : BLOCK + 8, :]

    _, dt, cum, entry, dt_end = step_rows(proj[:, conv_width : conv_width + LANES], heads[...], masks)
    columns = as_columns(cum, entry, dt_end)
    gaps = columns[:, : 4 * SLOT]
    gap_right_fill(right, jnp.log(jnp.maximum(dt, TINY)) - cum, hl)
    bm, cm = act[:, width : width + STATE], act[:, width + STATE :]
    same = (aux_v[:, 3:4] == masks[0:1, :]) & (iota2((BLOCK, BLOCK), 0) >= iota2((BLOCK, BLOCK), 1))
    inner = jnp.where(same, dot(cm, bm, NT), 0.0)
    left = iota2((BLOCK, PAIR), 1) < HEADDIM
    top = iota2((PAIR, STATE), 0) < HEADDIM
    last = entry[:, BLOCK - 1 : BLOCK]
    s_out[0] = state[...].astype(BF)
    carried[...] = dot(columns, spreads[...], NN)
    carried[:, :width] = carried[:, :width] * dot(cm, s_out[0], NT)
    for pair in range(hl // 2):
        first = 2 * pair
        lo, hi = pair * PAIR, (pair + 1) * PAIR
        xp = act[:, lo:hi]
        mix = []
        for h in (first, first + 1):
            decay = jnp.exp(jnp.minimum(dot(gaps, right[:, h * BLOCK : (h + 1) * BLOCK], NN), CAP))
            mix.append((inner * decay).astype(BF))
        xf = xp.astype(F32)
        y = dot(jnp.concatenate(mix, axis=1), stacked(left, xp), NN)
        y += carried[:, lo:hi] + skip[0:1, lo:hi] * xf
        y_out[:, lo:hi] = y.astype(BF)
        weighted = (xf * carried[:, width + lo : width + hi]).astype(BF)
        keep = jnp.where(top, last[first : first + 1], last[first + 1 : first + 2])
        state[lo:hi, :] = keep * state[lo:hi, :] + dot(weighted, bm, TN)


def backward_kernel(place, proj, conv_w, skip, heads, aux, masks, act, slope, dy, s_in, *refs, hl):
    dproj, dco, dvec, dskip, dwin, grad_s, dcb, colsum, dkeep, right, carried, later_w, spreads, picks, sums, used, into = refs[-17:]
    width = hl * HEADDIM
    conv_width = width + 2 * STATE

    @pl.when(pl.program_id(0) == 0)
    def _():
        dvec[...] = jnp.zeros(dvec.shape, F32)
        dskip[...] = jnp.zeros(dskip.shape, F32)
        dwin[BLOCK : BLOCK + 8, :] = jnp.zeros((8, conv_width), F32)
        grad_s[...] = jnp.zeros(grad_s.shape, F32)
        colsum[...] = jnp.zeros(colsum.shape, F32)
        dkeep[...] = jnp.zeros(dkeep.shape, F32)
        gap_right_init(right, hl)
        head_spread_init(spreads, hl)
        picks[...] = jnp.where(iota2(picks.shape, 0) == iota2(picks.shape, 1) // BLOCK, 1.0, 0.0).astype(BF)
        sums[...] = jnp.where(iota2(sums.shape, 0) == iota2(sums.shape, 1) // HEADDIM, 1.0, 0.0).astype(BF)

    aux_v = aux[...]
    lifted, dt, cum, entry, dt_end = step_rows(proj[:, conv_width : conv_width + LANES], heads[...], masks)
    a_neg = heads[:, 1:2]
    columns = as_columns(jnp.log(jnp.maximum(dt, TINY)) - cum, entry, dt_end)
    gaps = columns[:, : 4 * SLOT]
    gap_right_fill(right, cum, hl)
    bm, cm = act[:, width : width + STATE], act[:, width + STATE :]
    same = (aux_v[:, 3:4] == masks[0:1, :]) & (iota2((BLOCK, BLOCK), 0) <= iota2((BLOCK, BLOCK), 1))
    inner = jnp.where(same, dot(bm, cm, NT), 0.0)
    left = iota2((BLOCK, PAIR), 1) < HEADDIM
    top = iota2((PAIR, STATE), 0) < HEADDIM
    last = entry[:, BLOCK - 1 : BLOCK]
    d_row = jnp.zeros((SLOT, BLOCK), F32)
    d_b = jnp.zeros((BLOCK, STATE), F32)
    d_c = jnp.zeros((BLOCK, STATE), F32)
    spreaded = dot(columns, spreads[...], NN)
    carried[...] = spreaded
    later_w[:, :width] = dot(cm, s_in[0], NT)
    later_w[:, width:] = dot(bm, grad_s[...].astype(BF), NT)

    for pair in range(hl // 2):
        first = 2 * pair
        lo, hi = pair * PAIR, (pair + 1) * PAIR
        xp, dyp = act[:, lo:hi], dy[:, lo:hi]
        xf, dyf = xp.astype(F32), dyp.astype(F32)
        d_mix = dot(stacked(left, xp), dyp, NT)
        mix, pairwise = [], []
        d_inner = 0.0
        for at, h in enumerate((first, first + 1)):
            decay = jnp.exp(jnp.minimum(dot(gaps, right[:, h * BLOCK : (h + 1) * BLOCK], NN), CAP))
            mix.append((inner * decay).astype(BF))
            part = d_mix[at * BLOCK : (at + 1) * BLOCK] * decay
            d_inner += part
            part = (part * inner).astype(BF)
            pairwise.append(part)
            colsum[h : h + 1, :] = jnp.sum(tree(part.astype(F32)), axis=0, keepdims=True)
        d_row += dot(picks[:, first * BLOCK : (first + 2) * BLOCK], jnp.concatenate(pairwise, axis=1), NT)
        if pair == 0:
            dcb[...] = d_inner
        else:
            dcb[...] += d_inner
        later = grad_s[lo:hi, :]
        low = s_in[0, lo:hi, :]
        end_p = carried[:, width + lo : width + hi]
        from_end = later_w[:, width + lo : width + hi] * end_p
        dx = dot(jnp.concatenate(mix, axis=1), stacked(left, dyp), NN) + from_end + skip[0:1, lo:hi] * dyf
        dwin[0:BLOCK, lo:hi] = slope[:, lo:hi].astype(F32) * dx
        used[:, lo:hi] = (from_end * xf).astype(BF)
        entering = carried[:, lo:hi] * dyf
        into[:, lo:hi] = (entering * later_w[:, lo:hi]).astype(BF)
        entering = entering.astype(BF)
        dskip[:, lo:hi] += tree(xf * dyf)
        kept = later * low.astype(F32)
        dkeep[first : first + 1, :] = jnp.sum(tree(kept[:HEADDIM]), axis=0, keepdims=True)
        dkeep[first + 1 : first + 2, :] = jnp.sum(tree(kept[HEADDIM:]), axis=0, keepdims=True)
        weighted = (xf * end_p).astype(BF)
        d_b += dot(weighted, later.astype(BF), NN)
        d_c += dot(entering, low, NN)
        keep = jnp.where(top, last[first : first + 1], last[first + 1 : first + 2])
        grad_s[lo:hi, :] = dot(entering, cm, TN) + keep * later

    d_inner = jnp.where(same, dcb[...], 0.0).astype(BF)
    d_b += dot(d_inner, cm, NN)
    d_c += dot(d_inner, bm, TN)
    dwin[0:BLOCK, width : width + STATE] = slope[:, width : width + STATE].astype(F32) * d_b
    dwin[0:BLOCK, width + STATE :] = slope[:, width + STATE :].astype(F32) * d_c

    d_end = dot(sums[...], used[...], NT)
    through = d_row + d_end
    d_last = jnp.sum(d_end, axis=1, keepdims=True) + jnp.sum(dkeep[...], axis=1, keepdims=True) * last
    d_cum = dot(sums[...], into[...], NT) + colsum[...] - through
    d_cum += jnp.where(iota2((SLOT, BLOCK), 1) == BLOCK - 1, d_last, 0.0)
    d_a = running_sum(d_cum, True)
    sig = jax.nn.sigmoid(lifted)
    d_raw = through * jnp.where(dt > TINY, sig / jnp.maximum(dt, TINY), 1.0) + d_a * a_neg * sig
    d_raw = jnp.where(iota2((SLOT, BLOCK), 0) < hl, d_raw, 0.0)
    dproj[:, conv_width : conv_width + LANES] = jnp.concatenate([d_raw, jnp.zeros((LANES - SLOT, BLOCK), F32)], axis=0).T.astype(BF)
    lane = iota2((SLOT, LANES), 1)
    d_log = jnp.sum(d_a * dt, axis=1, keepdims=True) * a_neg
    dvec[...] += jnp.where(lane == 0, d_log, jnp.where(lane == 1, jnp.sum(d_raw, axis=1, keepdims=True), 0.0))

    valid = [spread(aux_v, 4 + tap) for tap in range(CONV - 1)]
    for lo in range(0, conv_width, LANES):
        hi = lo + LANES
        own = dwin[0:BLOCK, lo:hi]
        dco[:, lo:hi] = own.astype(BF)
        grad = conv_w[CONV - 1 : CONV, lo:hi] * own
        for tap in range(CONV - 1):
            ahead = CONV - 1 - tap
            grad += conv_w[tap : tap + 1, lo:hi] * (dwin[ahead : ahead + BLOCK, lo:hi] * valid[tap])
        dproj[:, lo:hi] = grad.astype(BF)
    dwin[BLOCK : BLOCK + 8, :] = dwin[0:8, :]


def taps_kernel(place, proj, aux, dco, dconv, dwin):
    conv_width = dco.shape[1]

    @pl.when(pl.program_id(0) == 0)
    def _():
        dconv[...] = jnp.zeros(dconv.shape, F32)
        dwin[BLOCK : BLOCK + 8, :] = jnp.zeros((8, conv_width), F32)

    aux_v = aux[...]
    valid = [spread(aux_v, 4 + tap) for tap in range(CONV - 1)]
    for lo in range(0, conv_width, LANES):
        hi = lo + LANES
        own = dco[:, lo:hi].astype(F32)
        dwin[0:BLOCK, lo:hi] = own
        value = proj[:, lo:hi].astype(F32)
        dconv[CONV * 8 : CONV * 8 + 8, lo:hi] += tree(own)
        dconv[(CONV - 1) * 8 : CONV * 8, lo:hi] += tree(own * value)
        for tap in range(CONV - 1):
            ahead = CONV - 1 - tap
            moved = dwin[ahead : ahead + BLOCK, lo:hi] * valid[tap]
            dconv[tap * 8 : tap * 8 + 8, lo:hi] += tree(moved * value)
    dwin[BLOCK : BLOCK + 8, :] = dwin[0:8, :]


def segment_aux(segments):
    micro, length = segments.shape
    nb = length // BLOCK
    seg = segments.astype(F32)
    blocks = seg.reshape(micro, nb, BLOCK)
    prev = jnp.concatenate([jnp.full((micro, 1), -1.0, F32), blocks[:, :-1, -1]], axis=1)
    reach = range(CONV - 1, 0, -1)
    earlier = [jnp.pad(seg, ((0, 0), (by, 0)), constant_values=-1.0)[:, :length] == seg for by in reach]
    later = [jnp.pad(seg, ((0, 0), (0, by)), constant_values=-1.0)[:, by:] == seg for by in reach]
    columns = [c.astype(F32) for c in (*earlier, seg, *later, jnp.zeros_like(seg))]
    aux = jnp.stack(columns, axis=-1).reshape(micro * length, 8)
    zero = jnp.zeros_like(blocks)
    masks = [blocks, blocks == prev[:, :, None], blocks == blocks[:, :, -1:]] + [zero] * 5
    return aux, jnp.stack([m.astype(F32) for m in masks], axis=2).reshape(micro * nb * 8, BLOCK)


def head_columns(a_log, dt_bias):
    hl = a_log.shape[0]
    both = jnp.stack([dt_bias, -jnp.exp(a_log)], axis=1)
    return jnp.pad(both, ((0, SLOT - hl), (0, LANES - 2)))


def scan_forward(place, proj, conv_w, skip, heads, aux, masks, hl):
    tokens = proj.shape[0]
    nb = tokens // MICRO // BLOCK
    width = hl * HEADDIM
    conv_width = width + 2 * STATE
    held = lambda m, j, place: (m * nb + (j ^ place[0]), 0)
    at = lambda m, j, place: (m * nb + j, 0)
    whole = lambda m, j, place: (0, 0)
    grid_spec = pltpu.PrefetchScalarGridSpec(
        num_scalar_prefetch=1,
        grid=(MICRO, nb),
        in_specs=[
            pl.BlockSpec((BLOCK, conv_width + LANES), held),
            pl.BlockSpec((8, conv_width), whole),
            pl.BlockSpec(skip.shape, whole),
            pl.BlockSpec(heads.shape, whole),
            pl.BlockSpec((BLOCK, 8), at),
            pl.BlockSpec((8, BLOCK), at),
        ],
        out_specs=[
            pl.BlockSpec((BLOCK, width), held),
            pl.BlockSpec((1, width, STATE), lambda m, j, place: (m * nb + j, 0, 0)),
            pl.BlockSpec((BLOCK, conv_width), held),
            pl.BlockSpec((BLOCK, conv_width), held),
        ],
        scratch_shapes=[
            pltpu.VMEM((BLOCK + 8, conv_width), F32),
            pltpu.VMEM((width, STATE), F32),
            pltpu.VMEM((4 * SLOT, hl * BLOCK), BF),
            pltpu.VMEM((BLOCK, 2 * width), F32),
            pltpu.VMEM((LANES, 2 * width), BF),
        ],
    )
    return pl.pallas_call(
        functools.partial(forward_kernel, hl=hl),
        grid_spec=grid_spec,
        out_shape=[
            jax.ShapeDtypeStruct((tokens, width), BF),
            jax.ShapeDtypeStruct((MICRO * nb, width, STATE), BF),
            jax.ShapeDtypeStruct((tokens, conv_width), BF),
            jax.ShapeDtypeStruct((tokens, conv_width), BF),
        ],
        compiler_params=pltpu.CompilerParams(vmem_limit_bytes=VMEM, dimension_semantics=("arbitrary", "arbitrary")),
        name="scan_forward",
    )(place, proj, conv_w, skip, heads, aux, masks)


def scan_backward(place, micro, proj, conv_w, skip, heads, aux, masks, act, slope, dy, states, hl, *done):
    tokens = proj.shape[0] // MICRO
    nb = tokens // BLOCK
    width = hl * HEADDIM
    conv_width = width + 2 * STATE
    full = conv_width + LANES
    first = micro * nb
    held = lambda j, place: (first + ((nb - 1 - j) ^ place[0]), 0)
    at = lambda j, place: (first + nb - 1 - j, 0)
    whole = lambda j, place: (0, 0)
    grid_spec = pltpu.PrefetchScalarGridSpec(
        num_scalar_prefetch=1,
        grid=(nb,),
        in_specs=[
            pl.BlockSpec((BLOCK, full), held),
            pl.BlockSpec((8, conv_width), whole),
            pl.BlockSpec(skip.shape, whole),
            pl.BlockSpec(heads.shape, whole),
            pl.BlockSpec((BLOCK, 8), at),
            pl.BlockSpec((8, BLOCK), at),
            pl.BlockSpec((BLOCK, conv_width), held),
            pl.BlockSpec((BLOCK, conv_width), held),
            pl.BlockSpec((BLOCK, width), held),
            pl.BlockSpec((1, width, STATE), lambda j, place: (first + nb - 1 - j, 0, 0)),
        ]
        + [pl.BlockSpec(memory_space=pl.ANY)] * len(done),
        out_specs=[
            pl.BlockSpec((BLOCK, full), lambda j, place: ((nb - 1 - j) ^ place[0], 0)),
            pl.BlockSpec((BLOCK, conv_width), lambda j, place: ((nb - 1 - j) ^ place[0], 0)),
            pl.BlockSpec((SLOT, LANES), whole),
            pl.BlockSpec((8, width), whole),
        ],
        scratch_shapes=[
            pltpu.VMEM((BLOCK + 8, conv_width), F32),
            pltpu.VMEM((width, STATE), F32),
            pltpu.VMEM((BLOCK, BLOCK), F32),
            pltpu.VMEM((SLOT, BLOCK), F32),
            pltpu.VMEM((SLOT, STATE), F32),
            pltpu.VMEM((4 * SLOT, hl * BLOCK), BF),
            pltpu.VMEM((BLOCK, 2 * width), F32),
            pltpu.VMEM((BLOCK, 2 * width), F32),
            pltpu.VMEM((LANES, 2 * width), BF),
            pltpu.VMEM((SLOT, hl * BLOCK), BF),
            pltpu.VMEM((SLOT, width), BF),
            pltpu.VMEM((BLOCK, width), BF),
            pltpu.VMEM((BLOCK, width), BF),
        ],
    )
    return pl.pallas_call(
        functools.partial(backward_kernel, hl=hl),
        grid_spec=grid_spec,
        out_shape=[
            jax.ShapeDtypeStruct((tokens, full), BF),
            jax.ShapeDtypeStruct((tokens, conv_width), BF),
            jax.ShapeDtypeStruct((SLOT, LANES), F32),
            jax.ShapeDtypeStruct((8, width), F32),
        ],
        compiler_params=pltpu.CompilerParams(vmem_limit_bytes=VMEM, dimension_semantics=("arbitrary",)),
        name="scan_backward",
    )(place, proj, conv_w, skip, heads, aux, masks, act, slope, dy, states, *done)


def tap_gradients(place, micro, proj, aux, dco):
    tokens, conv_width = dco.shape
    nb = tokens // BLOCK
    grid_spec = pltpu.PrefetchScalarGridSpec(
        num_scalar_prefetch=1,
        grid=(nb,),
        in_specs=[
            pl.BlockSpec((BLOCK, proj.shape[1]), lambda j, place: (micro * nb + ((nb - 1 - j) ^ place[0]), 0)),
            pl.BlockSpec((BLOCK, 8), lambda j, place: (micro * nb + nb - 1 - j, 0)),
            pl.BlockSpec((BLOCK, conv_width), lambda j, place: ((nb - 1 - j) ^ place[0], 0)),
        ],
        out_specs=pl.BlockSpec((8 * (CONV + 1), conv_width), lambda j, place: (0, 0)),
        scratch_shapes=[pltpu.VMEM((BLOCK + 8, conv_width), F32)],
    )
    return pl.pallas_call(
        taps_kernel,
        grid_spec=grid_spec,
        out_shape=jax.ShapeDtypeStruct((8 * (CONV + 1), conv_width), F32),
        compiler_params=pltpu.CompilerParams(vmem_limit_bytes=VMEM, dimension_semantics=("arbitrary",)),
        name="tap_gradients",
    )(place, proj, aux, dco)


def fetch(pieces, buffer, sems, step):
    @pl.when(step == 0)
    def _():
        pltpu.make_async_copy(pieces[0], buffer.at[0], sems.at[0]).start()

    for at in range(1, len(pieces)):

        @pl.when(step == at - 1)
        def _():
            pltpu.make_async_copy(pieces[at], buffer.at[at % 2], sems.at[at % 2]).start()

    slot = step % 2
    pltpu.make_async_copy(pieces[0], buffer.at[slot], sems.at[slot]).wait()
    return slot


def emit(value, targets, buffer, sems, micro, place, bits, step, steps):
    slot = step % 2
    rows = value.shape[0] // 2

    def waiting(at):
        for half in range(2):
            pltpu.make_async_copy(buffer.at[at, pl.ds(half * rows, rows)], targets[0].at[0, 0], sems.at[at, half]).wait()

    @pl.when(step >= 2)
    def _():
        waiting(slot)

    buffer[slot] = value
    for half, bit in enumerate(bits):
        index = place // (2 * bit) * bit + place % bit
        set_ = (place // bit) % 2
        for target, wanted in ((targets[2 * half], 1), (targets[2 * half + 1], 0)):

            @pl.when(set_ == wanted)
            def _():
                pltpu.make_async_copy(
                    buffer.at[slot, pl.ds(half * rows, rows)], target.at[micro, index], sems.at[slot, half]
                ).start()

    @pl.when(step == steps - 1)
    def _():
        waiting(0)
        waiting(1)


def emitted(some, n, depth):
    shapes = [jax.ShapeDtypeStruct((some, n // 2, BLOCK // 2, depth), BF)] * 4
    return shapes, [pl.BlockSpec(memory_space=pl.ANY)] * 4, [pltpu.VMEM((2, BLOCK, depth), BF), pltpu.SemaphoreType.DMA((2, 2))]


def fixed(array):
    return pl.BlockSpec(array.shape, lambda i: (0, 0), pipeline_mode=pl.Buffered(1))


def by_rows(width):
    return pl.BlockSpec((BLOCK, width), lambda i: (i, 0))


def arbitrary(name):
    return dict(compiler_params=pltpu.CompilerParams(vmem_limit_bytes=VMEM, dimension_semantics=("arbitrary",)), name=name)


def in_kernel(*refs, count):
    pieces, w, (proj, hidden, buffer, sems) = refs[1 : count + 1], refs[count + 1], refs[-4:]
    slot = fetch(pieces, buffer, sems, pl.program_id(0))
    value = buffer[slot]
    hidden[...] = value
    proj[...] = dot(value, w[...], NN).astype(BF)


def in_project(pieces, places, total, w, earlier=(), done=()):
    count = len(pieces)
    depth, width = w.shape
    anywhere = [pl.BlockSpec(memory_space=pl.ANY)]
    at = lambda i, table: (table[i], 0)
    return pl.pallas_call(
        functools.partial(in_kernel, count=count),
        grid_spec=pltpu.PrefetchScalarGridSpec(
            num_scalar_prefetch=1,
            grid=(count,),
            in_specs=anywhere * count
            + [pl.BlockSpec(w.shape, lambda i, table: (0, 0), pipeline_mode=pl.Buffered(1))]
            + anywhere * (len(earlier) + len(done)),
            out_specs=[pl.BlockSpec((BLOCK, width), at), pl.BlockSpec((BLOCK, depth), at)],
            scratch_shapes=[pltpu.VMEM((2, BLOCK, depth), BF), pltpu.SemaphoreType.DMA((2,))],
        ),
        out_shape=[
            jax.ShapeDtypeStruct((total * BLOCK, width), BF),
            jax.ShapeDtypeStruct((total * BLOCK, depth), BF),
        ],
        input_output_aliases={count + 2 + i: i for i in range(len(earlier))},
        **arbitrary("in_project"),
    )(jnp.array(places, jnp.int32), *pieces, w, *earlier, *done)


def gate_kernel(*refs, count):
    pieces, (z, w_o, y, gain, dn_out, cot_out, sums, buffer, sems) = refs[:count], refs[count:]
    slot = fetch(pieces, buffer, sems, pl.program_id(0))
    cot = buffer[slot]
    cot_out[...] = cot
    dn = dot(cot, w_o[...], NN)
    dn_out[...] = dn.astype(BF)
    zf = z[...].astype(F32)
    gz = y[...].astype(F32) * (zf * jax.nn.sigmoid(zf))
    ones = jnp.ones((8, gz.shape[1]), BF)
    first = dot(ones, (gz * gz).astype(BF), NT)
    second = dot(ones, (dn * gain[0:1, :] * gz).astype(BF), NT)
    step = pl.program_id(0)
    sums[pl.ds(step, 1), :] = first[0:1]
    sums[pl.ds(count + step, 1), :] = second[0:1]


def gate_forward(pieces, z, w_o, y, gain):
    count = len(pieces)
    depth, width = w_o.shape
    return pl.pallas_call(
        functools.partial(gate_kernel, count=count),
        grid=(count,),
        in_specs=[pl.BlockSpec(memory_space=pl.ANY)] * count + [by_rows(width), fixed(w_o), by_rows(width), fixed(gain)],
        out_specs=[by_rows(width), by_rows(depth), pl.BlockSpec((2 * count, BLOCK), lambda i: (0, 0))],
        out_shape=[
            jax.ShapeDtypeStruct((count * BLOCK, width), BF),
            jax.ShapeDtypeStruct((count * BLOCK, depth), BF),
            jax.ShapeDtypeStruct((2 * count, BLOCK), F32),
        ],
        scratch_shapes=[pltpu.VMEM((2, BLOCK, depth), BF), pltpu.SemaphoreType.DMA((2,))],
        **arbitrary("gate_forward"),
    )(*pieces, z, w_o, y, gain)


def out_kernel(z_in, dn_in, y_in, sums, gain, w_o, normed, dy, dz, dgain, *refs, n, bits):
    step = pl.program_id(0)
    @pl.when(pl.program_id(0) == 0)
    def _():
        dgain[...] = jnp.zeros(dgain.shape, F32)

    scale = lax.rsqrt(sums[pl.ds(step, 1), :] / INNER + NORM_EPS)
    slope = scale * scale * scale * sums[pl.ds(MICRO * n + step, 1), :] / INNER
    row = iota2((LANES, BLOCK), 0)
    columns = jnp.where(row == 0, scale, jnp.where(row == 1, slope, 0.0)).T
    scale, slope = columns[:, 0:1], columns[:, 1:2]
    for lo in range(0, normed.shape[1], 2 * LANES):
        hi = lo + 2 * LANES
        z, y, dn = z_in[:, lo:hi].astype(F32), y_in[:, lo:hi].astype(F32), dn_in[:, lo:hi].astype(F32)
        sig = jax.nn.sigmoid(z)
        silu = z * sig
        gz = y * silu
        unit = gz * scale
        normed[:, lo:hi] = (unit * gain[0:1, lo:hi]).astype(BF)
        dgain[:, lo:hi] += jnp.sum((dn * unit).reshape(BLOCK // 8, 8, 2 * LANES), axis=0)
        d_gz = dn * gain[0:1, lo:hi] * scale - gz * slope
        dy[:, lo:hi] = (d_gz * silu).astype(BF)
        dz[:, lo:hi] = (d_gz * y * (sig + silu * (1.0 - sig))).astype(BF)
    out = dot(normed[...], w_o[...], NT).astype(BF)
    emit(out, refs[:4], refs[4], refs[5], step // n, step % n, bits, step, MICRO * n)


def out_project(z, dn, y, sums, gain, w_o, bits):
    depth, width = w_o.shape
    tokens = z.shape[0]
    n = tokens // BLOCK // MICRO
    one = by_rows(width)
    shapes, places, scratch = emitted(MICRO, n, depth)
    return pl.pallas_call(
        functools.partial(out_kernel, n=n, bits=bits),
        grid=(tokens // BLOCK,),
        in_specs=[one, one, one, fixed(sums), fixed(gain), fixed(w_o)],
        out_specs=[one, one, one, pl.BlockSpec((8, width), lambda i: (0, 0))] + places,
        out_shape=[jax.ShapeDtypeStruct((tokens, width), BF)] * 3 + [jax.ShapeDtypeStruct((8, width), F32)] + shapes,
        scratch_shapes=scratch,
        **arbitrary("out_project"),
    )(z, dn, y, sums, gain, w_o)


def back_kernel(dz, px, w_z, w_x, *refs, n, bits):
    step = pl.program_id(0)
    out = (dot(dz[...], w_z[...], NT) + dot(px[...], w_x[...], NT)).astype(BF)
    emit(out, refs[:4], refs[4], refs[5], 0, step, bits, step, n)


def back_project(micro, dz, px, w_z, w_x, bits):
    tokens, width = px.shape
    depth = w_z.shape[0]
    n = tokens // BLOCK
    shapes, places, scratch = emitted(1, n, depth)
    return pl.pallas_call(
        functools.partial(back_kernel, n=n, bits=bits),
        grid=(n,),
        in_specs=[pl.BlockSpec((BLOCK, dz.shape[1]), lambda i: (micro * n + i, 0)), by_rows(width), fixed(w_z), fixed(w_x)],
        out_specs=places,
        out_shape=shapes,
        scratch_shapes=scratch,
        **arbitrary("back_project"),
    )(dz, px, w_z, w_x)


def shard_kernel(spot, *refs, n, hl):
    fronts, backs, (weight, gain, shard_in, shard_out, last) = refs[:n], refs[n : 2 * n], refs[2 * n :]
    rank, own = spot[0], spot[1]
    width = hl * HEADDIM
    rows = weight.shape[0]
    lane = iota2((rows, LANES), 1)
    square = jnp.zeros((rows, LANES), F32)
    scaled = jnp.zeros((rows, LANES), F32)
    shared = [jnp.zeros((rows, LANES), F32) for _ in range(2 * STATE // LANES + 1)]
    for mask in range(n):
        at = (rank ^ mask) * width
        for lo in range(0, width, LANES):
            spot_z = pl.multiple_of(at + lo, LANES)
            spot_x = pl.multiple_of(INNER + at + lo, LANES)
            out = fronts[mask][:, lo : lo + LANES].astype(F32)
            z = fronts[mask][:, width + lo : width + lo + LANES].astype(F32)
            x = backs[mask][:, lo : lo + LANES].astype(F32)
            shard_out[:, pl.ds(spot_z, LANES)] = out
            shard_in[:, pl.ds(spot_z, LANES)] = z
            shard_in[:, pl.ds(spot_x, LANES)] = x
            square += out * out + z * z + x * x
            scaled += weight[:, pl.ds(spot_z, LANES)].astype(BF).astype(F32) * z
            scaled += weight[:, pl.ds(spot_x, LANES)].astype(BF).astype(F32) * x
        for at_lane in range(2 * STATE // LANES):
            lo = width + at_lane * LANES
            shared[at_lane] += backs[mask][:, lo : lo + LANES].astype(F32)
        steps = jnp.where(lane < hl, backs[mask][:, width + 2 * STATE :].astype(F32), 0.0)
        shared[-1] += pltpu.roll(steps, (rank ^ mask) * hl, 1)
    for at_lane, one in enumerate(shared):
        lo = 2 * INNER + at_lane * LANES
        wide = min(LANES, weight.shape[1] - lo)
        one = one[:, :wide]
        shard_in[:, lo : lo + wide] = one
        square += jnp.concatenate([one * one, jnp.zeros((rows, LANES - wide), F32)], axis=1) if wide < LANES else one * one
        part = weight[:, lo : lo + wide].astype(BF).astype(F32) * one
        scaled += jnp.concatenate([part, jnp.zeros((rows, LANES - wide), F32)], axis=1) if wide < LANES else part
    d_gain = jnp.sum(scaled, axis=1, keepdims=True) / gain[:, 0:1]
    start = own * rows
    line = jnp.sum(jnp.where(lane == start % LANES + iota2((rows, LANES), 0), d_gain, 0.0), axis=0, keepdims=True)
    total = jnp.sum(jnp.sum(square, axis=0, keepdims=True), axis=1, keepdims=True)
    row, col = iota2(last.shape, 0), iota2(last.shape, 1)
    last[...] = jnp.where(row == start // LANES, line, 0.0) + jnp.where((row == D // LANES) & (col == 0), total, 0.0)


def shards(spot, fronts, backs, weight, gain, hl):
    rows = weight.shape[0]
    return pl.pallas_call(
        functools.partial(shard_kernel, n=len(fronts), hl=hl),
        grid_spec=pltpu.PrefetchScalarGridSpec(
            num_scalar_prefetch=1,
            grid=(1,),
            in_specs=[pl.BlockSpec(one.shape, lambda i, spot: (0, 0)) for one in (*fronts, *backs, weight, gain)],
            out_specs=[
                pl.BlockSpec(weight.shape, lambda i, spot: (0, 0)),
                pl.BlockSpec((rows, INNER), lambda i, spot: (0, 0)),
                pl.BlockSpec((D // LANES + 8, LANES), lambda i, spot: (0, 0)),
            ],
        ),
        out_shape=[
            jax.ShapeDtypeStruct(weight.shape, F32),
            jax.ShapeDtypeStruct((rows, INNER), F32),
            jax.ShapeDtypeStruct((D // LANES + 8, LANES), F32),
        ],
        **arbitrary("shards"),
    )(spot, *fronts, *backs, weight, gain)


def small_kernel(conv_0, conv_1, vec_0, vec_1, skip_0, skip_1, gain, out):
    width = gain.shape[1]
    out[...] = jnp.zeros(out.shape, F32)
    for tap in range(CONV + 1):
        rows = slice(tap * 8, tap * 8 + 8)
        out[tap : tap + 1, :] = jnp.sum(conv_0[rows, :] + conv_1[rows, :], axis=0, keepdims=True)
    out[5:6, :width] = jnp.sum(gain[...], axis=0, keepdims=True)
    out[6:7, :width] = jnp.sum(skip_0[...] + skip_1[...], axis=0, keepdims=True)
    vec = vec_0[...] + vec_1[...]
    head, lane = iota2((SLOT, LANES), 0), iota2((SLOT, LANES), 1)
    line = jnp.where(lane == head, vec[:, 0:1], jnp.where(lane == SLOT + head, vec[:, 1:2], 0.0))
    out[7:8, :LANES] = jnp.sum(line, axis=0, keepdims=True)


def small_gradients(*parts):
    return pl.pallas_call(
        small_kernel,
        out_shape=jax.ShapeDtypeStruct((8, parts[0].shape[1]), F32),
        name="small_gradients",
    )(*parts)


def place_kernel(spot, *refs, width):
    *pieces, out = refs
    shared = 0.0
    for mask, piece in enumerate(pieces):
        at = (spot[0] ^ mask) * width
        for lo in range(0, width, LANES):
            out[:, pl.ds(pl.multiple_of(at + lo, LANES), LANES)] = piece[:, lo : lo + LANES]
        shared = shared + piece[:, width:]
    out[:, INNER:] = shared


def place_small(spot, pieces, width):
    return pl.pallas_call(
        functools.partial(place_kernel, width=width),
        grid_spec=pltpu.PrefetchScalarGridSpec(
            num_scalar_prefetch=1,
            grid=(1,),
            in_specs=[pl.BlockSpec(one.shape, lambda i, spot: (0, 0)) for one in pieces],
            out_specs=pl.BlockSpec((8, CH), lambda i, spot: (0, 0)),
        ),
        out_shape=jax.ShapeDtypeStruct((8, CH), F32),
        **arbitrary("place_small"),
    )(spot, *pieces)

def swapped(value, axis, mask):
    return lax.ppermute(value, axis, [(i, i ^ mask) for i in range(lax.axis_size(axis))])


def axis_bits(axis):
    return [1 << i for i in range(lax.axis_size(axis).bit_length() - 1)]


def micro_order(micro, axis):
    bits = axis_bits(axis)
    return bits if micro % 2 == 0 else bits[::-1]


def nothing(*refs):
    pass


def after(values, *done):
    values = list(values)
    anywhere = pl.BlockSpec(memory_space=pl.ANY)
    held = pl.pallas_call(
        nothing,
        in_specs=[anywhere] * (len(values) + len(done)),
        out_specs=[anywhere] * len(values),
        out_shape=[jax.ShapeDtypeStruct(v.shape, v.dtype) for v in values],
        input_output_aliases={at: at for at in range(len(values))},
        name="after",
    )(*values, *done)
    return list(held)


def gather_stages(own):
    held = [{0: own[micro]} for micro in range(MICRO)]
    for turn in range(len(axis_bits("seq"))):
        got = []
        for micro in range(MICRO):
            bit = micro_order(micro, "seq")[turn]
            got.append({at ^ bit: swapped(held[micro][at], "seq", bit) for at in held[micro]})
        wait = yield [piece for one in got for piece in one.values()], [piece for one in held for piece in one.values()]
        for micro in range(MICRO):
            if wait is not None:
                got[micro] = dict(zip(got[micro], after(got[micro].values(), *wait)))
            held[micro].update(got[micro])
    yield [held[micro][at] for micro in range(MICRO) for at in range(len(held[micro]))]


def scatter_stages(parts):
    n = 2 * parts[0].shape[1]
    away, stay = list(parts[0::2]), list(parts[1::2])
    places = [[at for at in range(n) if not at & micro_order(half, "seq")[0]] for half in range(2)]
    join = lambda one, more: (one.astype(F32) + more.astype(F32)).astype(BF)
    pick = lambda a, at: jnp.concatenate([a[:, k : k + 1] for k in at], axis=1)
    turns = len(axis_bits("seq"))
    for turn in range(turns):
        got = [swapped(away[half], "seq", micro_order(half, "seq")[turn]) for half in range(2)]
        wait = yield got, away
        if wait is not None:
            got = after(got, *wait)
        if turn == turns - 1:
            break
        held, away, stay = stay, [], []
        for half in range(2):
            bit = micro_order(half, "seq")[turn + 1]
            leave = [at for at, place in enumerate(places[half]) if place & bit]
            keep = [at for at, place in enumerate(places[half]) if not place & bit]
            away.append(join(pick(held[half], leave), pick(got[half], leave)))
            stay.append(join(pick(held[half], keep), pick(got[half], keep)))
            places[half] = [places[half][at] for at in keep]
    yield jnp.concatenate([join(one, more)[:, 0] for one, more in zip(stay, got)], axis=1), None


def finish(stages, wait=None):
    last = None
    try:
        while True:
            last = stages.send(wait)
    except StopIteration:
        return last[0]


def turned(entries, rank):
    entries = list(entries)
    for bit in axis_bits("seq"):
        flip = (rank & bit) != 0
        entries = [jnp.where(flip, entries[at ^ bit], entries[at]) for at in range(len(entries))]
    return entries


def exchange(entries, rank):
    entries = turned(entries, rank)
    return entries, [swapped(one, "seq", mask) for mask, one in enumerate(entries) if mask]


def sum_pieces(value):
    n = value.shape[-2]
    total = value
    for mask in range(1, n):
        got = swapped(value, "seq", mask)
        total = total + jnp.concatenate([got[..., at ^ mask : (at ^ mask) + 1, :] for at in range(n)], axis=-2)
    return total


def adamw(master, gradient, first, second, clip, decay):
    clipped = gradient * clip
    first_new = BETA_ONE * first + (1.0 - BETA_ONE) * clipped
    second_new = BETA_TWO * second + (1.0 - BETA_TWO) * clipped * clipped
    update = first_new / FIX_ONE / (jnp.sqrt(second_new / FIX_TWO) + ADAM_EPS) + decay * master
    return (-LEARN_RATE * update, first_new, second_new)


def per_device(tokens, cotangent, segments, in_weight, in_m, in_v, conv_weight, conv_m, conv_v,
               out_weight, out_m, out_v, packed, packed_m, packed_v):
    n = lax.axis_size("seq")
    rank = lax.axis_index("seq")
    own = lax.axis_index("dp") * n + rank
    place = rank.astype(jnp.int32).reshape(1)
    ndev = n * lax.axis_size("dp")
    hl = HEADS // n
    xw = hl * HEADDIM
    rows = D // ndev
    piece = tokens.shape[1]
    count = MICRO * n * piece
    xs = INNER + INNER
    bc = 2 * STATE
    xc = xw + bc + LANES
    cw = conv_weight.shape[1]
    conv_cols = -(-(CONV + 1) * cw // rows)

    in_low = in_weight.astype(BF)
    out_low = out_weight.astype(BF).T
    conv_flat = conv_weight.astype(BF).reshape(-1)
    conv_flat = jnp.pad(conv_flat, (0, conv_cols * rows - conv_flat.shape[0])).reshape(rows, conv_cols)
    column = lambda a, q, width: a[:, q * width : (q + 1) * width]
    pad = jnp.zeros((rows, LANES - hl - conv_cols), BF)
    send_x = [
        jnp.concatenate(
            [column(in_low[:, INNER:xs], q, xw), in_low[:, xs : xs + bc], column(in_low[:, xs + bc :], q, hl), conv_flat, pad], axis=1
        )
        for q in range(n)
    ]
    gain_in = packed[3 * HEADS : 3 * HEADS + D]
    send_x = turned(send_x, rank)
    got_wx = [one if not mask else swapped(one, "seq", mask) for mask, one in enumerate(send_x)]
    a_log = lax.dynamic_slice_in_dim(packed, rank * hl, hl)
    skip = lax.dynamic_slice_in_dim(packed, HEADS + rank * hl, hl)
    dt_bias = lax.dynamic_slice_in_dim(packed, 2 * HEADS + rank * hl, hl)
    gain_out = lax.dynamic_slice_in_dim(packed, 3 * HEADS + D + rank * xw, xw)
    aux, masks = segment_aux(segments)
    heads = head_columns(a_log, dt_bias)
    skip = jnp.broadcast_to(jnp.repeat(skip, HEADDIM)[None], (8, xw))

    tok = tokens.astype(F32)
    r_in = lax.rsqrt(jnp.mean(tok * tok, axis=-1, keepdims=True) + NORM_EPS)
    hidden_stages = gather_stages((tok * r_in * gain_in).astype(BF))
    arrived, sent = next(hidden_stages)
    more, _ = hidden_stages.send(None)
    got_wx = jnp.concatenate(turned(got_wx[:1] + after(got_wx[1:], *sent), rank), axis=0)
    w_x = lax.all_gather(got_wx, "dp", axis=0, tiled=True)
    send_zo = jnp.stack(turned([jnp.concatenate([column(in_low, q, xw), column(out_low, q, xw)], axis=1) for q in range(n)], rank))
    [send_zo] = after([send_zo], got_wx, more[0], more[2])
    got_wzo = [send_zo[mask] if not mask else swapped(send_zo[mask], "seq", mask) for mask in range(n)]
    got_wzo = jnp.concatenate(turned(got_wzo, rank), axis=0)
    w_z = lax.all_gather(got_wzo[:, :xw], "dp", axis=0, tiled=True)
    w_o = lax.all_gather(got_wzo[:, xw:], "dp", axis=0, tiled=True)
    conv_full = w_x[:, xw + bc + hl : xw + bc + hl + conv_cols].reshape(ndev, rows * conv_cols)[:, : (CONV + 1) * cw]
    conv_full = conv_full.reshape(ndev, CONV + 1, cw).transpose(1, 0, 2).reshape(CONV + 1, CH)
    conv_loc = jnp.concatenate([lax.dynamic_slice_in_dim(conv_full, rank * xw, xw, 1), conv_full[:, INNER:]], axis=1).astype(F32)
    conv_loc = jnp.pad(conv_loc, ((0, 8 - CONV - 1), (0, 0)))

    for _ in axis_bits("seq")[1:]:
        arrived, more = more, hidden_stages.send(None)
        more = more[0] if isinstance(more, tuple) else more
    late = [micro * n + at for micro in range(MICRO) for at in range(n) if at & (last := micro_order(micro, "seq")[-1]) and at != last]
    soon = [at for at in range(MICRO * n) if at not in late]
    soon.sort(key=lambda at: (at % n).bit_count())
    earlier = in_project([more[at] for at in soon], soon, MICRO * n, w_x, done=(aux, masks, conv_loc))
    late_pieces = after([more[at] for at in late], earlier[0])
    proj_x, hidden = in_project(late_pieces, late, MICRO * n, w_x, earlier)

    cot_stages = gather_stages(after([cotangent[micro] for micro in range(MICRO)], *late_pieces))
    next(cot_stages)
    y, states, act, slope = scan_forward(place, proj_x, conv_loc, skip, heads, aux, masks, hl)
    for bit in axis_bits("seq"):
        cot = cot_stages.send([proj_x] if bit == 1 else [y])
    gain = jnp.broadcast_to(gain_out[None], (8, xw))
    [w_z] = after([w_z], y)
    z = dot(hidden, w_z, NN).astype(BF)
    dn, cot, sums = gate_forward(cot, z, w_o, y, gain)
    sums = sum_pieces(sums.reshape(2, MICRO, n, piece)).reshape(-1, BLOCK)
    first_bits = tuple(micro_order(half, "seq")[0] for half in range(2))
    normed, dy, dz, d_gain_out, *out_part = out_project(z, dn, y, sums, gain, w_o, first_bits)

    scatter = lambda a: lax.psum_scatter(a, "dp", scatter_dimension=0, tiled=True)
    split = lambda a: [a[q * rows : (q + 1) * rows] for q in range(n)]
    out_stages = scatter_stages(out_part)
    next(out_stages)
    part_o = dot(cot, normed, TN).astype(BF)
    part_z = dot(hidden, dz, TN).astype(BF)
    got_o, got_z = scatter(part_o), scatter(part_z)

    through_in = lambda micro, one: back_project(micro, dz, one, w_z, w_x, first_bits)
    scan_back = lambda micro, *done: scan_backward(
        place, micro, proj_x, conv_loc, skip, heads, aux, masks, act, slope, dy, states, hl, *done
    )

    px_0, dco_0, vec_0, skip_0 = scan_back(0, part_o, part_z)
    hid_0 = through_in(0, px_0)
    out_got, out_sent = out_stages.send([hid_0[0]])
    stages_0 = scatter_stages(hid_0)
    hid_got, sent = next(stages_0)
    px_1, dco_1, vec_1, skip_1 = scan_back(1, *sent, *out_sent)
    [px_1] = after([px_1], *hid_got, *out_got)
    part_x = dot(hidden, jnp.concatenate([px_0, px_1], axis=0), TN).astype(BF)
    got_x = scatter(part_x)
    hid_got, sent = stages_0.send([part_x])
    spot = jnp.stack([rank, own]).astype(jnp.int32)
    own_gain = lax.dynamic_slice_in_dim(gain_in, own * rows, rows)[:, None]
    [px_1] = after([px_1], part_x, *sent)
    hid_1 = through_in(1, px_1)
    [got_o, got_z] = after([got_o, got_z], part_x)
    sent_oz, got_oz = exchange(split(jnp.concatenate([got_o, got_z], axis=1)), rank)
    dco_0, dco_1 = after([dco_0, dco_1], hid_1[0], *got_oz)
    conv_0, conv_1 = (tap_gradients(place, micro, proj_x, aux, one) for micro, one in enumerate((dco_0, dco_1)))
    stages_1 = scatter_stages(after(hid_1, *hid_got))
    hid_got, _ = next(stages_1)
    small = small_gradients(conv_0, conv_1, vec_0, vec_1, skip_0, skip_1, d_gain_out)
    [small] = after([small], *hid_got)
    output = (tok + finish(out_stages, [small]).astype(F32)).astype(BF)
    for bit in axis_bits("dp"):
        small = small + swapped(small, "dp", bit)
    _, hid_sent = stages_1.send(None)
    [got_x] = after([got_x], small, output, *hid_sent)
    sent_x, got_x = exchange(split(got_x), rank)
    [small] = after([small], *sent_x)
    small = [small] + after([swapped(small, "seq", mask) for mask in range(1, n)], *got_x)
    small = place_small(spot, small, xw)
    conv_tot, gain_out_tot = small[: CONV + 1], small[5, :INNER]
    skip_tot = jnp.sum(small[6, :INNER].reshape(HEADS, HEADDIM), axis=1)
    by_head = small[7, :INNER].reshape(n, xw)
    a_log_tot, dt_bias_tot = by_head[:, :hl].reshape(-1), by_head[:, SLOT : SLOT + hl].reshape(-1)
    shard_conv = lax.dynamic_slice_in_dim(conv_tot, own * cw, cw, 1)
    conv_sq = jnp.sum(conv_tot * conv_tot)
    shard_in, shard_out, last = shards(spot, sent_oz[:1] + got_oz, sent_x[:1] + got_x, in_weight, own_gain, hl)
    shard_out = shard_out.T
    d_hidden = jnp.concatenate([finish(stages_0, [hid_1[0]]), finish(stages_1, got_x)], axis=0).astype(F32)
    dh = d_hidden * gain_in
    d_tok = r_in * (dh - tok * (r_in * r_in) * jnp.mean(dh * tok, axis=-1, keepdims=True))
    input_grad = (cotangent.astype(F32) + d_tok).astype(BF)

    stages = [(axis, bit) for axis in ("seq", "dp") for bit in axis_bits(axis)]
    for axis, bit in stages:
        last = last + swapped(last, axis, bit)
    vec_tot = jnp.concatenate([a_log_tot, skip_tot, dt_bias_tot, last[: D // LANES].reshape(-1), gain_out_tot])
    grad_norm = jnp.sqrt(last[D // LANES, 0] + conv_sq + jnp.sum(vec_tot * vec_tot))
    clip = jnp.minimum(1.0, CLIP_NORM / (grad_norm + 1e-06))
    in_new = adamw(in_weight, shard_in, in_m, in_v, clip, WEIGHT_DECAY)
    conv_new = adamw(conv_weight, shard_conv, conv_m, conv_v, clip, WEIGHT_DECAY)
    out_new = adamw(out_weight, shard_out, out_m, out_v, clip, WEIGHT_DECAY)
    vec_new = adamw(packed, vec_tot, packed_m, packed_v, clip, 0.0)
    return (
        output, input_grad, grad_norm,
        in_weight + in_new[0], in_new[1], in_new[2],
        conv_new[0], conv_new[1], conv_new[2],
        out_weight + out_new[0], out_new[1], out_new[2],
        vec_new[0], vec_new[1], vec_new[2],
    )


def solution(mesh):
    tok, col, row = P(None, ALL, None), P(None, ALL), P(ALL, None)
    return jax.shard_map(
        per_device,
        mesh=mesh,
        in_specs=(tok, tok, P(None, "dp"), row, row, row, col, col, col, col, col, col, P(), P(), P()),
        out_specs=(tok, tok, P(), row, row, row, col, col, col, col, col, col, P(), P(), P()),
        check_vma=False,
    )
```

```python
import functools

import jax
import jax.numpy as jnp
from jax import lax
from jax.experimental import pallas as pl
from jax.experimental.pallas import tpu as pltpu
from jax.sharding import PartitionSpec as P

D = 2048
HEADS = 64
HEADDIM = 64
STATE = 128
CONV = 4
BLOCK = 256
MICRO = 2
INNER = 4096
CH = 4352
NORM_EPS = 1e-05
LEARN_RATE = 0.004
BETA_ONE = 0.9
BETA_TWO = 0.95
FIX_ONE = 1.0 - 0.9**10
FIX_TWO = 1.0 - 0.95**10
ADAM_EPS = 1e-08
WEIGHT_DECAY = 0.1
CLIP_NORM = 1.0
BF = jnp.bfloat16
F32 = jnp.float32
ALL = ("dp", "seq")


def dot(a, b, dims, out=F32):
    return lax.dot_general(a, b, (dims, ((), ())), preferred_element_type=out)


NN = ((1,), (0,))
NT = ((1,), (1,))
TN = ((0,), (0,))
LANES = 128
PAIR = 2 * HEADDIM
VMEM = 56 * 1024 * 1024
SLOT = 16
TINY = 1e-37
CAP = 85.0


def iota2(shape, dim):
    return lax.broadcasted_iota(jnp.int32, shape, dim)


def tree(value, rows=8):
    while value.shape[0] > rows:
        half = value.shape[0] // 2
        value = value[:half] + value[half:]
    return value


def thirds(value):
    high = value.astype(BF).astype(F32)
    rest = value - high
    mid = rest.astype(BF).astype(F32)
    return high, mid, (rest - mid).astype(BF).astype(F32)


def running_sum(values, reverse):
    row, col = iota2((BLOCK, BLOCK), 0), iota2((BLOCK, BLOCK), 1)
    ones = jnp.where(row >= col if reverse else row <= col, 1.0, 0.0).astype(BF)
    sums = dot(jnp.concatenate(thirds(values), axis=0).astype(BF), ones, NN)
    return sums[:SLOT] + sums[SLOT : 2 * SLOT] + sums[2 * SLOT :]


def step_rows(raw, heads, masks):
    lifted = raw.astype(F32).T[:SLOT] + heads[:, 0:1]
    dt = jnp.maximum(lifted, 0.0) + jnp.log1p(jnp.exp(-jnp.abs(lifted)))
    cum = running_sum(dt * heads[:, 1:2], False)
    entry = jnp.exp(cum) * masks[1:2, :]
    dt_end = dt * jnp.exp(cum[:, BLOCK - 1 : BLOCK] - cum) * masks[2:3, :]
    return lifted, dt, cum, entry, dt_end


def two(value):
    high = value.astype(BF).astype(F32)
    return [high, value - high]


def as_columns(gap_rows, entry, dt_end):
    ones = jnp.where(iota2((SLOT, BLOCK), 0) < 3, 1.0, 0.0)
    return jnp.concatenate([*thirds(gap_rows), ones, *two(entry), *two(dt_end)], axis=0).T.astype(BF)


def gap_right_init(right, hl):
    row = iota2((3 * SLOT, BLOCK), 0)
    for h in range(hl):
        right[0 : 3 * SLOT, h * BLOCK : (h + 1) * BLOCK] = jnp.where((row & (SLOT - 1)) == h, 1.0, 0.0).astype(BF)


def gap_right_fill(right, values, hl):
    row = iota2((SLOT, BLOCK), 0)
    high, mid, low = thirds(values)
    for h in range(hl):
        one = slice(h, h + 1)
        slab = jnp.where(row == 0, high[one], jnp.where(row == 1, mid[one], jnp.where(row == 2, low[one], 0.0)))
        right[3 * SLOT :, h * BLOCK : (h + 1) * BLOCK] = slab.astype(BF)


def head_spread_init(spreads, hl):
    row, col = iota2(spreads.shape, 0), iota2(spreads.shape, 1)
    head = jnp.where(col < hl * HEADDIM, col, col - hl * HEADDIM) // HEADDIM
    slot = jnp.where(col < hl * HEADDIM, 2, 3)
    spreads[...] = jnp.where(((row & (SLOT - 1)) == head) & (row // (2 * SLOT) == slot), 1.0, 0.0).astype(BF)


def stacked(left, pair_values):
    zero = jnp.zeros_like(pair_values)
    return jnp.concatenate([jnp.where(left, pair_values, zero), jnp.where(left, zero, pair_values)], axis=0)


def conv_chunk(window, conv_w, valid, lo, hi):
    out = conv_w[CONV : CONV + 1, lo:hi] + conv_w[CONV - 1 : CONV, lo:hi] * window[8 : 8 + BLOCK, lo:hi]
    for tap in range(CONV - 1):
        out += conv_w[tap : tap + 1, lo:hi] * (window[5 + tap : 5 + tap + BLOCK, lo:hi] * valid[tap])
    return out


def spread(aux_v, at):
    return jnp.broadcast_to(aux_v[:, at : at + 1], (BLOCK, LANES))


def forward_kernel(place, proj, conv_w, skip, heads, aux, masks, y_out, s_out, act, slope, window, state, right, carried, spreads, *, hl):
    width = hl * HEADDIM
    conv_width = width + 2 * STATE

    @pl.when(pl.program_id(1) == 0)
    def _():
        window[0:8, :] = jnp.zeros((8, conv_width), F32)
        state[...] = jnp.zeros(state.shape, F32)
        gap_right_init(right, hl)
        head_spread_init(spreads, hl)

    aux_v = aux[...]
    valid = [spread(aux_v, tap) for tap in range(CONV - 1)]
    for lo in range(0, conv_width, LANES):
        hi = lo + LANES
        window[8 : 8 + BLOCK, lo:hi] = proj[:, lo:hi].astype(F32)
        out = conv_chunk(window, conv_w, valid, lo, hi)
        sig = jax.nn.sigmoid(out)
        silu = out * sig
        act[:, lo:hi] = silu.astype(BF)
        slope[:, lo:hi] = (sig + silu * (1.0 - sig)).astype(BF)
    window[0:8, :] = window[BLOCK : BLOCK + 8, :]

    _, dt, cum, entry, dt_end = step_rows(proj[:, conv_width : conv_width + LANES], heads[...], masks)
    columns = as_columns(cum, entry, dt_end)
    gaps = columns[:, : 4 * SLOT]
    gap_right_fill(right, jnp.log(jnp.maximum(dt, TINY)) - cum, hl)
    bm, cm = act[:, width : width + STATE], act[:, width + STATE :]
    same = (aux_v[:, 3:4] == masks[0:1, :]) & (iota2((BLOCK, BLOCK), 0) >= iota2((BLOCK, BLOCK), 1))
    inner = jnp.where(same, dot(cm, bm, NT), 0.0)
    left = iota2((BLOCK, PAIR), 1) < HEADDIM
    top = iota2((PAIR, STATE), 0) < HEADDIM
    last = entry[:, BLOCK - 1 : BLOCK]
    s_out[0] = state[...].astype(BF)
    carried[...] = dot(columns, spreads[...], NN)
    carried[:, :width] = carried[:, :width] * dot(cm, s_out[0], NT)
    for pair in range(hl // 2):
        first = 2 * pair
        lo, hi = pair * PAIR, (pair + 1) * PAIR
        xp = act[:, lo:hi]
        mix = []
        for h in (first, first + 1):
            decay = jnp.exp(jnp.minimum(dot(gaps, right[:, h * BLOCK : (h + 1) * BLOCK], NN), CAP))
            mix.append((inner * decay).astype(BF))
        xf = xp.astype(F32)
        y = dot(jnp.concatenate(mix, axis=1), stacked(left, xp), NN)
        y += carried[:, lo:hi] + skip[0:1, lo:hi] * xf
        y_out[:, lo:hi] = y.astype(BF)
        weighted = (xf * carried[:, width + lo : width + hi]).astype(BF)
        keep = jnp.where(top, last[first : first + 1], last[first + 1 : first + 2])
        state[lo:hi, :] = keep * state[lo:hi, :] + dot(weighted, bm, TN)


def backward_kernel(place, proj, conv_w, skip, heads, aux, masks, act, slope, dy, s_in, *refs, hl):
    dproj, dco, dvec, dskip, dwin, grad_s, dcb, colsum, dkeep, right, carried, later_w, spreads, picks, sums, used, into = refs[-17:]
    width = hl * HEADDIM
    conv_width = width + 2 * STATE

    @pl.when(pl.program_id(0) == 0)
    def _():
        dvec[...] = jnp.zeros(dvec.shape, F32)
        dskip[...] = jnp.zeros(dskip.shape, F32)
        dwin[BLOCK : BLOCK + 8, :] = jnp.zeros((8, conv_width), F32)
        grad_s[...] = jnp.zeros(grad_s.shape, F32)
        colsum[...] = jnp.zeros(colsum.shape, F32)
        dkeep[...] = jnp.zeros(dkeep.shape, F32)
        gap_right_init(right, hl)
        head_spread_init(spreads, hl)
        picks[...] = jnp.where(iota2(picks.shape, 0) == iota2(picks.shape, 1) // BLOCK, 1.0, 0.0).astype(BF)
        sums[...] = jnp.where(iota2(sums.shape, 0) == iota2(sums.shape, 1) // HEADDIM, 1.0, 0.0).astype(BF)

    aux_v = aux[...]
    lifted, dt, cum, entry, dt_end = step_rows(proj[:, conv_width : conv_width + LANES], heads[...], masks)
    a_neg = heads[:, 1:2]
    columns = as_columns(jnp.log(jnp.maximum(dt, TINY)) - cum, entry, dt_end)
    gaps = columns[:, : 4 * SLOT]
    gap_right_fill(right, cum, hl)
    bm, cm = act[:, width : width + STATE], act[:, width + STATE :]
    same = (aux_v[:, 3:4] == masks[0:1, :]) & (iota2((BLOCK, BLOCK), 0) <= iota2((BLOCK, BLOCK), 1))
    inner = jnp.where(same, dot(bm, cm, NT), 0.0)
    left = iota2((BLOCK, PAIR), 1) < HEADDIM
    top = iota2((PAIR, STATE), 0) < HEADDIM
    last = entry[:, BLOCK - 1 : BLOCK]
    d_row = jnp.zeros((SLOT, BLOCK), F32)
    d_b = jnp.zeros((BLOCK, STATE), F32)
    d_c = jnp.zeros((BLOCK, STATE), F32)
    spreaded = dot(columns, spreads[...], NN)
    carried[...] = spreaded
    later_w[:, :width] = dot(cm, s_in[0], NT)
    later_w[:, width:] = dot(bm, grad_s[...].astype(BF), NT)

    for pair in range(hl // 2):
        first = 2 * pair
        lo, hi = pair * PAIR, (pair + 1) * PAIR
        xp, dyp = act[:, lo:hi], dy[:, lo:hi]
        xf, dyf = xp.astype(F32), dyp.astype(F32)
        d_mix = dot(stacked(left, xp), dyp, NT)
        mix, pairwise = [], []
        d_inner = 0.0
        for at, h in enumerate((first, first + 1)):
            decay = jnp.exp(jnp.minimum(dot(gaps, right[:, h * BLOCK : (h + 1) * BLOCK], NN), CAP))
            mix.append((inner * decay).astype(BF))
            part = d_mix[at * BLOCK : (at + 1) * BLOCK] * decay
            d_inner += part
            part = (part * inner).astype(BF)
            pairwise.append(part)
            colsum[h : h + 1, :] = jnp.sum(tree(part.astype(F32)), axis=0, keepdims=True)
        d_row += dot(picks[:, first * BLOCK : (first + 2) * BLOCK], jnp.concatenate(pairwise, axis=1), NT)
        if pair == 0:
            dcb[...] = d_inner
        else:
            dcb[...] += d_inner
        later = grad_s[lo:hi, :]
        low = s_in[0, lo:hi, :]
        end_p = carried[:, width + lo : width + hi]
        from_end = later_w[:, width + lo : width + hi] * end_p
        dx = dot(jnp.concatenate(mix, axis=1), stacked(left, dyp), NN) + from_end + skip[0:1, lo:hi] * dyf
        dwin[0:BLOCK, lo:hi] = slope[:, lo:hi].astype(F32) * dx
        used[:, lo:hi] = (from_end * xf).astype(BF)
        entering = carried[:, lo:hi] * dyf
        into[:, lo:hi] = (entering * later_w[:, lo:hi]).astype(BF)
        entering = entering.astype(BF)
        dskip[:, lo:hi] += tree(xf * dyf)
        kept = later * low.astype(F32)
        dkeep[first : first + 1, :] = jnp.sum(tree(kept[:HEADDIM]), axis=0, keepdims=True)
        dkeep[first + 1 : first + 2, :] = jnp.sum(tree(kept[HEADDIM:]), axis=0, keepdims=True)
        weighted = (xf * end_p).astype(BF)
        d_b += dot(weighted, later.astype(BF), NN)
        d_c += dot(entering, low, NN)
        keep = jnp.where(top, last[first : first + 1], last[first + 1 : first + 2])
        grad_s[lo:hi, :] = dot(entering, cm, TN) + keep * later

    d_inner = jnp.where(same, dcb[...], 0.0).astype(BF)
    d_b += dot(d_inner, cm, NN)
    d_c += dot(d_inner, bm, TN)
    dwin[0:BLOCK, width : width + STATE] = slope[:, width : width + STATE].astype(F32) * d_b
    dwin[0:BLOCK, width + STATE :] = slope[:, width + STATE :].astype(F32) * d_c

    d_end = dot(sums[...], used[...], NT)
    through = d_row + d_end
    d_last = jnp.sum(d_end, axis=1, keepdims=True) + jnp.sum(dkeep[...], axis=1, keepdims=True) * last
    d_cum = dot(sums[...], into[...], NT) + colsum[...] - through
    d_cum += jnp.where(iota2((SLOT, BLOCK), 1) == BLOCK - 1, d_last, 0.0)
    d_a = running_sum(d_cum, True)
    sig = jax.nn.sigmoid(lifted)
    d_raw = through * jnp.where(dt > TINY, sig / jnp.maximum(dt, TINY), 1.0) + d_a * a_neg * sig
    d_raw = jnp.where(iota2((SLOT, BLOCK), 0) < hl, d_raw, 0.0)
    dproj[:, conv_width : conv_width + LANES] = jnp.concatenate([d_raw, jnp.zeros((LANES - SLOT, BLOCK), F32)], axis=0).T.astype(BF)
    lane = iota2((SLOT, LANES), 1)
    d_log = jnp.sum(d_a * dt, axis=1, keepdims=True) * a_neg
    dvec[...] += jnp.where(lane == 0, d_log, jnp.where(lane == 1, jnp.sum(d_raw, axis=1, keepdims=True), 0.0))

    valid = [spread(aux_v, 4 + tap) for tap in range(CONV - 1)]
    for lo in range(0, conv_width, LANES):
        hi = lo + LANES
        own = dwin[0:BLOCK, lo:hi]
        dco[:, lo:hi] = own.astype(BF)
        grad = conv_w[CONV - 1 : CONV, lo:hi] * own
        for tap in range(CONV - 1):
            ahead = CONV - 1 - tap
            grad += conv_w[tap : tap + 1, lo:hi] * (dwin[ahead : ahead + BLOCK, lo:hi] * valid[tap])
        dproj[:, lo:hi] = grad.astype(BF)
    dwin[BLOCK : BLOCK + 8, :] = dwin[0:8, :]


def taps_kernel(place, proj, aux, dco, dconv, dwin):
    conv_width = dco.shape[1]

    @pl.when(pl.program_id(0) == 0)
    def _():
        dconv[...] = jnp.zeros(dconv.shape, F32)
        dwin[BLOCK : BLOCK + 8, :] = jnp.zeros((8, conv_width), F32)

    aux_v = aux[...]
    valid = [spread(aux_v, 4 + tap) for tap in range(CONV - 1)]
    for lo in range(0, conv_width, LANES):
        hi = lo + LANES
        own = dco[:, lo:hi].astype(F32)
        dwin[0:BLOCK, lo:hi] = own
        value = proj[:, lo:hi].astype(F32)
        dconv[CONV * 8 : CONV * 8 + 8, lo:hi] += tree(own)
        dconv[(CONV - 1) * 8 : CONV * 8, lo:hi] += tree(own * value)
        for tap in range(CONV - 1):
            ahead = CONV - 1 - tap
            moved = dwin[ahead : ahead + BLOCK, lo:hi] * valid[tap]
            dconv[tap * 8 : tap * 8 + 8, lo:hi] += tree(moved * value)
    dwin[BLOCK : BLOCK + 8, :] = dwin[0:8, :]


def segment_aux(segments):
    micro, length = segments.shape
    nb = length // BLOCK
    seg = segments.astype(F32)
    blocks = seg.reshape(micro, nb, BLOCK)
    prev = jnp.concatenate([jnp.full((micro, 1), -1.0, F32), blocks[:, :-1, -1]], axis=1)
    reach = range(CONV - 1, 0, -1)
    earlier = [jnp.pad(seg, ((0, 0), (by, 0)), constant_values=-1.0)[:, :length] == seg for by in reach]
    later = [jnp.pad(seg, ((0, 0), (0, by)), constant_values=-1.0)[:, by:] == seg for by in reach]
    columns = [c.astype(F32) for c in (*earlier, seg, *later, jnp.zeros_like(seg))]
    aux = jnp.stack(columns, axis=-1).reshape(micro * length, 8)
    zero = jnp.zeros_like(blocks)
    masks = [blocks, blocks == prev[:, :, None], blocks == blocks[:, :, -1:]] + [zero] * 5
    return aux, jnp.stack([m.astype(F32) for m in masks], axis=2).reshape(micro * nb * 8, BLOCK)


def head_columns(a_log, dt_bias):
    hl = a_log.shape[0]
    both = jnp.stack([dt_bias, -jnp.exp(a_log)], axis=1)
    return jnp.pad(both, ((0, SLOT - hl), (0, LANES - 2)))


def scan_forward(place, proj, conv_w, skip, heads, aux, masks, hl):
    tokens = proj.shape[0]
    nb = tokens // MICRO // BLOCK
    width = hl * HEADDIM
    conv_width = width + 2 * STATE
    held = lambda m, j, place: (m * nb + (j ^ place[0]), 0)
    at = lambda m, j, place: (m * nb + j, 0)
    whole = lambda m, j, place: (0, 0)
    grid_spec = pltpu.PrefetchScalarGridSpec(
        num_scalar_prefetch=1,
        grid=(MICRO, nb),
        in_specs=[
            pl.BlockSpec((BLOCK, conv_width + LANES), held),
            pl.BlockSpec((8, conv_width), whole),
            pl.BlockSpec(skip.shape, whole),
            pl.BlockSpec(heads.shape, whole),
            pl.BlockSpec((BLOCK, 8), at),
            pl.BlockSpec((8, BLOCK), at),
        ],
        out_specs=[
            pl.BlockSpec((BLOCK, width), held),
            pl.BlockSpec((1, width, STATE), lambda m, j, place: (m * nb + j, 0, 0)),
            pl.BlockSpec((BLOCK, conv_width), held),
            pl.BlockSpec((BLOCK, conv_width), held),
        ],
        scratch_shapes=[
            pltpu.VMEM((BLOCK + 8, conv_width), F32),
            pltpu.VMEM((width, STATE), F32),
            pltpu.VMEM((4 * SLOT, hl * BLOCK), BF),
            pltpu.VMEM((BLOCK, 2 * width), F32),
            pltpu.VMEM((LANES, 2 * width), BF),
        ],
    )
    return pl.pallas_call(
        functools.partial(forward_kernel, hl=hl),
        grid_spec=grid_spec,
        out_shape=[
            jax.ShapeDtypeStruct((tokens, width), BF),
            jax.ShapeDtypeStruct((MICRO * nb, width, STATE), BF),
            jax.ShapeDtypeStruct((tokens, conv_width), BF),
            jax.ShapeDtypeStruct((tokens, conv_width), BF),
        ],
        compiler_params=pltpu.CompilerParams(vmem_limit_bytes=VMEM, dimension_semantics=("arbitrary", "arbitrary")),
        name="scan_forward",
    )(place, proj, conv_w, skip, heads, aux, masks)


def scan_backward(place, micro, proj, conv_w, skip, heads, aux, masks, act, slope, dy, states, hl, *done):
    tokens = proj.shape[0] // MICRO
    nb = tokens // BLOCK
    width = hl * HEADDIM
    conv_width = width + 2 * STATE
    full = conv_width + LANES
    first = micro * nb
    held = lambda j, place: (first + ((nb - 1 - j) ^ place[0]), 0)
    at = lambda j, place: (first + nb - 1 - j, 0)
    whole = lambda j, place: (0, 0)
    grid_spec = pltpu.PrefetchScalarGridSpec(
        num_scalar_prefetch=1,
        grid=(nb,),
        in_specs=[
            pl.BlockSpec((BLOCK, full), held),
            pl.BlockSpec((8, conv_width), whole),
            pl.BlockSpec(skip.shape, whole),
            pl.BlockSpec(heads.shape, whole),
            pl.BlockSpec((BLOCK, 8), at),
            pl.BlockSpec((8, BLOCK), at),
            pl.BlockSpec((BLOCK, conv_width), held),
            pl.BlockSpec((BLOCK, conv_width), held),
            pl.BlockSpec((BLOCK, width), held),
            pl.BlockSpec((1, width, STATE), lambda j, place: (first + nb - 1 - j, 0, 0)),
        ]
        + [pl.BlockSpec(memory_space=pl.ANY)] * len(done),
        out_specs=[
            pl.BlockSpec((BLOCK, full), lambda j, place: ((nb - 1 - j) ^ place[0], 0)),
            pl.BlockSpec((BLOCK, conv_width), lambda j, place: ((nb - 1 - j) ^ place[0], 0)),
            pl.BlockSpec((SLOT, LANES), whole),
            pl.BlockSpec((8, width), whole),
        ],
        scratch_shapes=[
            pltpu.VMEM((BLOCK + 8, conv_width), F32),
            pltpu.VMEM((width, STATE), F32),
            pltpu.VMEM((BLOCK, BLOCK), F32),
            pltpu.VMEM((SLOT, BLOCK), F32),
            pltpu.VMEM((SLOT, STATE), F32),
            pltpu.VMEM((4 * SLOT, hl * BLOCK), BF),
            pltpu.VMEM((BLOCK, 2 * width), F32),
            pltpu.VMEM((BLOCK, 2 * width), F32),
            pltpu.VMEM((LANES, 2 * width), BF),
            pltpu.VMEM((SLOT, hl * BLOCK), BF),
            pltpu.VMEM((SLOT, width), BF),
            pltpu.VMEM((BLOCK, width), BF),
            pltpu.VMEM((BLOCK, width), BF),
        ],
    )
    return pl.pallas_call(
        functools.partial(backward_kernel, hl=hl),
        grid_spec=grid_spec,
        out_shape=[
            jax.ShapeDtypeStruct((tokens, full), BF),
            jax.ShapeDtypeStruct((tokens, conv_width), BF),
            jax.ShapeDtypeStruct((SLOT, LANES), F32),
            jax.ShapeDtypeStruct((8, width), F32),
        ],
        compiler_params=pltpu.CompilerParams(vmem_limit_bytes=VMEM, dimension_semantics=("arbitrary",)),
        name="scan_backward",
    )(place, proj, conv_w, skip, heads, aux, masks, act, slope, dy, states, *done)


def tap_gradients(place, micro, proj, aux, dco):
    tokens, conv_width = dco.shape
    nb = tokens // BLOCK
    grid_spec = pltpu.PrefetchScalarGridSpec(
        num_scalar_prefetch=1,
        grid=(nb,),
        in_specs=[
            pl.BlockSpec((BLOCK, proj.shape[1]), lambda j, place: (micro * nb + ((nb - 1 - j) ^ place[0]), 0)),
            pl.BlockSpec((BLOCK, 8), lambda j, place: (micro * nb + nb - 1 - j, 0)),
            pl.BlockSpec((BLOCK, conv_width), lambda j, place: ((nb - 1 - j) ^ place[0], 0)),
        ],
        out_specs=pl.BlockSpec((8 * (CONV + 1), conv_width), lambda j, place: (0, 0)),
        scratch_shapes=[pltpu.VMEM((BLOCK + 8, conv_width), F32)],
    )
    return pl.pallas_call(
        taps_kernel,
        grid_spec=grid_spec,
        out_shape=jax.ShapeDtypeStruct((8 * (CONV + 1), conv_width), F32),
        compiler_params=pltpu.CompilerParams(vmem_limit_bytes=VMEM, dimension_semantics=("arbitrary",)),
        name="tap_gradients",
    )(place, proj, aux, dco)


def fetch(pieces, buffer, sems, step):
    @pl.when(step == 0)
    def _():
        pltpu.make_async_copy(pieces[0], buffer.at[0], sems.at[0]).start()

    for at in range(1, len(pieces)):

        @pl.when(step == at - 1)
        def _():
            pltpu.make_async_copy(pieces[at], buffer.at[at % 2], sems.at[at % 2]).start()

    slot = step % 2
    pltpu.make_async_copy(pieces[0], buffer.at[slot], sems.at[slot]).wait()
    return slot


def emit(value, targets, buffer, sems, micro, place, bits, step, steps):
    slot = step % 2
    rows = value.shape[0] // 2

    def waiting(at):
        for half in range(2):
            pltpu.make_async_copy(buffer.at[at, pl.ds(half * rows, rows)], targets[0].at[0, 0], sems.at[at, half]).wait()

    @pl.when(step >= 2)
    def _():
        waiting(slot)

    buffer[slot] = value
    for half, bit in enumerate(bits):
        index = place // (2 * bit) * bit + place % bit
        set_ = (place // bit) % 2
        for target, wanted in ((targets[2 * half], 1), (targets[2 * half + 1], 0)):

            @pl.when(set_ == wanted)
            def _():
                pltpu.make_async_copy(
                    buffer.at[slot, pl.ds(half * rows, rows)], target.at[micro, index], sems.at[slot, half]
                ).start()

    @pl.when(step == steps - 1)
    def _():
        waiting(0)
        waiting(1)


def emitted(some, n, depth):
    shapes = [jax.ShapeDtypeStruct((some, n // 2, BLOCK // 2, depth), BF)] * 4
    return shapes, [pl.BlockSpec(memory_space=pl.ANY)] * 4, [pltpu.VMEM((2, BLOCK, depth), BF), pltpu.SemaphoreType.DMA((2, 2))]


def fixed(array):
    return pl.BlockSpec(array.shape, lambda i: (0, 0), pipeline_mode=pl.Buffered(1))


def by_rows(width):
    return pl.BlockSpec((BLOCK, width), lambda i: (i, 0))


def arbitrary(name):
    return dict(compiler_params=pltpu.CompilerParams(vmem_limit_bytes=VMEM, dimension_semantics=("arbitrary",)), name=name)


def in_kernel(*refs, count):
    pieces, w, (proj, hidden, buffer, sems) = refs[1 : count + 1], refs[count + 1], refs[-4:]
    slot = fetch(pieces, buffer, sems, pl.program_id(0))
    value = buffer[slot]
    hidden[...] = value
    proj[...] = dot(value, w[...], NN).astype(BF)


def in_project(pieces, places, total, w, earlier=(), done=()):
    count = len(pieces)
    depth, width = w.shape
    anywhere = [pl.BlockSpec(memory_space=pl.ANY)]
    at = lambda i, table: (table[i], 0)
    return pl.pallas_call(
        functools.partial(in_kernel, count=count),
        grid_spec=pltpu.PrefetchScalarGridSpec(
            num_scalar_prefetch=1,
            grid=(count,),
            in_specs=anywhere * count
            + [pl.BlockSpec(w.shape, lambda i, table: (0, 0), pipeline_mode=pl.Buffered(1))]
            + anywhere * (len(earlier) + len(done)),
            out_specs=[pl.BlockSpec((BLOCK, width), at), pl.BlockSpec((BLOCK, depth), at)],
            scratch_shapes=[pltpu.VMEM((2, BLOCK, depth), BF), pltpu.SemaphoreType.DMA((2,))],
        ),
        out_shape=[
            jax.ShapeDtypeStruct((total * BLOCK, width), BF),
            jax.ShapeDtypeStruct((total * BLOCK, depth), BF),
        ],
        input_output_aliases={count + 2 + i: i for i in range(len(earlier))},
        **arbitrary("in_project"),
    )(jnp.array(places, jnp.int32), *pieces, w, *earlier, *done)


def gate_kernel(*refs, count):
    pieces, (z, w_o, y, gain, dn_out, cot_out, sums, buffer, sems) = refs[:count], refs[count:]
    slot = fetch(pieces, buffer, sems, pl.program_id(0))
    cot = buffer[slot]
    cot_out[...] = cot
    dn = dot(cot, w_o[...], NN)
    dn_out[...] = dn.astype(BF)
    zf = z[...].astype(F32)
    gz = y[...].astype(F32) * (zf * jax.nn.sigmoid(zf))
    ones = jnp.ones((8, gz.shape[1]), BF)
    first = dot(ones, (gz * gz).astype(BF), NT)
    second = dot(ones, (dn * gain[0:1, :] * gz).astype(BF), NT)
    step = pl.program_id(0)
    sums[pl.ds(step, 1), :] = first[0:1]
    sums[pl.ds(count + step, 1), :] = second[0:1]


def gate_forward(pieces, z, w_o, y, gain):
    count = len(pieces)
    depth, width = w_o.shape
    return pl.pallas_call(
        functools.partial(gate_kernel, count=count),
        grid=(count,),
        in_specs=[pl.BlockSpec(memory_space=pl.ANY)] * count + [by_rows(width), fixed(w_o), by_rows(width), fixed(gain)],
        out_specs=[by_rows(width), by_rows(depth), pl.BlockSpec((2 * count, BLOCK), lambda i: (0, 0))],
        out_shape=[
            jax.ShapeDtypeStruct((count * BLOCK, width), BF),
            jax.ShapeDtypeStruct((count * BLOCK, depth), BF),
            jax.ShapeDtypeStruct((2 * count, BLOCK), F32),
        ],
        scratch_shapes=[pltpu.VMEM((2, BLOCK, depth), BF), pltpu.SemaphoreType.DMA((2,))],
        **arbitrary("gate_forward"),
    )(*pieces, z, w_o, y, gain)


def out_kernel(z_in, dn_in, y_in, sums, gain, w_o, normed, dy, dz, dgain, *refs, n, bits):
    step = pl.program_id(0)
    @pl.when(pl.program_id(0) == 0)
    def _():
        dgain[...] = jnp.zeros(dgain.shape, F32)

    scale = lax.rsqrt(sums[pl.ds(step, 1), :] / INNER + NORM_EPS)
    slope = scale * scale * scale * sums[pl.ds(MICRO * n + step, 1), :] / INNER
    row = iota2((LANES, BLOCK), 0)
    columns = jnp.where(row == 0, scale, jnp.where(row == 1, slope, 0.0)).T
    scale, slope = columns[:, 0:1], columns[:, 1:2]
    for lo in range(0, normed.shape[1], 2 * LANES):
        hi = lo + 2 * LANES
        z, y, dn = z_in[:, lo:hi].astype(F32), y_in[:, lo:hi].astype(F32), dn_in[:, lo:hi].astype(F32)
        sig = jax.nn.sigmoid(z)
        silu = z * sig
        gz = y * silu
        unit = gz * scale
        normed[:, lo:hi] = (unit * gain[0:1, lo:hi]).astype(BF)
        dgain[:, lo:hi] += jnp.sum((dn * unit).reshape(BLOCK // 8, 8, 2 * LANES), axis=0)
        d_gz = dn * gain[0:1, lo:hi] * scale - gz * slope
        dy[:, lo:hi] = (d_gz * silu).astype(BF)
        dz[:, lo:hi] = (d_gz * y * (sig + silu * (1.0 - sig))).astype(BF)
    out = dot(normed[...], w_o[...], NT).astype(BF)
    emit(out, refs[:4], refs[4], refs[5], step // n, step % n, bits, step, MICRO * n)


def out_project(z, dn, y, sums, gain, w_o, bits):
    depth, width = w_o.shape
    tokens = z.shape[0]
    n = tokens // BLOCK // MICRO
    one = by_rows(width)
    shapes, places, scratch = emitted(MICRO, n, depth)
    return pl.pallas_call(
        functools.partial(out_kernel, n=n, bits=bits),
        grid=(tokens // BLOCK,),
        in_specs=[one, one, one, fixed(sums), fixed(gain), fixed(w_o)],
        out_specs=[one, one, one, pl.BlockSpec((8, width), lambda i: (0, 0))] + places,
        out_shape=[jax.ShapeDtypeStruct((tokens, width), BF)] * 3 + [jax.ShapeDtypeStruct((8, width), F32)] + shapes,
        scratch_shapes=scratch,
        **arbitrary("out_project"),
    )(z, dn, y, sums, gain, w_o)


def back_kernel(dz, px, w_z, w_x, *refs, n, bits):
    step = pl.program_id(0)
    out = (dot(dz[...], w_z[...], NT) + dot(px[...], w_x[...], NT)).astype(BF)
    emit(out, refs[:4], refs[4], refs[5], 0, step, bits, step, n)


def back_project(micro, dz, px, w_z, w_x, bits):
    tokens, width = px.shape
    depth = w_z.shape[0]
    n = tokens // BLOCK
    shapes, places, scratch = emitted(1, n, depth)
    return pl.pallas_call(
        functools.partial(back_kernel, n=n, bits=bits),
        grid=(n,),
        in_specs=[pl.BlockSpec((BLOCK, dz.shape[1]), lambda i: (micro * n + i, 0)), by_rows(width), fixed(w_z), fixed(w_x)],
        out_specs=places,
        out_shape=shapes,
        scratch_shapes=scratch,
        **arbitrary("back_project"),
    )(dz, px, w_z, w_x)


def shard_kernel(spot, *refs, n, hl):
    fronts, backs, (weight, gain, shard_in, shard_out, last) = refs[:n], refs[n : 2 * n], refs[2 * n :]
    rank, own = spot[0], spot[1]
    width = hl * HEADDIM
    rows = weight.shape[0]
    lane = iota2((rows, LANES), 1)
    square = jnp.zeros((rows, LANES), F32)
    scaled = jnp.zeros((rows, LANES), F32)
    shared = [jnp.zeros((rows, LANES), F32) for _ in range(2 * STATE // LANES + 1)]
    for mask in range(n):
        at = (rank ^ mask) * width
        for lo in range(0, width, LANES):
            spot_z = pl.multiple_of(at + lo, LANES)
            spot_x = pl.multiple_of(INNER + at + lo, LANES)
            out = fronts[mask][:, lo : lo + LANES].astype(F32)
            z = fronts[mask][:, width + lo : width + lo + LANES].astype(F32)
            x = backs[mask][:, lo : lo + LANES].astype(F32)
            shard_out[:, pl.ds(spot_z, LANES)] = out
            shard_in[:, pl.ds(spot_z, LANES)] = z
            shard_in[:, pl.ds(spot_x, LANES)] = x
            square += out * out + z * z + x * x
            scaled += weight[:, pl.ds(spot_z, LANES)].astype(BF).astype(F32) * z
            scaled += weight[:, pl.ds(spot_x, LANES)].astype(BF).astype(F32) * x
        for at_lane in range(2 * STATE // LANES):
            lo = width + at_lane * LANES
            shared[at_lane] += backs[mask][:, lo : lo + LANES].astype(F32)
        steps = jnp.where(lane < hl, backs[mask][:, width + 2 * STATE :].astype(F32), 0.0)
        shared[-1] += pltpu.roll(steps, (rank ^ mask) * hl, 1)
    for at_lane, one in enumerate(shared):
        lo = 2 * INNER + at_lane * LANES
        wide = min(LANES, weight.shape[1] - lo)
        one = one[:, :wide]
        shard_in[:, lo : lo + wide] = one
        square += jnp.concatenate([one * one, jnp.zeros((rows, LANES - wide), F32)], axis=1) if wide < LANES else one * one
        part = weight[:, lo : lo + wide].astype(BF).astype(F32) * one
        scaled += jnp.concatenate([part, jnp.zeros((rows, LANES - wide), F32)], axis=1) if wide < LANES else part
    d_gain = jnp.sum(scaled, axis=1, keepdims=True) / gain[:, 0:1]
    start = own * rows
    line = jnp.sum(jnp.where(lane == start % LANES + iota2((rows, LANES), 0), d_gain, 0.0), axis=0, keepdims=True)
    total = jnp.sum(jnp.sum(square, axis=0, keepdims=True), axis=1, keepdims=True)
    row, col = iota2(last.shape, 0), iota2(last.shape, 1)
    last[...] = jnp.where(row == start // LANES, line, 0.0) + jnp.where((row == D // LANES) & (col == 0), total, 0.0)


def shards(spot, fronts, backs, weight, gain, hl):
    rows = weight.shape[0]
    return pl.pallas_call(
        functools.partial(shard_kernel, n=len(fronts), hl=hl),
        grid_spec=pltpu.PrefetchScalarGridSpec(
            num_scalar_prefetch=1,
            grid=(1,),
            in_specs=[pl.BlockSpec(one.shape, lambda i, spot: (0, 0)) for one in (*fronts, *backs, weight, gain)],
            out_specs=[
                pl.BlockSpec(weight.shape, lambda i, spot: (0, 0)),
                pl.BlockSpec((rows, INNER), lambda i, spot: (0, 0)),
                pl.BlockSpec((D // LANES + 8, LANES), lambda i, spot: (0, 0)),
            ],
        ),
        out_shape=[
            jax.ShapeDtypeStruct(weight.shape, F32),
            jax.ShapeDtypeStruct((rows, INNER), F32),
            jax.ShapeDtypeStruct((D // LANES + 8, LANES), F32),
        ],
        **arbitrary("shards"),
    )(spot, *fronts, *backs, weight, gain)


def small_kernel(conv_0, conv_1, vec_0, vec_1, skip_0, skip_1, gain, out):
    width = gain.shape[1]
    out[...] = jnp.zeros(out.shape, F32)
    for tap in range(CONV + 1):
        rows = slice(tap * 8, tap * 8 + 8)
        out[tap : tap + 1, :] = jnp.sum(conv_0[rows, :] + conv_1[rows, :], axis=0, keepdims=True)
    out[5:6, :width] = jnp.sum(gain[...], axis=0, keepdims=True)
    out[6:7, :width] = jnp.sum(skip_0[...] + skip_1[...], axis=0, keepdims=True)
    vec = vec_0[...] + vec_1[...]
    head, lane = iota2((SLOT, LANES), 0), iota2((SLOT, LANES), 1)
    line = jnp.where(lane == head, vec[:, 0:1], jnp.where(lane == SLOT + head, vec[:, 1:2], 0.0))
    out[7:8, :LANES] = jnp.sum(line, axis=0, keepdims=True)


def small_gradients(*parts):
    return pl.pallas_call(
        small_kernel,
        out_shape=jax.ShapeDtypeStruct((8, parts[0].shape[1]), F32),
        name="small_gradients",
    )(*parts)


def place_kernel(spot, *refs, width):
    *pieces, out = refs
    shared = 0.0
    for mask, piece in enumerate(pieces):
        at = (spot[0] ^ mask) * width
        for lo in range(0, width, LANES):
            out[:, pl.ds(pl.multiple_of(at + lo, LANES), LANES)] = piece[:, lo : lo + LANES]
        shared = shared + piece[:, width:]
    out[:, INNER:] = shared


def place_small(spot, pieces, width):
    return pl.pallas_call(
        functools.partial(place_kernel, width=width),
        grid_spec=pltpu.PrefetchScalarGridSpec(
            num_scalar_prefetch=1,
            grid=(1,),
            in_specs=[pl.BlockSpec(one.shape, lambda i, spot: (0, 0)) for one in pieces],
            out_specs=pl.BlockSpec((8, CH), lambda i, spot: (0, 0)),
        ),
        out_shape=jax.ShapeDtypeStruct((8, CH), F32),
        **arbitrary("place_small"),
    )(spot, *pieces)

def swapped(value, axis, mask):
    return lax.ppermute(value, axis, [(i, i ^ mask) for i in range(lax.axis_size(axis))])


def axis_bits(axis):
    return [1 << i for i in range(lax.axis_size(axis).bit_length() - 1)]


def micro_order(micro, axis):
    bits = axis_bits(axis)
    return bits if micro % 2 == 0 else bits[::-1]


def nothing(*refs):
    pass


def after(values, *done):
    values = list(values)
    anywhere = pl.BlockSpec(memory_space=pl.ANY)
    held = pl.pallas_call(
        nothing,
        in_specs=[anywhere] * (len(values) + len(done)),
        out_specs=[anywhere] * len(values),
        out_shape=[jax.ShapeDtypeStruct(v.shape, v.dtype) for v in values],
        input_output_aliases={at: at for at in range(len(values))},
        name="after",
    )(*values, *done)
    return list(held)


def gather_stages(own):
    held = [{0: own[micro]} for micro in range(MICRO)]
    for turn in range(len(axis_bits("seq"))):
        got = []
        for micro in range(MICRO):
            bit = micro_order(micro, "seq")[turn]
            got.append({at ^ bit: swapped(held[micro][at], "seq", bit) for at in held[micro]})
        wait = yield [piece for one in got for piece in one.values()], [piece for one in held for piece in one.values()]
        for micro in range(MICRO):
            if wait is not None:
                got[micro] = dict(zip(got[micro], after(got[micro].values(), *wait)))
            held[micro].update(got[micro])
    yield [held[micro][at] for micro in range(MICRO) for at in range(len(held[micro]))]


def scatter_stages(parts):
    n = 2 * parts[0].shape[1]
    away, stay = list(parts[0::2]), list(parts[1::2])
    places = [[at for at in range(n) if not at & micro_order(half, "seq")[0]] for half in range(2)]
    join = lambda one, more: (one.astype(F32) + more.astype(F32)).astype(BF)
    pick = lambda a, at: jnp.concatenate([a[:, k : k + 1] for k in at], axis=1)
    turns = len(axis_bits("seq"))
    for turn in range(turns):
        got = [swapped(away[half], "seq", micro_order(half, "seq")[turn]) for half in range(2)]
        wait = yield got, away
        if wait is not None:
            got = after(got, *wait)
        if turn == turns - 1:
            break
        held, away, stay = stay, [], []
        for half in range(2):
            bit = micro_order(half, "seq")[turn + 1]
            leave = [at for at, place in enumerate(places[half]) if place & bit]
            keep = [at for at, place in enumerate(places[half]) if not place & bit]
            away.append(join(pick(held[half], leave), pick(got[half], leave)))
            stay.append(join(pick(held[half], keep), pick(got[half], keep)))
            places[half] = [places[half][at] for at in keep]
    yield jnp.concatenate([join(one, more)[:, 0] for one, more in zip(stay, got)], axis=1), None


def finish(stages, wait=None):
    last = None
    try:
        while True:
            last = stages.send(wait)
    except StopIteration:
        return last[0]


def turned(entries, rank):
    entries = list(entries)
    for bit in axis_bits("seq"):
        flip = (rank & bit) != 0
        entries = [jnp.where(flip, entries[at ^ bit], entries[at]) for at in range(len(entries))]
    return entries


def exchange(entries, rank):
    entries = turned(entries, rank)
    return entries, [swapped(one, "seq", mask) for mask, one in enumerate(entries) if mask]


def sum_pieces(value):
    n = value.shape[-2]
    total = value
    for mask in range(1, n):
        got = swapped(value, "seq", mask)
        total = total + jnp.concatenate([got[..., at ^ mask : (at ^ mask) + 1, :] for at in range(n)], axis=-2)
    return total


def adamw(master, gradient, first, second, clip, decay):
    clipped = gradient * clip
    first_new = BETA_ONE * first + (1.0 - BETA_ONE) * clipped
    second_new = BETA_TWO * second + (1.0 - BETA_TWO) * clipped * clipped
    update = first_new / FIX_ONE / (jnp.sqrt(second_new / FIX_TWO) + ADAM_EPS) + decay * master
    return (-LEARN_RATE * update, first_new, second_new)


def per_device(tokens, cotangent, segments, in_weight, in_m, in_v, conv_weight, conv_m, conv_v,
               out_weight, out_m, out_v, packed, packed_m, packed_v):
    n = lax.axis_size("seq")
    rank = lax.axis_index("seq")
    own = lax.axis_index("dp") * n + rank
    place = rank.astype(jnp.int32).reshape(1)
    ndev = n * lax.axis_size("dp")
    hl = HEADS // n
    xw = hl * HEADDIM
    rows = D // ndev
    piece = tokens.shape[1]
    count = MICRO * n * piece
    xs = INNER + INNER
    bc = 2 * STATE
    xc = xw + bc + LANES
    cw = conv_weight.shape[1]
    conv_cols = -(-(CONV + 1) * cw // rows)

    in_low = in_weight.astype(BF)
    out_low = out_weight.astype(BF).T
    conv_flat = conv_weight.astype(BF).reshape(-1)
    conv_flat = jnp.pad(conv_flat, (0, conv_cols * rows - conv_flat.shape[0])).reshape(rows, conv_cols)
    column = lambda a, q, width: a[:, q * width : (q + 1) * width]
    pad = jnp.zeros((rows, LANES - hl - conv_cols), BF)
    send_x = [
        jnp.concatenate(
            [column(in_low[:, INNER:xs], q, xw), in_low[:, xs : xs + bc], column(in_low[:, xs + bc :], q, hl), conv_flat, pad], axis=1
        )
        for q in range(n)
    ]
    gain_in = packed[3 * HEADS : 3 * HEADS + D]
    send_x = turned(send_x, rank)
    got_wx = [one if not mask else swapped(one, "seq", mask) for mask, one in enumerate(send_x)]
    a_log = lax.dynamic_slice_in_dim(packed, rank * hl, hl)
    skip = lax.dynamic_slice_in_dim(packed, HEADS + rank * hl, hl)
    dt_bias = lax.dynamic_slice_in_dim(packed, 2 * HEADS + rank * hl, hl)
    gain_out = lax.dynamic_slice_in_dim(packed, 3 * HEADS + D + rank * xw, xw)
    aux, masks = segment_aux(segments)
    heads = head_columns(a_log, dt_bias)
    skip = jnp.broadcast_to(jnp.repeat(skip, HEADDIM)[None], (8, xw))

    tok = tokens.astype(F32)
    r_in = lax.rsqrt(jnp.mean(tok * tok, axis=-1, keepdims=True) + NORM_EPS)
    hidden_stages = gather_stages((tok * r_in * gain_in).astype(BF))
    arrived, sent = next(hidden_stages)
    more, _ = hidden_stages.send(None)
    got_wx = jnp.concatenate(turned(got_wx[:1] + after(got_wx[1:], *sent), rank), axis=0)
    w_x = lax.all_gather(got_wx, "dp", axis=0, tiled=True)
    send_zo = jnp.stack(turned([jnp.concatenate([column(in_low, q, xw), column(out_low, q, xw)], axis=1) for q in range(n)], rank))
    [send_zo] = after([send_zo], got_wx, more[0], more[2])
    got_wzo = [send_zo[mask] if not mask else swapped(send_zo[mask], "seq", mask) for mask in range(n)]
    got_wzo = jnp.concatenate(turned(got_wzo, rank), axis=0)
    w_z = lax.all_gather(got_wzo[:, :xw], "dp", axis=0, tiled=True)
    w_o = lax.all_gather(got_wzo[:, xw:], "dp", axis=0, tiled=True)
    conv_full = w_x[:, xw + bc + hl : xw + bc + hl + conv_cols].reshape(ndev, rows * conv_cols)[:, : (CONV + 1) * cw]
    conv_full = conv_full.reshape(ndev, CONV + 1, cw).transpose(1, 0, 2).reshape(CONV + 1, CH)
    conv_loc = jnp.concatenate([lax.dynamic_slice_in_dim(conv_full, rank * xw, xw, 1), conv_full[:, INNER:]], axis=1).astype(F32)
    conv_loc = jnp.pad(conv_loc, ((0, 8 - CONV - 1), (0, 0)))

    for _ in axis_bits("seq")[1:]:
        arrived, more = more, hidden_stages.send(None)
        more = more[0] if isinstance(more, tuple) else more
    late = [micro * n + at for micro in range(MICRO) for at in range(n) if at & (last := micro_order(micro, "seq")[-1]) and at != last]
    soon = [at for at in range(MICRO * n) if at not in late]
    soon.sort(key=lambda at: (at % n).bit_count())
    earlier = in_project([more[at] for at in soon], soon, MICRO * n, w_x, done=(aux, masks, conv_loc))
    late_pieces = after([more[at] for at in late], earlier[0])
    proj_x, hidden = in_project(late_pieces, late, MICRO * n, w_x, earlier)

    cot_stages = gather_stages(after([cotangent[micro] for micro in range(MICRO)], *late_pieces))
    next(cot_stages)
    y, states, act, slope = scan_forward(place, proj_x, conv_loc, skip, heads, aux, masks, hl)
    for bit in axis_bits("seq"):
        cot = cot_stages.send([proj_x] if bit == 1 else [y])
    gain = jnp.broadcast_to(gain_out[None], (8, xw))
    [w_z] = after([w_z], y)
    z = dot(hidden, w_z, NN).astype(BF)
    dn, cot, sums = gate_forward(cot, z, w_o, y, gain)
    sums = sum_pieces(sums.reshape(2, MICRO, n, piece)).reshape(-1, BLOCK)
    first_bits = tuple(micro_order(half, "seq")[0] for half in range(2))
    normed, dy, dz, d_gain_out, *out_part = out_project(z, dn, y, sums, gain, w_o, first_bits)

    scatter = lambda a: lax.psum_scatter(a, "dp", scatter_dimension=0, tiled=True)
    split = lambda a: [a[q * rows : (q + 1) * rows] for q in range(n)]
    out_stages = scatter_stages(out_part)
    next(out_stages)
    part_o = dot(cot, normed, TN).astype(BF)
    part_z = dot(hidden, dz, TN).astype(BF)
    got_o, got_z = scatter(part_o), scatter(part_z)

    through_in = lambda micro, one: back_project(micro, dz, one, w_z, w_x, first_bits)
    scan_back = lambda micro, *done: scan_backward(
        place, micro, proj_x, conv_loc, skip, heads, aux, masks, act, slope, dy, states, hl, *done
    )

    px_0, dco_0, vec_0, skip_0 = scan_back(0, part_o, part_z)
    hid_0 = through_in(0, px_0)
    out_got, out_sent = out_stages.send([hid_0[0]])
    stages_0 = scatter_stages(hid_0)
    hid_got, sent = next(stages_0)
    px_1, dco_1, vec_1, skip_1 = scan_back(1, *sent, *out_sent)
    [px_1] = after([px_1], *hid_got, *out_got)
    part_x = dot(hidden, jnp.concatenate([px_0, px_1], axis=0), TN).astype(BF)
    got_x = scatter(part_x)
    hid_got, sent = stages_0.send([part_x])
    spot = jnp.stack([rank, own]).astype(jnp.int32)
    own_gain = lax.dynamic_slice_in_dim(gain_in, own * rows, rows)[:, None]
    [px_1] = after([px_1], part_x, *sent)
    hid_1 = through_in(1, px_1)
    [got_o, got_z] = after([got_o, got_z], part_x)
    sent_oz, got_oz = exchange(split(jnp.concatenate([got_o, got_z], axis=1)), rank)
    dco_0, dco_1 = after([dco_0, dco_1], hid_1[0])
    conv_0, conv_1 = (tap_gradients(place, micro, proj_x, aux, one) for micro, one in enumerate((dco_0, dco_1)))
    stages_1 = scatter_stages(after(hid_1, *hid_got))
    hid_got, _ = next(stages_1)
    small = small_gradients(conv_0, conv_1, vec_0, vec_1, skip_0, skip_1, d_gain_out)
    [small] = after([small], *hid_got)
    output = (tok + finish(out_stages, [small]).astype(F32)).astype(BF)
    for bit in axis_bits("dp"):
        small = small + swapped(small, "dp", bit)
    _, hid_sent = stages_1.send(None)
    [got_x] = after([got_x], output, *hid_sent, *got_oz)
    sent_x, got_x = exchange(split(got_x), rank)
    [small] = after([small], *sent_x)
    small = [small] + after([swapped(small, "seq", mask) for mask in range(1, n)], *got_x)
    small = place_small(spot, small, xw)
    conv_tot, gain_out_tot = small[: CONV + 1], small[5, :INNER]
    skip_tot = jnp.sum(small[6, :INNER].reshape(HEADS, HEADDIM), axis=1)
    by_head = small[7, :INNER].reshape(n, xw)
    a_log_tot, dt_bias_tot = by_head[:, :hl].reshape(-1), by_head[:, SLOT : SLOT + hl].reshape(-1)
    shard_conv = lax.dynamic_slice_in_dim(conv_tot, own * cw, cw, 1)
    conv_sq = jnp.sum(conv_tot * conv_tot)
    shard_in, shard_out, last = shards(spot, sent_oz[:1] + got_oz, sent_x[:1] + got_x, in_weight, own_gain, hl)
    shard_out = shard_out.T
    d_hidden = jnp.concatenate([finish(stages_0, [hid_1[0]]), finish(stages_1, got_x)], axis=0).astype(F32)
    dh = d_hidden * gain_in
    d_tok = r_in * (dh - tok * (r_in * r_in) * jnp.mean(dh * tok, axis=-1, keepdims=True))
    input_grad = (cotangent.astype(F32) + d_tok).astype(BF)

    stages = [(axis, bit) for axis in ("seq", "dp") for bit in axis_bits(axis)]
    for axis, bit in stages:
        last = last + swapped(last, axis, bit)
    vec_tot = jnp.concatenate([a_log_tot, skip_tot, dt_bias_tot, last[: D // LANES].reshape(-1), gain_out_tot])
    grad_norm = jnp.sqrt(last[D // LANES, 0] + conv_sq + jnp.sum(vec_tot * vec_tot))
    clip = jnp.minimum(1.0, CLIP_NORM / (grad_norm + 1e-06))
    in_new = adamw(in_weight, shard_in, in_m, in_v, clip, WEIGHT_DECAY)
    conv_new = adamw(conv_weight, shard_conv, conv_m, conv_v, clip, WEIGHT_DECAY)
    out_new = adamw(out_weight, shard_out, out_m, out_v, clip, WEIGHT_DECAY)
    vec_new = adamw(packed, vec_tot, packed_m, packed_v, clip, 0.0)
    return (
        output, input_grad, grad_norm,
        in_weight + in_new[0], in_new[1], in_new[2],
        conv_new[0], conv_new[1], conv_new[2],
        out_weight + out_new[0], out_new[1], out_new[2],
        vec_new[0], vec_new[1], vec_new[2],
    )


def solution(mesh):
    tok, col, row = P(None, ALL, None), P(None, ALL), P(ALL, None)
    return jax.shard_map(
        per_device,
        mesh=mesh,
        in_specs=(tok, tok, P(None, "dp"), row, row, row, col, col, col, col, col, col, P(), P(), P()),
        out_specs=(tok, tok, P(), row, row, row, col, col, col, col, col, col, P(), P(), P()),
        check_vma=False,
    )
```
